32 devices in a mesh: dp: 8 (over y, x, core), chan: 4 (over z).
Axes of the slice: x: 2, y: 2, z: 4, core: 2. Of those that a mesh axis runs over, the one named last changes fastest.
Arguments:
- stream: bfloat16 [8192, 768], P('dp', 'chan'), may hold values from -32 to 32, as said below
- segments: int32 [8192], P('dp'), may hold values from 0 to 64, as said below
- cotangent: bfloat16 [8192, 768], P('dp', 'chan'), may hold values from -6 to 6
- norm_one: float32 [2, 768], P(None, 'chan'), may hold values from 0.1 to 1.9
- in_proj: bfloat16 [2, 768, 3, 768], P(None, None, None, 'chan'), may hold values from -0.21875 to 0.21875
- short_taps: float32 [2, 3, 3, 768], P(None, None, None, 'chan'), may hold values from -3 to 3
- cond_in: float32 [2, 12, 128, 128], P(None, 'chan'), may hold values from -0.5 to 0.5
- cond_out: float32 [2, 12, 128, 128], P(None, 'chan'), may hold values from -0.5 to 0.5
- filter_spec: float32 [2, 2, 1024, 768], P(None, None, None, 'chan'), may hold values from -4 to 4
- out_proj: bfloat16 [2, 768, 768], P(None, 'chan'), may hold values from -0.21875 to 0.21875
- norm_two: float32 [2, 768], P(None, 'chan'), may hold values from 0.1 to 1.9
- gate_proj: bfloat16 [2, 768, 3072], P(None, None, 'chan'), may hold values from -0.21875 to 0.21875
- up_proj: bfloat16 [2, 768, 3072], P(None, None, 'chan'), may hold values from -0.21875 to 0.21875
- down_proj: bfloat16 [2, 3072, 768], P(None, 'chan'), may hold values from -0.109375 to 0.109375
Outputs:
- output: float32 [8192, 768], P('dp', 'chan')
- stream_grad: float32 [8192, 768], P('dp', 'chan')
- norm_one_grad: float32 [2, 768], P(None, 'chan')
- in_proj_grad: float32 [2, 768, 3, 768], P(None, None, None, 'chan')
- short_taps_grad: float32 [2, 3, 3, 768], P(None, None, None, 'chan')
- cond_in_grad: float32 [2, 12, 128, 128], P(None, 'chan')
- cond_out_grad: float32 [2, 12, 128, 128], P(None, 'chan')
- filter_spec_grad: float32 [2, 2, 1024, 768], P(None, None, None, 'chan')
- out_proj_grad: float32 [2, 768, 768], P(None, 'chan')
- norm_two_grad: float32 [2, 768], P(None, 'chan')
- gate_proj_grad: float32 [2, 768, 3072], P(None, None, 'chan')
- up_proj_grad: float32 [2, 768, 3072], P(None, None, 'chan')
- down_proj_grad: float32 [2, 3072, 768], P(None, 'chan')
The draws below stay inside these ranges and needn't reach their ends.
Inputs may be any that keep to these rules, and one draw needn't show every extreme that they name: `stream`: activations; within each pack the channels' scales differ widely. `segments`: within each pack of 1024 rows the numbers start at 0 on its first row, rise by 0 or 1 from one row to the next, and end at 64 on its last row.
All inputs are finite; a program needn't handle non-finite values.
Results may differ from the reference program's by a relative error of at most 0.025.
Values may be sent and summed in bfloat16 or wider, within the bound.
A program may use at most 320 MiB of HBM per device.

```python
import jax
import jax.numpy as jnp
from jax import lax

D = 768
FF = 3072
SEQ = 1024
E = 64
FH = 128
LAYERS = 2
TOKENS = 8192
H = 12


def draw_stream(key, part):
    key_base, key_chan, key_rows = jax.random.split(key, 3)
    channel_pos = jnp.arange(D, dtype=jnp.float32) / D
    chan_scale = 10.0 ** (channel_pos - 0.5) * jax.random.uniform(key_chan, (D,), jnp.float32, 0.7, 1.4)
    row_scale = jnp.exp(jax.random.uniform(key_rows, (TOKENS,), jnp.float32, -1.204, 1.099))
    base = jax.random.normal(key_base, (TOKENS, D), jnp.float32)
    values = jnp.clip(base * row_scale[:, None] * chan_scale[None, :], -32.0, 32.0)
    return values.astype(jnp.bfloat16)


def draw_segments(key, part):
    key_bound, key_offset = jax.random.split(jax.random.fold_in(key, 7))
    pack_count = TOKENS // SEQ
    boundary = jax.random.randint(key_bound, (pack_count, SEQ), 0, 16) == 0
    offset = jax.random.randint(key_offset, (pack_count, 1), 1, 16)
    position = jnp.arange(SEQ, dtype=jnp.int32)[None, :]
    forced = position % 16 == offset
    start_ones = jnp.where((boundary | forced) & (position != 0), 1, 0).astype(jnp.int32)
    running = jnp.minimum(jnp.cumsum(start_ones, axis=1), SEQ // 16)
    return running.reshape(TOKENS).astype(jnp.int32)


def levels(key, extent, shards, low, top_value):
    factor_of = 1.0
    for axis_at, parts in shards:
        steps = jax.random.uniform(jax.random.fold_in(jax.random.fold_in(key, 6), axis_at), (parts,), jnp.float32, low / len(shards), top_value / len(shards))
        factor_of = factor_of * jnp.repeat(jnp.exp(steps), extent[axis_at] // parts).reshape((-1,) + (1,) * (len(extent) - 1 - axis_at))
    return factor_of


def scatter_about(stream_key, dims, scale, limit, shards=(), kind=jnp.bfloat16):
    values = scale * jax.random.normal(stream_key, dims, jnp.float32)
    if shards:
        values = values * levels(stream_key, dims, shards, -0.22, 0.18)
    return jnp.clip(values, -limit, limit).astype(kind)


def setup_inputs(seed: int = 0) -> dict:
    key_list = jax.random.split(jax.random.key(seed), 15)
    stream = draw_stream(jax.random.fold_in(key_list[14], 71), 0)
    segments = draw_segments(jax.random.fold_in(key_list[14], 71), 0)
    cotangent = scatter_about(key_list[2], (TOKENS, D), 1.0, 6.0, ((0, 8), (1, 4)))
    norm_one = jnp.clip(1.0 + 0.18 * jax.random.normal(key_list[3], (LAYERS, D), jnp.float32), 0.1, 1.9)
    in_proj = scatter_about(key_list[4], (LAYERS, D, 3, D), D ** -0.5, 0.21875, ((3, 4),))
    short_taps = scatter_about(key_list[5], (LAYERS, 3, 3, D), 0.6, 3.0, ((3, 4),), jnp.float32)
    cond_in = scatter_about(key_list[6], (LAYERS, H, 2 * E, FH), (2 * E) ** -0.5, 0.5, ((1, 4),), jnp.float32)
    cond_out = scatter_about(key_list[7], (LAYERS, H, FH, 2 * E), FH ** -0.5, 0.5, ((1, 4),), jnp.float32)
    filter_spec = scatter_about(key_list[8], (LAYERS, 2, SEQ, D), 0.7, 4.0, ((3, 4),), jnp.float32)
    out_proj = scatter_about(key_list[9], (LAYERS, D, D), D ** -0.5, 0.21875, ((1, 4),))
    norm_two = jnp.clip(1.0 + 0.18 * jax.random.normal(key_list[10], (LAYERS, D), jnp.float32), 0.1, 1.9)
    gate_proj = scatter_about(key_list[11], (LAYERS, D, FF), D ** -0.5, 0.21875, ((2, 4),))
    up_proj = scatter_about(key_list[12], (LAYERS, D, FF), D ** -0.5, 0.21875, ((2, 4),))
    down_proj = scatter_about(key_list[13], (LAYERS, FF, D), FF ** -0.5, 0.109375, ((1, 4),))
    return dict(stream=stream, segments=segments, cotangent=cotangent, norm_one=norm_one, in_proj=in_proj, short_taps=short_taps, cond_in=cond_in, cond_out=cond_out, filter_spec=filter_spec, out_proj=out_proj, norm_two=norm_two, gate_proj=gate_proj, up_proj=up_proj, down_proj=down_proj)


EPSILON = 1e-05
PRECISE = lax.Precision.HIGHEST

@jax.custom_vjp
def low(v):
    return lax.optimization_barrier(v.astype(jnp.bfloat16)).astype(jnp.float32)

@jax.custom_vjp
def low_back(v):
    return v

def low_keep(v):
    return (low(v), None)

def low_pass(kept, grad):
    return (grad,)

def back_keep(v):
    return (v, None)

def back_low(kept, grad):
    return (low(grad),)
low.defvjp(low_keep, low_pass)
low_back.defvjp(back_keep, back_low)

def layer_norm(values, norm_gain):
    average = lax.optimization_barrier(jnp.mean(values, axis=-1, keepdims=True))
    centered = values - average
    variance = lax.optimization_barrier(jnp.mean(centered * centered, axis=-1, keepdims=True))
    return centered * lax.rsqrt(variance + EPSILON) * norm_gain

def mix_core(projected, taps, weight_in, weight_out, spectrum, mask_prev, mask_next, pack_count):
    row_count = projected.shape[0]
    length = row_count // pack_count
    chan_width = projected.shape[2]
    zero_row = jnp.zeros((1,) + projected.shape[1:], projected.dtype)
    preceding = jnp.concatenate([zero_row, projected[:-1]], 0) * mask_prev[:, None, None]
    following = jnp.concatenate([projected[1:], zero_row], 0) * mask_next[:, None, None]
    short_out = taps[0] * preceding + taps[1] * projected + taps[2] * following
    short_out = short_out.reshape(pack_count, length, 3, chan_width)
    query_part = short_out[:, :, 0]
    value_part = short_out[:, :, 1]
    cond_part = short_out[:, :, 2]
    cond_hat = jnp.fft.fft(cond_part, axis=1, norm='ortho')
    value_hat = jnp.fft.fft(value_part, axis=1, norm='ortho')
    head_count = weight_in.shape[0]
    group_size = chan_width // head_count
    grouped = (pack_count, length, head_count, group_size)
    features = jnp.concatenate([jnp.real(cond_hat).reshape(grouped), jnp.imag(cond_hat).reshape(grouped)], -1)
    inner_act = jax.nn.gelu(jnp.einsum('pkhi,hif->pkhf', features, weight_in, precision=PRECISE), approximate=False)
    filter_made = jnp.einsum('pkhf,hfo->pkho', inner_act, weight_out, precision=PRECISE)
    kernel_real = spectrum[0] + filter_made[..., :group_size].reshape(pack_count, length, chan_width)
    kernel_imag = spectrum[1] + filter_made[..., group_size:].reshape(pack_count, length, chan_width)
    value_real = jnp.real(value_hat)
    value_imag = jnp.imag(value_hat)
    prod_hat = lax.complex(value_real * kernel_real - value_imag * kernel_imag, value_real * kernel_imag + value_imag * kernel_real)
    mixed_out = jnp.real(jnp.fft.ifft(prod_hat, axis=1, norm='ortho'))
    return (query_part * mixed_out).reshape(row_count, chan_width)

def one_layer(values, weights, mask_prev, mask_next, pack_count):
    gain_one, in_weight, taps, weight_in, weight_out, spectrum, out_weight, gain_two, gate_weight, up_weight, down_weight = weights
    normed_a = low(layer_norm(values, gain_one))
    projected = low_back(jnp.einsum('rd,dsc->rsc', normed_a, in_weight, precision=PRECISE))
    gated = low(mix_core(projected, taps, weight_in, weight_out, spectrum, mask_prev, mask_next, pack_count))
    middle = values + low_back(jnp.dot(gated, out_weight, precision=PRECISE))
    normed_b = low(layer_norm(middle, gain_two))
    gate_val = low_back(jnp.dot(normed_b, gate_weight, precision=PRECISE))
    up_val = low_back(jnp.dot(normed_b, up_weight, precision=PRECISE))
    hidden = low(jax.nn.gelu(gate_val, approximate=False) * up_val)
    return middle + low_back(jnp.dot(hidden, down_weight, precision=PRECISE))

def reference(stream, segments, cotangent, norm_one, in_proj, short_taps, cond_in, cond_out, filter_spec, out_proj, norm_two, gate_proj, up_proj, down_proj):
    params = tuple((weight.astype(jnp.float32) for weight in (norm_one, in_proj, short_taps, cond_in, cond_out, filter_spec, out_proj, norm_two, gate_proj, up_proj, down_proj)))
    total_packs = stream.shape[0] // SEQ
    pack_group = 4 if total_packs % 4 == 0 else 2 if total_packs % 2 == 0 else 1
    block_count = total_packs // pack_group
    block_rows = pack_group * SEQ
    inputs = stream.astype(jnp.float32).reshape(block_count, block_rows, D)
    cotangents = cotangent.astype(jnp.float32).reshape(block_count, block_rows, D)
    seg_blocks = segments.reshape(block_count, block_rows)
    position = jnp.arange(block_rows, dtype=jnp.int32) % SEQ
    no_flag = jnp.zeros((1,), dtype=bool)

    def one_block(carried, sample):
        block_in, block_cot, block_seg = sample
        same_seg = block_seg[1:] == block_seg[:-1]
        mask_prev = jnp.where((position != 0) & jnp.concatenate([no_flag, same_seg]), 1.0, 0.0).astype(jnp.float32)
        mask_next = jnp.where((position != SEQ - 1) & jnp.concatenate([same_seg, no_flag]), 1.0, 0.0).astype(jnp.float32)

        def forward(values, weights):
            for layer_number in range(LAYERS):
                values = one_layer(values, tuple((weight[layer_number] for weight in weights)), mask_prev, mask_next, pack_group)
            return values
        result, pullback = jax.vjp(forward, block_in, params)
        input_grad, weight_grads = pullback(block_cot)
        summed = tuple((total + part_grad for total, part_grad in zip(carried, weight_grads)))
        return (summed, (result, input_grad))
    start_grads = tuple((jnp.zeros_like(weight) for weight in params))
    final_grads, (results, input_grads) = lax.scan(one_block, start_grads, (inputs, cotangents, seg_blocks))
    return (results.reshape(TOKENS, D), input_grads.reshape(TOKENS, D), final_grads[0], final_grads[1], final_grads[2], final_grads[3], final_grads[4], final_grads[5], final_grads[6], final_grads[7], final_grads[8], final_grads[9], final_grads[10])
```

```python
import functools
import math
from types import SimpleNamespace

import jax
import jax.numpy as jnp
import numpy as np
from jax import lax
from jax.experimental import pallas as pl
from jax.experimental.pallas import tpu as pltpu
from jax.sharding import Mesh
from jax.sharding import PartitionSpec as P

EPSILON = 1e-05
BF = jnp.bfloat16
F32 = jnp.float32


def dft_tables(length):
    positions = np.arange(length)
    angles = (positions[:, None] * positions[None, :] % length) * (2.0 * math.pi / length)
    scale = 1.0 / math.sqrt(length)
    cosine = np.asarray(np.cos(angles) * scale, dtype=np.float32)
    sine = np.asarray(-np.sin(angles) * scale, dtype=np.float32)
    return jnp.asarray(cosine, BF), jnp.asarray(sine, BF)


def normal_cdf(x):
    return 0.5 * (1.0 + lax.erf(x * (2.0**-0.5)))


def normal_pdf(x):
    return jnp.exp(-0.5 * x * x) * (1.0 / math.sqrt(2.0 * math.pi))


MESH = pl.DeviceIdType.MESH
VMEM_LIMIT = 58 << 20
CHUNKS = 2
PARTS = 8


def nt_dot(a, b):
    return lax.dot_general(a, b, (((1,), (1,)), ((), ())), preferred_element_type=F32)


def tn_dot(a, b):
    return lax.dot_general(a, b, (((0,), (0,)), ((), ())), preferred_element_type=F32)


def nn_dot(a, b):
    return jnp.dot(a, b, preferred_element_type=F32)


def aligned(index, size):
    return pl.ds(pl.multiple_of(index * size, size), size)


class Place:
    def __init__(self):
        self.col = lax.axis_index("col")
        self.half = lax.axis_index("half")
        self.chan = lax.axis_index("chan")
        odd = lax.rem(self.chan, 2)
        self.pack = self.chan // 2
        self.own = self.half == self.pack
        self.other_half = 1 - self.half
        self.near_chan = self.chan + 1 - 2 * odd
        self.far_chan = self.chan + 2 - 4 * self.pack
        self.rank = 2 * self.half + odd
        flip_near, flip_peer = 1 - 2 * odd, 2 - 4 * self.half
        self.ranks = [
            self.rank,
            self.rank + flip_near,
            self.rank + flip_peer,
            self.rank + flip_near + flip_peer,
        ]

    def col_at(self, step):
        return lax.rem(self.col + step, 4)

    def barrier(self):
        sem = pltpu.get_barrier_semaphore()
        devices = [{"col": self.col_at(j)} for j in range(1, 4)]
        for i in range(1, 8):
            half = self.half if i < 4 else self.other_half
            devices.append({"half": half, "chan": lax.rem(self.chan + i, 4)})
        for device in devices:
            pl.semaphore_signal(sem, inc=1, device_id=device, device_id_type=MESH)
        pl.semaphore_wait(sem, len(devices))


def remote(src, dst, send_sem, recv_sem, device):
    return pltpu.make_async_remote_copy(
        src_ref=src,
        dst_ref=dst,
        send_sem=send_sem,
        recv_sem=recv_sem,
        device_id=device,
        device_id_type=MESH,
    )


def await_recv(ref, recv_sem, send_sem):
    remote(ref, ref, send_sem, recv_sem, {"half": 1 - lax.axis_index("half")}).wait_recv()


def await_send(ref, send_sem, recv_sem):
    remote(ref, ref, send_sem, recv_sem, {"half": 1 - lax.axis_index("half")}).wait_send()


class Group:
    def __init__(self, place, r, rows):
        self.place = place
        self.near = {"chan": place.near_chan}
        self.peer = {"half": place.other_half}
        self.send, self.recv = r.group_send, r.group_recv
        self.to_peer, self.from_peer = r.to_peer, r.from_peer
        self.to_near, self.from_near = r.to_near, r.from_near
        self.rows, self.size = rows, rows // CHUNKS
        self.started = []

    @staticmethod
    def scratch(rows, width):
        return dict(
            group_send=pltpu.SemaphoreType.DMA((6, CHUNKS)),
            group_recv=pltpu.SemaphoreType.DMA((6, CHUNKS)),
            to_peer=pltpu.VMEM((2, rows, width), BF),
            from_peer=pltpu.VMEM((2, rows, width), BF),
            to_near=pltpu.VMEM((rows, width), BF),
            from_near=pltpu.VMEM((rows, width), BF),
        )

    def at(self, which, chunk=None):
        start = self.place.ranks[which] * self.rows
        if chunk is None:
            return pl.ds(pl.multiple_of(start, self.rows), self.rows)
        return pl.ds(pl.multiple_of(start + chunk * self.size, self.size), self.size)

    def start(self, src, dst, kind, chunk, device):
        copy = remote(src, dst, self.send.at[kind, chunk], self.recv.at[kind, chunk], device)
        copy.start()
        self.started.append(copy)

    def arrived(self, ref, kind, chunk):
        await_recv(ref, self.recv.at[kind, chunk], self.send.at[kind, chunk])

    def gather_start(self, full):
        for chunk in range(CHUNKS):
            own = full.at[self.at(0, chunk)]
            self.start(own, own, 0, chunk, self.near)
        for chunk in range(CHUNKS):
            own = full.at[self.at(0, chunk)]
            self.start(own, own, 1, chunk, self.peer)

    def gather_peer(self, full):
        for chunk in range(CHUNKS):
            self.arrived(full.at[self.at(2, chunk)], 1, chunk)

    def gather_near(self, full, chunk):
        piece = full.at[self.at(1, chunk)]
        self.arrived(piece, 0, chunk)
        self.start(piece, piece, 2, chunk, self.peer)

    def gather_diagonal(self, full, chunk):
        self.arrived(full.at[self.at(3, chunk)], 2, chunk)

    def piece(self, chunk):
        return pl.ds(chunk * self.size, self.size)

    def reduce_peer(self, slot, chunk, value):
        at = self.piece(chunk)
        self.to_peer[slot, at] = value.astype(BF)
        self.start(self.to_peer.at[slot, at], self.from_peer.at[slot, at], 3 + slot, chunk, self.peer)

    def reduce_near(self, chunk, value):
        at = self.piece(chunk)
        self.arrived(self.from_peer.at[1, at], 4, chunk)
        self.to_near[at] = (value + self.from_peer[1, at].astype(F32)).astype(BF)
        self.start(self.to_near.at[at], self.from_near.at[at], 5, chunk, self.near)

    def reduce_end(self, chunk):
        at = self.piece(chunk)
        self.arrived(self.from_peer.at[0, at], 3, chunk)
        self.arrived(self.from_near.at[at], 5, chunk)
        return self.from_peer[0, at].astype(F32) + self.from_near[at].astype(F32)

    def reduce_whole(self, kind, part):
        for chunk in range(CHUNKS):
            value = part[chunk * self.size : (chunk + 1) * self.size]
            if kind == "near":
                self.reduce_near(chunk, value)
            else:
                self.reduce_peer({"peer": 0, "diagonal": 1}[kind], chunk, value)

    def finish(self):
        for copy in self.started:
            copy.wait_send()


class Fetch:
    def __init__(self, place, r, pairs):
        self.place, self.pairs = place, pairs
        self.send, self.recv = r.fetch_send, r.fetch_recv

    @staticmethod
    def scratch(count):
        return dict(
            fetch_send=pltpu.SemaphoreType.DMA((count, 7)),
            fetch_recv=pltpu.SemaphoreType.DMA((count, 8)),
        )

    def cut(self, ref, axis, parts, index):
        at = aligned(index, ref.shape[axis] // parts)
        return ref.at[(slice(None),) * axis + (at,)]

    def index(self, parts, col, half):
        return col * 2 + half if parts == 8 else col

    def start(self):
        p = self.place
        owner = {"half": p.pack, "chan": p.far_chan}

        for a, (src, dst, axis, parts) in enumerate(self.pairs):

            def send(a=a, src=src, dst=dst, axis=axis, parts=parts):
                index = self.index(parts, p.col, p.half)
                remote(
                    self.cut(src, axis, parts, index),
                    self.cut(dst, axis, parts, index),
                    self.send.at[a, 0],
                    self.recv.at[a, p.half if parts == 8 else 0],
                    owner,
                ).start()

            if parts == 8:
                send()
            else:
                pl.when(p.half == 0)(send)

    def forward(self):
        p = self.place

        @pl.when(jnp.logical_not(p.own))
        def _():
            for a, (src, dst, axis, parts) in enumerate(self.pairs):
                for s in range(parts // 4):
                    piece = self.cut(dst, axis, parts, self.index(parts, p.col, s))
                    await_recv(piece, self.recv.at[a, s], self.send.at[a, 0])
                    for j in range(1, 4):
                        remote(
                            piece,
                            piece,
                            self.send.at[a, 2 * j - 1 + s],
                            self.recv.at[a, 2 * j + s],
                            {"col": p.col_at(j)},
                        ).start()

    def finish(self):
        p = self.place
        for a, (src, dst, axis, parts) in enumerate(self.pairs):

            def sent(a=a, src=src, axis=axis, parts=parts):
                piece = self.cut(src, axis, parts, self.index(parts, p.col, p.half))
                await_send(piece, self.send.at[a, 0], self.recv.at[a, 0])

            if parts == 8:
                sent()
            else:
                pl.when(p.half == 0)(sent)

        @pl.when(jnp.logical_not(p.own))
        def _():
            for a, (src, dst, axis, parts) in enumerate(self.pairs):
                for s in range(parts // 4):
                    for j in range(1, 4):
                        piece = self.cut(dst, axis, parts, self.index(parts, p.col_at(4 - j), s))
                        await_recv(piece, self.recv.at[a, 2 * j + s], self.send.at[a, 0])
                        await_send(piece, self.send.at[a, 2 * j - 1 + s], self.recv.at[a, 0])


class Load:
    def __init__(self, place, r, sources):
        self.place, self.sources, self.sem = place, sources, r.load_sem

    @staticmethod
    def scratch(count):
        return dict(load_sem=pltpu.SemaphoreType.DMA((count,)))

    def start(self):
        p = self.place

        @pl.when(p.own)
        def _():
            for a, (own, fetched, to) in enumerate(self.sources):
                pltpu.make_async_copy(own, to, self.sem.at[a]).start()

        @pl.when(jnp.logical_not(p.own))
        def _():
            for a, (own, fetched, to) in enumerate(self.sources):
                pltpu.make_async_copy(fetched, to, self.sem.at[a]).start()

    def finish(self, which=None):
        for a in range(len(self.sources)) if which is None else which:
            own, fetched, to = self.sources[a]
            pltpu.make_async_copy(fetched, to, self.sem.at[a]).wait()


class Exchange:
    def __init__(self, place, r, src, dst):
        self.place, self.src, self.dst = place, src, dst
        self.send, self.recv, self.local = r.ex_send, r.ex_recv, r.ex_local
        self.size = src.shape[0] // 4

    @staticmethod
    def scratch():
        return dict(
            ex_send=pltpu.SemaphoreType.DMA((4,)),
            ex_recv=pltpu.SemaphoreType.DMA((4,)),
            ex_local=pltpu.SemaphoreType.DMA,
        )

    def each(self, act, act_self):
        p = self.place
        for j in range(4):
            chan = 2 * p.half + j % 2
            mine = (p.half == j // 2) & (p.chan == chan)
            src, dst = self.src.at[pl.ds(j * self.size, self.size)], self.dst.at[p.chan]

            def go(j=j, chan=chan, src=src, dst=dst):
                act(
                    remote(
                        src, dst, self.send.at[j], self.recv.at[p.chan],
                        {"half": j // 2, "chan": chan},
                    )
                )

            def stay(src=src, dst=dst):
                act_self(pltpu.make_async_copy(src, dst, self.local))

            pl.when(jnp.logical_not(mine))(go)
            pl.when(mine)(stay)

    def start(self):
        self.each(lambda c: c.start(), lambda c: c.start())

    def finish(self):
        p = self.place
        self.each(lambda c: c.wait_send(), lambda c: c.wait())
        for j in range(4):

            def wait(j=j):
                await_recv(self.dst.at[j], self.recv.at[j], self.send.at[0])

            pl.when(jnp.logical_not(p.own & (p.chan == j)))(wait)


class Return:
    def __init__(self, place, r, src, dst):
        self.place, self.src, self.dst = place, src, dst
        self.send, self.recv, self.local = r.back_send, r.back_recv, r.back_local
        self.size = src.shape[1]

    @staticmethod
    def scratch():
        return dict(
            back_send=pltpu.SemaphoreType.DMA((4,)),
            back_recv=pltpu.SemaphoreType.DMA((4,)),
            back_local=pltpu.SemaphoreType.DMA,
        )

    def each(self, act, act_self):
        p = self.place
        for j in range(4):
            mine = p.own & (p.chan == j)
            src, dst = self.src.at[j], self.dst.at[aligned(p.rank, self.size)]

            def go(j=j, src=src, dst=dst):
                act(
                    remote(
                        src, dst, self.send.at[j], self.recv.at[p.rank],
                        {"half": p.pack, "chan": j},
                    )
                )

            def stay(src=src, dst=dst):
                act_self(pltpu.make_async_copy(src, dst, self.local))

            pl.when(jnp.logical_not(mine))(go)
            pl.when(mine)(stay)

    def start(self):
        self.each(lambda c: c.start(), lambda c: c.start())

    def finish(self):
        p = self.place
        self.each(lambda c: c.wait_send(), lambda c: c.wait())
        for j in range(4):
            mine = (p.half == j // 2) & (p.chan == 2 * p.half + j % 2)

            def wait(j=j):
                await_recv(
                    self.dst.at[pl.ds(j * self.size, self.size)], self.recv.at[j], self.send.at[0]
                )

            pl.when(jnp.logical_not(mine))(wait)


class Scatter:
    def __init__(self, place, r, sources, totals):
        self.place, self.sources, self.totals = place, sources, totals
        self.r = r
        self.got = [getattr(r, f"sc_got{a}") for a in range(len(sources))]
        self.part = [getattr(r, f"sc_part{a}") for a in range(len(sources))]
        self.cross = [getattr(r, f"sc_cross{a}") for a in range(len(sources))]

    @staticmethod
    def scratch(shapes):
        n = len(shapes)
        out = dict(
            sc_send=pltpu.SemaphoreType.DMA((n, 5)),
            sc_recv=pltpu.SemaphoreType.DMA((n, 5)),
            sc_local=pltpu.SemaphoreType.DMA((n, 2)),
        )
        for a, (rows, width) in enumerate(shapes):
            out[f"sc_got{a}"] = pltpu.VMEM((4, rows // 4, width), BF)
            out[f"sc_part{a}"] = pltpu.VMEM((2, rows // 8, width), BF)
            out[f"sc_cross{a}"] = pltpu.VMEM((3, rows // 8, width), BF)
        return out

    def first(self, a, j):
        p, src = self.place, self.sources[a]
        return remote(
            src.at[aligned(p.col_at(j), src.shape[0] // 4)],
            self.got[a].at[j],
            self.r.sc_send.at[a, j - 1],
            self.r.sc_recv.at[a, j - 1],
            {"col": p.col_at(j)},
        )

    def kept(self, a):
        src = self.sources[a]
        return pltpu.make_async_copy(
            src.at[aligned(self.place.col, src.shape[0] // 4)],
            self.got[a].at[0],
            self.r.sc_local.at[a, 0],
        )

    def start(self, which=None):
        for a in range(len(self.sources)) if which is None else which:
            for j in range(1, 4):
                self.first(a, j).start()
            self.kept(a).start()

    def second(self, a, slot, part, half, chan):
        return remote(
            self.part[a].at[part],
            self.cross[a].at[slot],
            self.r.sc_send.at[a, 3 + slot],
            self.r.sc_recv.at[a, 3 + slot],
            {"half": half, "chan": chan},
        )

    def middle(self):
        p = self.place
        for a in range(len(self.sources)):
            self.kept(a).wait()
            for j in range(1, 4):
                self.first(a, j).wait()
            rows = self.part[a].shape[1]
            for s in range(2):
                at = pl.ds(s * rows, rows)
                got = self.got[a]
                total = (got[0, at].astype(F32) + got[1, at].astype(F32)) + (
                    got[2, at].astype(F32) + got[3, at].astype(F32)
                )
                self.part[a][s] = total.astype(BF)

            @pl.when(p.own)
            def _():
                self.second(a, 0, p.other_half, p.other_half, p.chan).start()

            @pl.when(jnp.logical_not(p.own))
            def _():
                self.second(a, 0, p.half, p.half, p.far_chan).start()
                self.second(a, 1, p.other_half, p.other_half, p.far_chan).start()

    def finish(self):
        p = self.place
        for a in range(len(self.sources)):
            cross = self.cross[a]
            await_recv(cross.at[0], self.r.sc_recv.at[a, 3], self.r.sc_send.at[a, 3])
            await_send(cross.at[0], self.r.sc_send.at[a, 3], self.r.sc_recv.at[a, 3])

            @pl.when(p.own)
            def _():
                self.totals[a][...] = (
                    cross[0].astype(F32) + self.part[a][p.half].astype(F32)
                ).astype(BF)

            @pl.when(jnp.logical_not(p.own))
            def _():
                await_recv(cross.at[1], self.r.sc_recv.at[a, 4], self.r.sc_send.at[a, 4])
                await_send(cross.at[1], self.r.sc_send.at[a, 4], self.r.sc_recv.at[a, 4])
                self.totals[a][...] = (cross[0].astype(F32) + cross[1].astype(F32)).astype(BF)


class Spread:
    def __init__(self, place, r, totals, results):
        self.place, self.totals, self.results, self.r = place, totals, results, r

    @staticmethod
    def scratch(count):
        return dict(
            sp_send=pltpu.SemaphoreType.DMA((count, 7)),
            sp_recv=pltpu.SemaphoreType.DMA((count, 7)),
            sp_local=pltpu.SemaphoreType.DMA((count,)),
        )

    def each(self, which):
        return range(len(self.totals)) if which is None else which

    def slot(self, a, col, half):
        result = self.results[a]
        return result.at[aligned(col * 2 + half, result.shape[0] // 8)]

    def local(self, a):
        p = self.place
        return pltpu.make_async_copy(
            self.totals[a], self.slot(a, p.col, p.half), self.r.sp_local.at[a]
        )

    def out(self, a, j):
        p = self.place
        device = {"col": p.col_at(j)} if j else {"half": p.other_half}
        return remote(
            self.totals[a],
            self.slot(a, p.col, p.half),
            self.r.sp_send.at[a, j],
            self.r.sp_recv.at[a, j],
            device,
        )

    def pass_on(self, a, j):
        p = self.place
        piece = self.slot(a, p.col_at(4 - j), p.half)
        return remote(
            piece, piece, self.r.sp_send.at[a, 3 + j], self.r.sp_recv.at[a, 3 + j],
            {"half": p.other_half},
        )

    def start(self, which=None):
        for a in self.each(which):
            for j in (1, 2, 3, 0):
                self.out(a, j).start()
            self.local(a).start()

    def forward(self, which=None):
        p = self.place
        for a in self.each(which):
            for j in range(1, 4):
                piece = self.slot(a, p.col_at(4 - j), p.half)
                await_recv(piece, self.r.sp_recv.at[a, j], self.r.sp_send.at[a, j])
                self.pass_on(a, j).start()

    def finish(self, which=None):
        p = self.place
        for a in self.each(which):
            for j in range(4):
                self.out(a, j).wait_send()
            self.local(a).wait()
            await_recv(
                self.slot(a, p.col, p.other_half), self.r.sp_recv.at[a, 0], self.r.sp_send.at[a, 0]
            )
            for j in range(1, 4):
                self.pass_on(a, j).wait_send()
                piece = self.slot(a, p.col_at(4 - j), p.other_half)
                await_recv(piece, self.r.sp_recv.at[a, 3 + j], self.r.sp_send.at[a, 3 + j])


def call_kernel(body, ins, outs, scratch, collective_id, flops, hbm=()):
    names = list(ins) + list(outs) + list(scratch)

    def run(*refs):
        body(SimpleNamespace(**dict(zip(names, refs))))

    def spec(name):
        return pl.BlockSpec(memory_space=pl.ANY if name in hbm else pltpu.VMEM)

    results = pl.pallas_call(
        run,
        out_shape=[jax.ShapeDtypeStruct(*o) for o in outs.values()],
        in_specs=[spec(n) for n in ins],
        out_specs=[spec(n) for n in outs],
        scratch_shapes=list(scratch.values()),
        compiler_params=pltpu.CompilerParams(
            collective_id=collective_id, has_side_effects=True, vmem_limit_bytes=VMEM_LIMIT
        ),
        cost_estimate=pl.CostEstimate(flops=flops, bytes_accessed=20 << 20, transcendentals=0),
    )(*ins.values())
    return SimpleNamespace(**dict(zip(outs, results)))


def normalized(x):
    average = jnp.mean(x, 1, keepdims=True)
    centered = x - average
    variance = jnp.mean(centered * centered, 1, keepdims=True)
    inv = lax.rsqrt(variance + EPSILON)
    return centered * inv, inv


def norm_grad_rows(grad, x, gain):
    xhat, inv = normalized(x)
    gain_part = jnp.sum(grad * xhat, 0, keepdims=True)
    scaled = grad * gain
    mean_plain = jnp.mean(scaled, 1, keepdims=True)
    mean_cross = jnp.mean(scaled * xhat, 1, keepdims=True)
    return inv * (scaled - mean_plain - xhat * mean_cross), gain_part


def start_body(r):
    place = Place()
    exchange = Exchange(place, r, r.stream, r.pieces)
    fetch = Fetch(place, r, mixer_pairs(r, 0))
    length = r.seg.shape[0]
    place.barrier()
    exchange.start()
    own, other = place.own, jnp.logical_not(place.own)

    def gain_copy(j):
        chan = lax.rem(place.chan + j, 4)
        return remote(r.small, r.gain_parts.at[j], r.gain_send.at[j], r.gain_recv.at[j], {"chan": chan})

    for j in range(1, 4):
        gain_copy(j).start()
    seg_copy = remote(r.seg, r.seg_got, r.gain_send.at[4], r.gain_recv.at[4], {"half": place.other_half})
    taps_copy = remote(r.taps, r.taps_got, r.gain_send.at[5], r.gain_recv.at[5], {"chan": place.far_chan})

    @pl.when(own)
    def _():
        seg_copy.start()
        taps_copy.start()

    fetch.start()
    r.padded[0:PAD] = jnp.full((PAD, 1), -1, jnp.int32)
    r.padded[PAD + length : 2 * PAD + length] = jnp.full((PAD, 1), -1, jnp.int32)

    @pl.when(own)
    def _():
        r.padded[PAD : PAD + length] = r.seg[...]
        r.taps_out[...] = r.taps[...]
        seg_copy.wait_send()
        taps_copy.wait_send()

    @pl.when(other)
    def _():
        seg_copy.wait_recv()
        taps_copy.wait_recv()
        r.padded[PAD : PAD + length] = r.seg_got[...]
        r.taps_out[...] = r.taps_got[...]

    here = r.padded[PAD : PAD + length]
    r.mask_prev[...] = jnp.where(r.padded[PAD - 1 : PAD - 1 + length] == here, 1.0, 0.0)
    r.mask_next[...] = jnp.where(r.padded[PAD + 1 : PAD + 1 + length] == here, 1.0, 0.0)
    for j in range(1, 4):
        gain_copy(j).wait()
    r.gain_parts[0] = r.small[...]
    parts = []
    for c in range(4):
        parts.append(r.gain_parts[lax.rem(place.chan - c + 4, 4)])
    r.gains[...] = jnp.concatenate(parts, 1)
    exchange.finish()
    r.values[...] = jnp.concatenate([r.pieces[j] for j in range(4)], 1).astype(F32)
    fetch.forward()
    fetch.finish()


def mixer_pairs(r, l):
    return [
        (r.in_proj.at[l], r.n_in, 1, 8),
        (r.cond_in.at[l], r.n_ci, 1, 8),
        (r.cond_out.at[l], r.n_co, 1, 8),
        (r.out_proj.at[l], r.n_out, 0, 4),
        (r.filter_spec.at[l], r.n_spec, 1, 8),
    ]


def ffn_pairs(r, l):
    return [
        (r.gate_proj.at[l], r.n_gate, 0, 8),
        (r.up_proj.at[l], r.n_up, 0, 8),
        (r.down_proj.at[l], r.n_down, 0, 8),
    ]


SOURCES = {
    "mixer": dict(
        in_proj="in", cond_in="ci", cond_out="co", out_proj="out", filter_spec="spec"
    ),
    "ffn": dict(gate_proj="gate", up_proj="up", down_proj="down"),
}


def fetch_sources(arrays, kind):
    return {n: arrays[n] for n in SOURCES[kind]}


def fetch_results(arrays, kind):
    return {"n_" + t: (arrays[n].shape[1:], arrays[n].dtype) for n, t in SOURCES[kind].items()}


def loaded(r, l, kind, skip=()):
    return [
        (getattr(r, n).at[l], getattr(r, "f_" + t), getattr(r, "w_" + t))
        for n, t in SOURCES[kind].items()
        if t not in skip
    ]


def load_inputs(arrays, fetched, kind, skip=()):
    keep = {n: t for n, t in SOURCES[kind].items() if t not in skip}
    ins = {n: arrays[n] for n in keep}
    ins.update({"f_" + t: getattr(fetched, "n_" + t) for t in keep.values()})
    scratch = {
        "w_" + t: pltpu.VMEM(arrays[n].shape[1:], arrays[n].dtype) for n, t in keep.items()
    }
    return ins, dict(scratch, **Load.scratch(len(keep))), tuple(ins)


def begin(arrays, stream, seg, small, taps):
    length, shard = stream.shape
    rows, width = length // 4, arrays["in_proj"].shape[2]
    sources = fetch_sources(arrays, "mixer")
    gains = small.shape[0]
    return call_kernel(
        start_body,
        dict(stream=stream, seg=seg, small=small, taps=taps, **sources),
        dict(
            values=((rows, width), F32),
            gains=((gains, width), F32),
            taps_out=(taps.shape, F32),
            mask_prev=((length, 1), F32),
            mask_next=((length, 1), F32),
            **fetch_results(arrays, "mixer"),
        ),
        dict(
            pieces=pltpu.VMEM((4, rows, shard), BF),
            gain_parts=pltpu.VMEM((4, gains, shard), F32),
            gain_send=pltpu.SemaphoreType.DMA((6,)),
            gain_recv=pltpu.SemaphoreType.DMA((6,)),
            seg_got=pltpu.VMEM((length, 1), jnp.int32),
            taps_got=pltpu.VMEM(taps.shape, F32),
            padded=pltpu.VMEM((length + 2 * PAD, 1), jnp.int32),
            **Exchange.scratch(),
            **Fetch.scratch(5),
        ),
        1,
        10**6,
        ("stream",) + tuple(sources),
    )


def ffn_forward_body(l, last, r):
    place = Place()
    rows = r.mid.shape[0]
    group = Group(place, r, rows)
    load = Load(place, r, loaded(r, l, "ffn"))
    load.start()
    layers = r.gains.shape[0] // 2
    gain = r.gains[layers + l : layers + l + 1]
    xhat, _ = normalized(r.mid[...])
    r.h_all[group.at(0)] = (xhat * gain).astype(BF)
    place.barrier()
    group.gather_start(r.h_all)
    if last:
        extra = Exchange(place, r, r.cotangent, r.pieces)
    else:
        extra = Fetch(place, r, mixer_pairs(r, l + 1))
    extra.start()
    load.finish()

    def block(at):
        h = r.h_all[at]
        gate = nn_dot(h, r.w_gate[...])
        up = nn_dot(h, r.w_up[...])
        r.gate_all[at] = gate.astype(BF)
        r.up_all[at] = up.astype(BF)
        hidden = (gate * normal_cdf(gate) * up).astype(BF)
        return nn_dot(hidden, r.w_down[...])

    r.out[...] = r.mid[...] + block(group.at(0))
    group.gather_peer(r.h_all)
    group.reduce_whole("peer", block(group.at(2)))
    for chunk in range(CHUNKS):
        group.gather_near(r.h_all, chunk)
        r.near_part[group.piece(chunk)] = block(group.at(1, chunk))
        group.gather_diagonal(r.h_all, chunk)
        group.reduce_peer(1, chunk, block(group.at(3, chunk)))
        group.reduce_near(chunk, r.near_part[group.piece(chunk)])
    if not last:
        extra.forward()
    for chunk in range(CHUNKS):
        r.out[group.piece(chunk)] += group.reduce_end(chunk)
    group.finish()
    extra.finish()
    if last:
        r.carried[...] = jnp.concatenate([r.pieces[j] for j in range(4)], 1).astype(F32)


def ffn_forward(l, arrays, mid, gains, fetched, cotangent):
    rows, width = mid.shape
    units = arrays["gate_proj"].shape[2]
    full = rows * 4
    last = l + 1 == arrays["in_proj"].shape[0]
    ins, scratch, hbm = load_inputs(arrays, fetched, "ffn")
    outs = dict(
        out=((rows, width), F32),
        h_all=((full, width), BF),
        gate_all=((full, units), BF),
        up_all=((full, units), BF),
    )
    if last:
        ins.update(cotangent=cotangent)
        outs.update(carried=((rows, width), F32))
        scratch.update(
            pieces=pltpu.VMEM((4, rows, cotangent.shape[1]), BF), **Exchange.scratch()
        )
        hbm += ("cotangent",)
    else:
        sources = fetch_sources(arrays, "mixer")
        ins.update(sources)
        outs.update(fetch_results(arrays, "mixer"))
        scratch.update(Fetch.scratch(5))
        hbm += tuple(sources)
    return call_kernel(
        functools.partial(ffn_forward_body, l, last),
        dict(mid=mid, gains=gains, **ins),
        outs,
        dict(
            near_part=pltpu.VMEM((rows, width), F32), **Group.scratch(rows, width), **scratch
        ),
        10 + l,
        6 * full * width * units,
        hbm,
    )


def ffn_backward_body(l, last, r):
    place = Place()
    rows, width = r.mid.shape
    units = r.gate_all.shape[1]
    group = Group(place, r, rows)
    load = Load(place, r, loaded(r, l, "ffn"))
    load.start()
    layers = r.gains.shape[0] // 2
    gain = r.gains[layers + l : layers + l + 1]
    r.g_all[group.at(0)] = r.carried[...].astype(BF)
    if last:
        shard = r.returned.shape[1]
        for j in range(4):
            r.leaving[j] = r.values[:, j * shard : (j + 1) * shard].astype(BF)
        back = Return(place, r, r.leaving, r.returned)
    place.barrier()
    group.gather_start(r.g_all)
    if last:
        back.start()
    else:
        spread = Spread(place, r, [r.ffn_total], [r.ffn_result])
        scatter = Scatter(place, r, mixer_grads(r), mixer_totals(r))
        spread.start()
        scatter.start()

    load.finish()

    def block(at):
        hidden_grad = nt_dot(r.g_all[at], r.w_down[...])
        gate = r.gate_all[at].astype(F32)
        up = r.up_all[at].astype(F32)
        cdf = normal_cdf(gate)
        act = gate * cdf
        r.hidden_all[at] = (act * up).astype(BF)
        gate_grad = (hidden_grad * up * (cdf + gate * normal_pdf(gate))).astype(BF)
        up_grad = (hidden_grad * act).astype(BF)
        r.gate_grads[at] = gate_grad
        r.up_grads[at] = up_grad
        return nt_dot(gate_grad, r.w_gate[...]) + nt_dot(up_grad, r.w_up[...])

    r.own_part[...] = block(group.at(0))
    group.gather_peer(r.g_all)
    group.reduce_whole("peer", block(group.at(2)))
    for chunk in range(CHUNKS):
        group.gather_near(r.g_all, chunk)
        r.near_part[group.piece(chunk)] = block(group.at(1, chunk))
        group.gather_diagonal(r.g_all, chunk)
        group.reduce_peer(1, chunk, block(group.at(3, chunk)))
        group.reduce_near(chunk, r.near_part[group.piece(chunk)])
    step = 256
    for u in range(units // step):
        cols = pl.ds(u * step, step)
        r.weight_grads[0 * width : 1 * width, cols] = tn_dot(r.h_all[...], r.gate_grads[:, cols]).astype(BF)
        r.weight_grads[1 * width : 2 * width, cols] = tn_dot(r.h_all[...], r.up_grads[:, cols]).astype(BF)
        r.weight_grads[pl.ds(2 * width + u * step, step)] = tn_dot(r.hidden_all[:, cols], r.g_all[...]).astype(BF)
    if not last:
        spread.forward()
        scatter.middle()
    for chunk in range(CHUNKS):
        r.own_part[group.piece(chunk)] += group.reduce_end(chunk)
    grad, gain_part = norm_grad_rows(r.own_part[...], r.mid[...], gain)
    r.mid_grad[...] = r.carried[...] + grad
    r.gain_grad[...] = gain_part
    group.finish()
    if last:
        back.finish()
        r.output[...] = r.returned[...].astype(F32)
    else:
        spread.finish()
        scatter.finish()


def mixer_grads(r):
    return [r.g_in, r.g_spec, r.g_out, r.g_mlp, r.g_small]


def mixer_totals(r):
    return [r.t_in, r.t_spec, r.t_out, r.t_mlp, r.t_small]


def mixer_results(r):
    return [r.r_in, r.r_spec, r.r_out, r.r_mlp, r.r_small]


GRADS = ("in", "spec", "out", "mlp", "small")


def ffn_backward(l, arrays, carried, mid, gains, fetched, saved, values, shard, pending):
    rows, width = mid.shape
    units = arrays["gate_proj"].shape[2]
    full = rows * 4
    last = values is not None
    big = pltpu.VMEM((full, units), BF)
    load_ins, load_scratch, hbm = load_inputs(arrays, fetched, "ffn")
    ins = dict(carried=carried, mid=mid, gains=gains, **load_ins, **saved)
    outs = dict(
        mid_grad=((rows, width), F32),
        weight_grads=((3 * width, units), BF),
        gain_grad=((1, width), F32),
    )
    if last:
        ins.update(values=values)
        outs.update(output=((full, shard), F32))
        scratch = dict(
            leaving=pltpu.VMEM((4, rows, shard), BF),
            returned=pltpu.VMEM((full, shard), BF),
            **Return.scratch(),
        )
    else:
        grads, ffn_total = pending
        ins.update(ffn_total=ffn_total, **{"g_" + n: grads[n] for n in GRADS})
        outs.update(
            ffn_result=((8 * ffn_total.shape[0], ffn_total.shape[1]), BF),
            **totals_of(grads),
        )
        scratch = dict(**Spread.scratch(1), **Scatter.scratch([grads[n].shape for n in GRADS]))
        hbm += tuple("g_" + n for n in GRADS)
    return call_kernel(
        functools.partial(ffn_backward_body, l, last),
        ins,
        outs,
        dict(
            near_part=pltpu.VMEM((rows, width), F32),
            own_part=pltpu.VMEM((rows, width), F32),
            g_all=pltpu.VMEM((full, width), BF),
            hidden_all=big,
            gate_grads=big,
            up_grads=big,
            **Group.scratch(rows, width),
            **load_scratch,
            **scratch,
        ),
        20 + l,
        12 * full * width * units,
        hbm,
    )


def totals_of(grads):
    return {"t_" + n: ((grads[n].shape[0] // 8, grads[n].shape[1]), BF) for n in GRADS}


PAD = 8


def shifted(ref, s, tile, size, offset):
    return ref[s, pl.ds(PAD + tile * size + offset, size)]


def mlp_tables(r):
    groups, feats, inner = r.w_ci.shape
    half = feats // 2
    for table in (r.in_re, r.in_im, r.out_re, r.out_im):
        table[...] = jnp.zeros_like(table)
    for g in range(groups):
        rows, cols = pl.ds(g * half, half), pl.ds(g * inner, inner)
        r.in_re[rows, cols] = r.w_ci[g, 0:half].astype(BF)
        r.in_im[rows, cols] = r.w_ci[g, half:feats].astype(BF)
        turned = r.w_co[g].T
        r.out_re[rows, cols] = turned[0:half].astype(BF)
        r.out_im[rows, cols] = turned[half:feats].astype(BF)


def mlp_scratch(shard, inner):
    table = pltpu.VMEM((shard, inner), BF)
    return dict(in_re=table, in_im=table, out_re=table, out_im=table)


def mixer_forward_body(l, r):
    place = Place()
    rows = r.values.shape[0]
    length = r.h_all.shape[0]
    lanes = r.w_in.shape[2]
    wide = r.both.shape[1] // 2
    tiles = 4
    size = length // tiles
    group = Group(place, r, rows)
    load = Load(place, r, loaded(r, l, "mixer"))
    load.start()
    xhat, _ = normalized(r.values[...])
    r.h_all[group.at(0)] = (xhat * r.gains[l : l + 1]).astype(BF)
    place.barrier()
    group.gather_start(r.h_all)
    fetch = Fetch(place, r, ffn_pairs(r, l))
    fetch.start()
    for s in range(3):
        r.padded[s, 0:PAD] = jnp.zeros((PAD, lanes), F32)
        r.padded[s, PAD + length : 2 * PAD + length] = jnp.zeros((PAD, lanes), F32)
    r.both[...] = jnp.zeros_like(r.both)
    load.finish()
    mlp_tables(r)

    def project(which, chunk=None):
        at = group.at(which, chunk)
        h = r.h_all[at]
        for s in range(3):
            proj = nn_dot(h, r.w_in[s])
            r.padded[s, pl.ds(pl.multiple_of(at.start + PAD, 8), at.size)] = proj
            r.proj_all[s, at] = proj.astype(BF)

    project(0)
    group.gather_peer(r.h_all)
    project(2)
    for chunk in range(CHUNKS):
        group.gather_near(r.h_all, chunk)
        project(1, chunk)
        group.gather_diagonal(r.h_all, chunk)
        project(3, chunk)

    def tap(o, s):
        at = 9 * l + 3 * o + s
        return r.taps[at : at + 1]

    for t in range(tiles):
        at = pl.ds(t * size, size)
        prev = r.mask_prev[at]
        following = r.mask_next[at]
        shorts = []
        for s in range(3):
            shorts.append(
                tap(0, s) * shifted(r.padded, s, t, size, -1) * prev
                + tap(1, s) * shifted(r.padded, s, t, size, 0)
                + tap(2, s) * shifted(r.padded, s, t, size, 1) * following
            )
        r.query_all[at] = shorts[0].astype(BF)
        r.both[at, 0:lanes] = shorts[1].astype(BF)
        r.both[at, wide : wide + lanes] = shorts[2].astype(BF)

    @pl.loop(0, tiles)
    def _(t):
        at = aligned(t, size)
        real = nn_dot(r.cosine[at], r.both[...])
        imag = nn_dot(r.sine[at], r.both[...])
        value_re, cond_re = real[:, :lanes], real[:, wide : wide + lanes].astype(BF)
        value_im, cond_im = imag[:, :lanes], imag[:, wide : wide + lanes].astype(BF)
        pre = nn_dot(cond_re, r.in_re[...]) + nn_dot(cond_im, r.in_im[...])
        inner = (pre * normal_cdf(pre)).astype(BF)
        kernel_re = r.w_spec[0, at] + nt_dot(inner, r.out_re[...])
        kernel_im = r.w_spec[1, at] + nt_dot(inner, r.out_im[...])
        r.prod_re[at] = (value_re * kernel_re - value_im * kernel_im).astype(BF)
        r.prod_im[at] = (value_re * kernel_im + value_im * kernel_re).astype(BF)
        r.pre_all[at] = pre.astype(BF)
        for i, x in enumerate((value_re, value_im, kernel_re, kernel_im, cond_re, cond_im)):
            r.spectra[i, at] = x.astype(BF)

    fetch.forward()

    def project_out(which):
        at = group.at(which)
        mixed = nn_dot(r.cosine[at], r.prod_re[...]) + nn_dot(r.sine[at], r.prod_im[...])
        r.mixed_all[at] = mixed.astype(BF)
        gated = (r.query_all[at].astype(F32) * mixed).astype(BF)
        r.gated_all[at] = gated
        return nn_dot(gated, r.w_out[...])

    group.reduce_whole("diagonal", project_out(3))
    group.reduce_whole("near", project_out(1))
    group.reduce_whole("peer", project_out(2))
    r.out[...] = r.values[...] + project_out(0)
    for chunk in range(CHUNKS):
        r.out[group.piece(chunk)] += group.reduce_end(chunk)
    group.finish()
    fetch.finish()


def mixer_forward(l, arrays, values, gains, taps, masks, fetched, tables):
    rows, width = values.shape
    length, lanes = arrays["filter_spec"].shape[2:]
    groups, _, units = arrays["cond_in"].shape[1:]
    wide = -(-lanes // 128) * 128
    inner = groups * units
    ins, scratch, hbm = load_inputs(arrays, fetched, "mixer")
    sources = fetch_sources(arrays, "ffn")
    return call_kernel(
        functools.partial(mixer_forward_body, l),
        dict(
            values=values, gains=gains, taps=taps, mask_prev=masks[0], mask_next=masks[1],
            cosine=tables[0], sine=tables[1], **ins, **sources,
        ),
        dict(
            out=((rows, width), F32),
            h_all=((length, width), BF),
            proj_all=((3, length, lanes), BF),
            query_all=((length, lanes), BF),
            mixed_all=((length, lanes), BF),
            spectra=((6, length, lanes), BF),
            pre_all=((length, inner), BF),
            gated_all=((length, lanes), BF),
            **fetch_results(arrays, "ffn"),
        ),
        dict(
            padded=pltpu.VMEM((3, length + 2 * PAD, lanes), F32),
            both=pltpu.VMEM((length, 2 * wide), BF),
            prod_re=pltpu.VMEM((length, lanes), BF),
            prod_im=pltpu.VMEM((length, lanes), BF),
            **mlp_scratch(lanes, inner),
            **Group.scratch(rows, width),
            **Fetch.scratch(3),
            **scratch,
        ),
        30 + l,
        6 * 10**9,
        hbm + tuple(sources),
    )


def mixer_backward_body(l, last, r):
    place = Place()
    rows = r.values.shape[0]
    length, width = r.h_all.shape
    lanes = r.w_in.shape[2]
    groups, feats, units = r.w_ci.shape
    half = feats // 2
    wide = r.both_re.shape[1] // 2
    tiles = 4
    size = length // tiles
    group = Group(place, r, rows)
    load = Load(place, r, loaded(r, l, "mixer", ("spec",)))
    load.start()
    r.m_all[group.at(0)] = r.mid_grad[...].astype(BF)
    place.barrier()
    group.gather_start(r.m_all)
    scatter = Scatter(place, r, [r.ffn_grads], [r.ffn_total])
    scatter.start()
    if not last:
        spread = Spread(place, r, mixer_totals(r), mixer_results(r))
        spread.start()
    for s in range(3):
        r.padded[s, 0:PAD] = jnp.zeros((PAD, lanes), F32)
        r.padded[s, PAD + length : 2 * PAD + length] = jnp.zeros((PAD, lanes), F32)
    r.both_re[...] = jnp.zeros_like(r.both_re)
    r.both_im[...] = jnp.zeros_like(r.both_im)
    r.sum_in[...] = jnp.zeros_like(r.sum_in)
    r.sum_out[...] = jnp.zeros_like(r.sum_out)
    load.finish()
    mlp_tables(r)

    def gated_back(which, chunk=None):
        at = group.at(which, chunk)
        gated_grad = nt_dot(r.m_all[at], r.w_out[...])
        to = pl.ds(pl.multiple_of(at.start + PAD, 8), at.size)
        r.padded[0, to] = gated_grad * r.mixed_all[at].astype(F32)
        r.q_g[at] = (gated_grad * r.query_all[at].astype(F32)).astype(BF)

    gated_back(0)
    group.gather_peer(r.m_all)
    gated_back(2)
    for chunk in range(CHUNKS):
        group.gather_near(r.m_all, chunk)
        gated_back(1, chunk)
        group.gather_diagonal(r.m_all, chunk)
        gated_back(3, chunk)

    @pl.loop(0, tiles)
    def _(t):
        at = aligned(t, size)
        real = nn_dot(r.cosine[at], r.q_g[...])
        imag = nn_dot(r.sine[at], r.q_g[...])
        value_re, value_im, kernel_re, kernel_im = [r.spectra[i, at].astype(F32) for i in range(4)]
        kernel_re_grad = (real * value_re + imag * value_im).astype(BF)
        kernel_im_grad = (imag * value_re - real * value_im).astype(BF)
        r.both_re[at, 0:lanes] = (real * kernel_re + imag * kernel_im).astype(BF)
        r.both_im[at, 0:lanes] = (imag * kernel_re - real * kernel_im).astype(BF)
        r.g_spec[at] = kernel_re_grad
        r.g_spec[pl.ds(pl.multiple_of(length + t * size, size), size)] = kernel_im_grad
        pre = r.pre_all[at].astype(F32)
        cdf = normal_cdf(pre)
        inner = (pre * cdf).astype(BF)
        inner_grad = nn_dot(kernel_re_grad, r.out_re[...]) + nn_dot(kernel_im_grad, r.out_im[...])
        pre_grad = (inner_grad * (cdf + pre * normal_pdf(pre))).astype(BF)
        r.both_re[at, wide : wide + lanes] = nt_dot(pre_grad, r.in_re[...]).astype(BF)
        r.both_im[at, wide : wide + lanes] = nt_dot(pre_grad, r.in_im[...]).astype(BF)
        r.sum_out[0] += tn_dot(kernel_re_grad, inner)
        r.sum_out[1] += tn_dot(kernel_im_grad, inner)
        r.sum_in[0] += tn_dot(r.spectra[4, at], pre_grad)
        r.sum_in[1] += tn_dot(r.spectra[5, at], pre_grad)

    @pl.loop(0, tiles)
    def _(t):
        at = aligned(t, size)
        both = nn_dot(r.cosine[at], r.both_re[...]) + nn_dot(r.sine[at], r.both_im[...])
        to = pl.ds(pl.multiple_of(t * size + PAD, 8), size)
        r.padded[1, to] = both[:, :lanes]
        r.padded[2, to] = both[:, wide : wide + lanes]

    def tap(o, s):
        at = 9 * l + 3 * o + s
        return r.taps[at : at + 1]

    r.g_small[...] = jnp.zeros_like(r.g_small)
    totals = [[None] * 3 for _ in range(3)]
    for t in range(tiles):
        at = pl.ds(t * size, size)
        prev = r.mask_prev[at]
        following = r.mask_next[at]
        for s in range(3):
            here = shifted(r.padded, s, t, size, 0)
            after = shifted(r.padded, s, t, size, 1) * following
            before = shifted(r.padded, s, t, size, -1) * prev
            r.proj_grads[s, at] = (
                tap(0, s) * after + tap(1, s) * here + tap(2, s) * before
            ).astype(BF)
            proj = r.proj_all[s, at].astype(F32)
            for o, g in enumerate((after, here, before)):
                part = jnp.sum(g * proj, 0, keepdims=True)
                totals[o][s] = part if t == 0 else totals[o][s] + part
    small = [totals[o][s] for o in range(3) for s in range(3)]

    def feats_grad(which):
        at = group.at(which)
        return sum(nt_dot(r.proj_grads[s, at], r.w_in[s]) for s in range(3))

    group.reduce_whole("diagonal", feats_grad(3))
    group.reduce_whole("near", feats_grad(1))
    group.reduce_whole("peer", feats_grad(2))
    r.own_part[...] = feats_grad(0)
    if not last:
        spread.forward()
    for s in range(3):
        r.g_in[s * width : (s + 1) * width] = tn_dot(r.h_all[...], r.proj_grads[s]).astype(BF)
    shard = r.w_out.shape[0]
    r.g_out[0:shard] = tn_dot(r.gated_all[...], r.m_all[...]).astype(BF)
    r.g_out[shard:] = jnp.zeros((r.g_out.shape[0] - shard, width), BF)
    for g in range(groups):
        rows_at, cols = slice(g * half, (g + 1) * half), slice(g * units, (g + 1) * units)
        at = g * feats
        r.g_mlp[at : at + half] = r.sum_in[0, rows_at, cols].astype(BF)
        r.g_mlp[at + half : at + feats] = r.sum_in[1, rows_at, cols].astype(BF)
        turned = jnp.concatenate([r.sum_out[0, rows_at, cols], r.sum_out[1, rows_at, cols]], 0)
        at += groups * feats
        r.g_mlp[at : at + units] = turned.T.astype(BF)
    for chunk in range(CHUNKS):
        r.own_part[group.piece(chunk)] += group.reduce_end(chunk)
    grad, gain_part = norm_grad_rows(r.own_part[...], r.values[...], r.gains[l : l + 1])
    r.carried[...] = r.mid_grad[...] + grad
    third = width // 3
    for i in range(3):
        small.append(gain_part[:, i * third : (i + 1) * third])
    for i in range(3):
        small.append(r.gain_two[:, i * third : (i + 1) * third])
    for i, x in enumerate(small):
        r.small_rows[i : i + 1, 0 : x.shape[1]] = x
    r.g_small[0:16] = r.small_rows[...].astype(BF)
    scatter.middle()
    group.finish()
    scatter.finish()
    if not last:
        spread.finish()


def mixer_backward(
    l, arrays, mid_grad, values, gains, taps, masks, fetched, tables, saved, gain_two, ffn_grads,
    pending,
):
    rows, width = values.shape
    length, lanes = saved["query_all"].shape
    groups, feats, units = arrays["cond_in"].shape[1:]
    inner = groups * units
    wide = -(-lanes // 128) * 128
    last = pending is None
    load_ins, load_scratch, hbm = load_inputs(arrays, fetched, "mixer", ("spec",))
    ins = dict(
        mid_grad=mid_grad, values=values, gains=gains, taps=taps, mask_prev=masks[0],
        mask_next=masks[1], cosine=tables[0], sine=tables[1], gain_two=gain_two,
        ffn_grads=ffn_grads, **load_ins, **saved,
    )
    grads = dict(
        g_in=((3 * width, lanes), BF),
        g_spec=((2 * length, lanes), BF),
        g_out=((-(-lanes // 128) * 128, width), BF),
        g_mlp=((2 * groups * feats, units), BF),
        g_small=((128, width // 3), BF),
    )
    outs = dict(
        carried=((rows, width), F32),
        ffn_total=((ffn_grads.shape[0] // 8, ffn_grads.shape[1]), BF),
        **grads,
    )
    scratch = dict(Scatter.scratch([ffn_grads.shape]), **load_scratch)
    hbm += ("ffn_grads",)
    if not last:
        ins.update(**{"t_" + n: pending[n] for n in GRADS})
        outs.update(
            **{"r_" + n: ((pending[n].shape[0] * 8, pending[n].shape[1]), BF) for n in GRADS}
        )
        scratch.update(Spread.scratch(len(GRADS)))
    return call_kernel(
        functools.partial(mixer_backward_body, l, last),
        ins,
        outs,
        dict(
            m_all=pltpu.VMEM((length, width), BF),
            padded=pltpu.VMEM((3, length + 2 * PAD, lanes), F32),
            q_g=pltpu.VMEM((length, lanes), BF),
            both_re=pltpu.VMEM((length, 2 * wide), BF),
            both_im=pltpu.VMEM((length, 2 * wide), BF),
            proj_grads=pltpu.VMEM((3, length, lanes), BF),
            own_part=pltpu.VMEM((rows, width), F32),
            sum_in=pltpu.VMEM((2, lanes, inner), F32),
            sum_out=pltpu.VMEM((2, lanes, inner), F32),
            small_rows=pltpu.VMEM((16, width // 3), F32),
            **mlp_scratch(lanes, inner),
            **Group.scratch(rows, width),
            **scratch,
        ),
        40 + l,
        9 * 10**9,
        hbm,
    )


def end_body(r):
    place = Place()
    scatter = Scatter(place, r, mixer_grads(r), mixer_totals(r))
    shard = r.returned.shape[1]
    for j in range(4):
        r.leaving[j] = r.carried[:, j * shard : (j + 1) * shard].astype(BF)
    back = Return(place, r, r.leaving, r.returned)
    spread = Spread(
        place, r, mixer_totals(r) + [r.ffn_total], mixer_results(r) + [r.ffn_result]
    )
    place.barrier()
    scatter.start()
    back.start()
    spread.start([5])
    scatter.middle()
    spread.forward([5])
    scatter.finish()
    spread.start(range(5))
    back.finish()
    r.stream_grad[...] = r.returned[...].astype(F32)
    spread.forward(range(5))
    spread.finish(range(6))

    layers = r.gain_parts.shape[1]
    r.gain_parts[0, 0] = r.r_small[0:16]
    for l in range(1, layers):
        r.gain_parts[0, l] = r.above[l - 1]

    def gain_copy(j):
        chan = lax.rem(place.chan + j, 4)
        return remote(
            r.gain_parts.at[0], r.gain_parts.at[j], r.gain_send.at[j], r.gain_recv.at[j], {"chan": chan}
        )

    for j in range(1, 4):
        gain_copy(j).start()
    for j in range(1, 4):
        gain_copy(j).wait()
    total = r.gain_parts[0].astype(F32)
    for j in range(1, 4):
        total += r.gain_parts[j].astype(F32)
    r.gain_grads[...] = total


def end(carried, shard, grads, ffn_total, above):
    rows, width = carried.shape
    layers = 1 + above.shape[0]
    shapes = [grads[n].shape for n in GRADS]
    hbm = tuple("g_" + n for n in GRADS)
    return call_kernel(
        end_body,
        dict(
            carried=carried, ffn_total=ffn_total, above=above,
            **{"g_" + n: grads[n] for n in GRADS},
        ),
        dict(
            stream_grad=((rows * 4, shard), F32),
            gain_grads=((layers, 16, width // 3), F32),
            ffn_result=((8 * ffn_total.shape[0], ffn_total.shape[1]), BF),
            **{"r_" + n: (grads[n].shape, BF) for n in GRADS},
        ),
        dict(
            leaving=pltpu.VMEM((4, rows, shard), BF),
            returned=pltpu.VMEM((rows * 4, shard), BF),
            gain_parts=pltpu.VMEM((4, layers, 16, width // 3), BF),
            gain_send=pltpu.SemaphoreType.DMA((4,)),
            gain_recv=pltpu.SemaphoreType.DMA((4,)),
            **{n: pltpu.VMEM(*s) for n, s in totals_of(grads).items()},
            **Return.scratch(),
            **Scatter.scratch(shapes),
            **Spread.scratch(len(GRADS) + 1),
        ),
        50,
        10**6,
        hbm,
    )


def on_device(
    stream,
    segments,
    cotangent,
    norm_one,
    in_proj,
    short_taps,
    cond_in,
    cond_out,
    filter_spec,
    out_proj,
    norm_two,
    gate_proj,
    up_proj,
    down_proj,
):
    chan = lax.axis_index("chan")
    layers, width = in_proj.shape[:2]
    shard = norm_one.shape[1]
    length = filter_spec.shape[2]
    groups, feats = cond_in.shape[1:3]
    tables = dft_tables(length)
    arrays = dict(
        in_proj=in_proj.transpose(0, 2, 1, 3),
        cond_in=cond_in,
        cond_out=cond_out,
        filter_spec=filter_spec,
        out_proj=out_proj,
        gate_proj=gate_proj,
        up_proj=up_proj,
        down_proj=down_proj,
    )

    def kept(result, names):
        return {n: getattr(result, n) for n in names}

    first = begin(
        arrays,
        stream,
        segments[:, None],
        jnp.concatenate([norm_one, norm_two], 0),
        short_taps.reshape(-1, shard),
    )
    gains, taps = first.gains, first.taps_out
    masks = (first.mask_prev, first.mask_next)
    values = first.values
    mixer_fetched = first
    saved = []
    for l in range(layers):
        mixed = mixer_forward(l, arrays, values, gains, taps, masks, mixer_fetched, tables)
        after = ffn_forward(l, arrays, mixed.out, gains, mixed, cotangent)
        saved.append((values, mixer_fetched, mixed, after))
        values, mixer_fetched = after.out, after
    carried = after.carried

    ffn_results, mixer_results_ = {}, {}
    grads, ffn_total, output = None, None, None
    for l in reversed(range(layers)):
        layer_in, mixer_fetched, mixed, after = saved[l]
        last = l + 1 == layers
        back = ffn_backward(
            l, arrays, carried, mixed.out, gains, mixed,
            kept(after, ("h_all", "gate_all", "up_all")),
            values if last else None, shard, None if last else (grads, ffn_total),
        )
        if last:
            output, pending = back.output, None
        else:
            ffn_results[l + 1] = back.ffn_result
            pending = {n: getattr(back, "t_" + n) for n in GRADS}
        saves = kept(
            mixed,
            ("h_all", "proj_all", "query_all", "mixed_all", "spectra", "pre_all", "gated_all"),
        )
        down = mixer_backward(
            l, arrays, back.mid_grad, layer_in, gains, taps, masks, mixer_fetched, tables, saves,
            back.gain_grad, back.weight_grads, pending,
        )
        if not last:
            mixer_results_[l + 1] = {n: getattr(down, "r_" + n) for n in GRADS}
        carried, ffn_total = down.carried, down.ffn_total
        grads = {n: getattr(down, "g_" + n) for n in GRADS}
    above = jnp.stack([mixer_results_[l]["small"][:16] for l in range(1, layers)])
    final = end(carried, shard, grads, ffn_total, above)
    ffn_results[0] = final.ffn_result
    mixer_results_[0] = {n: getattr(final, "r_" + n) for n in GRADS}

    def everywhere(x):
        return lax.psum(x, "outer") if lax.axis_size("outer") > 1 else x

    def stacked(get):
        return everywhere(jnp.stack([get(l) for l in range(layers)])).astype(F32)

    def mixer_stack(name, get):
        return stacked(lambda l: get(mixer_results_[l][name]))

    def ffn_stack(index):
        return stacked(lambda l: ffn_results[l][index * width : (index + 1) * width])

    gain_grads = everywhere(final.gain_grads)

    def gain_stack(at):
        whole = gain_grads[:, at : at + 3].reshape(layers, width)
        return lax.dynamic_slice_in_dim(whole, chan * shard, shard, 1)

    mlp_rows = groups * feats
    return (
        output,
        final.stream_grad,
        gain_stack(9),
        mixer_stack("in", lambda x: x.reshape(3, width, shard).transpose(1, 0, 2)),
        mixer_stack("small", lambda x: x[:9, :shard].reshape(short_taps.shape[1:])),
        mixer_stack("mlp", lambda x: x[:mlp_rows].reshape(cond_in.shape[1:])),
        mixer_stack("mlp", lambda x: x[mlp_rows:].reshape(cond_out.shape[1:])),
        mixer_stack("spec", lambda x: x.reshape(filter_spec.shape[1:])),
        mixer_stack("out", lambda x: x[:shard]),
        gain_stack(12),
        ffn_stack(0),
        ffn_stack(1),
        ffn_stack(2),
    )


def solution(mesh):
    dp_count, chan_count = mesh.devices.shape
    fine = Mesh(
        mesh.devices.reshape(dp_count // 8, 4, 2, chan_count), ("outer", "col", "half", "chan")
    )
    dp = ("outer", "col", "half")
    weight_specs = (
        P(None, "chan"),
        P(None, None, None, "chan"),
        P(None, None, None, "chan"),
        P(None, "chan", None, None),
        P(None, "chan", None, None),
        P(None, None, None, "chan"),
        P(None, "chan", None),
        P(None, "chan"),
        P(None, None, "chan"),
        P(None, None, "chan"),
        P(None, "chan", None),
    )
    return jax.shard_map(
        on_device,
        mesh=fine,
        in_specs=(P(dp, "chan"), P(dp), P(dp, "chan")) + weight_specs,
        out_specs=(P(dp, "chan"), P(dp, "chan")) + weight_specs,
        check_vma=False,
    )
```

```python
import functools
import math
from types import SimpleNamespace

import jax
import jax.numpy as jnp
import numpy as np
from jax import lax
from jax.experimental import pallas as pl
from jax.experimental.pallas import tpu as pltpu
from jax.sharding import Mesh
from jax.sharding import PartitionSpec as P

EPSILON = 1e-05
BF = jnp.bfloat16
F32 = jnp.float32


def dft_tables(length):
    positions = np.arange(length)
    angles = (positions[:, None] * positions[None, :] % length) * (2.0 * math.pi / length)
    scale = 1.0 / math.sqrt(length)
    cosine = np.asarray(np.cos(angles) * scale, dtype=np.float32)
    sine = np.asarray(-np.sin(angles) * scale, dtype=np.float32)
    return jnp.asarray(cosine, BF), jnp.asarray(sine, BF)


def normal_cdf(x):
    return 0.5 * (1.0 + lax.erf(x * (2.0**-0.5)))


def normal_pdf(x):
    return jnp.exp(-0.5 * x * x) * (1.0 / math.sqrt(2.0 * math.pi))


MESH = pl.DeviceIdType.MESH
VMEM_LIMIT = 58 << 20
CHUNKS = 2
PARTS = 8


def nt_dot(a, b):
    return lax.dot_general(a, b, (((1,), (1,)), ((), ())), preferred_element_type=F32)


def tn_dot(a, b):
    return lax.dot_general(a, b, (((0,), (0,)), ((), ())), preferred_element_type=F32)


def nn_dot(a, b):
    return jnp.dot(a, b, preferred_element_type=F32)


def aligned(index, size):
    return pl.ds(pl.multiple_of(index * size, size), size)


class Place:
    def __init__(self):
        self.col = lax.axis_index("col")
        self.half = lax.axis_index("half")
        self.chan = lax.axis_index("chan")
        odd = lax.rem(self.chan, 2)
        self.pack = self.chan // 2
        self.own = self.half == self.pack
        self.other_half = 1 - self.half
        self.near_chan = self.chan + 1 - 2 * odd
        self.far_chan = self.chan + 2 - 4 * self.pack
        self.rank = 2 * self.half + odd
        flip_near, flip_peer = 1 - 2 * odd, 2 - 4 * self.half
        self.ranks = [
            self.rank,
            self.rank + flip_near,
            self.rank + flip_peer,
            self.rank + flip_near + flip_peer,
        ]

    def col_at(self, step):
        return lax.rem(self.col + step, 4)

    def barrier(self):
        sem = pltpu.get_barrier_semaphore()
        devices = [{"col": self.col_at(j)} for j in range(1, 4)]
        for i in range(1, 8):
            half = self.half if i < 4 else self.other_half
            devices.append({"half": half, "chan": lax.rem(self.chan + i, 4)})
        for device in devices:
            pl.semaphore_signal(sem, inc=1, device_id=device, device_id_type=MESH)
        pl.semaphore_wait(sem, len(devices))


def remote(src, dst, send_sem, recv_sem, device):
    return pltpu.make_async_remote_copy(
        src_ref=src,
        dst_ref=dst,
        send_sem=send_sem,
        recv_sem=recv_sem,
        device_id=device,
        device_id_type=MESH,
    )


def await_recv(ref, recv_sem, send_sem):
    remote(ref, ref, send_sem, recv_sem, {"half": 1 - lax.axis_index("half")}).wait_recv()


def await_send(ref, send_sem, recv_sem):
    remote(ref, ref, send_sem, recv_sem, {"half": 1 - lax.axis_index("half")}).wait_send()


class Group:
    def __init__(self, place, r, rows, turn=0):
        self.place = place
        self.near = {"chan": place.near_chan}
        self.peer = {"half": place.other_half}
        self.send, self.recv = r.group_send.at[turn], r.group_recv.at[turn]
        self.to_peer, self.from_peer = r.to_peer.at[turn], r.from_peer.at[turn]
        self.to_near, self.from_near = r.to_near.at[turn], r.from_near.at[turn]
        self.rows, self.size = rows, rows // CHUNKS
        self.started = []

    @staticmethod
    def scratch(rows, width, turns=1):
        return dict(
            group_send=pltpu.SemaphoreType.DMA((turns, 6, CHUNKS)),
            group_recv=pltpu.SemaphoreType.DMA((turns, 6, CHUNKS)),
            to_peer=pltpu.VMEM((turns, 2, rows, width), BF),
            from_peer=pltpu.VMEM((turns, 2, rows, width), BF),
            to_near=pltpu.VMEM((turns, rows, width), BF),
            from_near=pltpu.VMEM((turns, rows, width), BF),
        )

    def at(self, which, chunk=None):
        start = self.place.ranks[which] * self.rows
        if chunk is None:
            return pl.ds(pl.multiple_of(start, self.rows), self.rows)
        return pl.ds(pl.multiple_of(start + chunk * self.size, self.size), self.size)

    def start(self, src, dst, kind, chunk, device):
        copy = remote(src, dst, self.send.at[kind, chunk], self.recv.at[kind, chunk], device)
        copy.start()
        self.started.append(copy)

    def arrived(self, ref, kind, chunk):
        await_recv(ref, self.recv.at[kind, chunk], self.send.at[kind, chunk])

    def gather_start(self, full):
        for chunk in range(CHUNKS):
            own = full.at[self.at(0, chunk)]
            self.start(own, own, 0, chunk, self.near)
        for chunk in range(CHUNKS):
            own = full.at[self.at(0, chunk)]
            self.start(own, own, 1, chunk, self.peer)

    def gather_peer(self, full):
        for chunk in range(CHUNKS):
            self.arrived(full.at[self.at(2, chunk)], 1, chunk)

    def gather_near(self, full, chunk):
        piece = full.at[self.at(1, chunk)]
        self.arrived(piece, 0, chunk)
        self.start(piece, piece, 2, chunk, self.peer)

    def gather_diagonal(self, full, chunk):
        self.arrived(full.at[self.at(3, chunk)], 2, chunk)

    def piece(self, chunk):
        return pl.ds(chunk * self.size, self.size)

    def reduce_peer(self, slot, chunk, value):
        at = self.piece(chunk)
        self.to_peer[slot, at] = value.astype(BF)
        self.start(self.to_peer.at[slot, at], self.from_peer.at[slot, at], 3 + slot, chunk, self.peer)

    def reduce_near(self, chunk, value):
        at = self.piece(chunk)
        self.arrived(self.from_peer.at[1, at], 4, chunk)
        self.to_near[at] = (value + self.from_peer[1, at].astype(F32)).astype(BF)
        self.start(self.to_near.at[at], self.from_near.at[at], 5, chunk, self.near)

    def reduce_end(self, chunk):
        at = self.piece(chunk)
        self.arrived(self.from_peer.at[0, at], 3, chunk)
        self.arrived(self.from_near.at[at], 5, chunk)
        return self.from_peer[0, at].astype(F32) + self.from_near[at].astype(F32)

    def reduce_whole(self, kind, part):
        for chunk in range(CHUNKS):
            value = part[chunk * self.size : (chunk + 1) * self.size]
            if kind == "near":
                self.reduce_near(chunk, value)
            else:
                self.reduce_peer({"peer": 0, "diagonal": 1}[kind], chunk, value)

    def finish(self):
        for copy in self.started:
            copy.wait_send()


class Weights:
    def __init__(self, place, sems, pairs):
        self.place, self.pairs = place, pairs
        self.send, self.recv, self.local = sems

    def cut(self, ref, axis, parts, index):
        at = aligned(index, ref.shape[axis] // parts)
        return ref.at[(slice(None),) * axis + (at,)]

    def index(self, parts, col, half):
        return col * 2 + half if parts == 8 else col

    def each_sent(self, act):
        p = self.place
        owner = {"half": p.pack, "chan": p.far_chan}
        for a, (src, dst, axis, parts) in enumerate(self.pairs):

            def send(a=a, src=src, dst=dst, axis=axis, parts=parts):
                index = self.index(parts, p.col, p.half)
                act(
                    remote(
                        self.cut(src, axis, parts, index),
                        self.cut(dst, axis, parts, index),
                        self.send.at[a, 0],
                        self.recv.at[a, p.half if parts == 8 else 0],
                        owner,
                    )
                )

            if parts == 8:
                send()
            else:
                pl.when(p.half == 0)(send)

    def start(self):
        self.each_sent(lambda c: c.start())

        @pl.when(self.place.own)
        def _():
            for a, (src, dst, axis, parts) in enumerate(self.pairs):
                pltpu.make_async_copy(src, dst, self.local.at[a]).start()

    def forward(self):
        p = self.place

        @pl.when(jnp.logical_not(p.own))
        def _():
            for a, (src, dst, axis, parts) in enumerate(self.pairs):
                for s in range(parts // 4):
                    piece = self.cut(dst, axis, parts, self.index(parts, p.col, s))
                    await_recv(piece, self.recv.at[a, s], self.send.at[a, 0])
                    for j in range(1, 4):
                        remote(
                            piece,
                            piece,
                            self.send.at[a, 2 * j - 1 + s],
                            self.recv.at[a, 2 * j + s],
                            {"col": p.col_at(j)},
                        ).start()

    def ready(self, which=None):
        p = self.place
        which = range(len(self.pairs)) if which is None else which

        @pl.when(p.own)
        def _():
            for a in which:
                src, dst, axis, parts = self.pairs[a]
                pltpu.make_async_copy(src, dst, self.local.at[a]).wait()

        @pl.when(jnp.logical_not(p.own))
        def _():
            for a in which:
                src, dst, axis, parts = self.pairs[a]
                for s in range(parts // 4):
                    for j in range(1, 4):
                        piece = self.cut(dst, axis, parts, self.index(parts, p.col_at(4 - j), s))
                        await_recv(piece, self.recv.at[a, 2 * j + s], self.send.at[a, 0])

    def finish(self):
        p = self.place
        self.each_sent(lambda c: c.wait_send())

        @pl.when(jnp.logical_not(p.own))
        def _():
            for a, (src, dst, axis, parts) in enumerate(self.pairs):
                for s in range(parts // 4):
                    for j in range(1, 4):
                        piece = self.cut(dst, axis, parts, self.index(parts, p.col_at(4 - j), s))
                        await_send(piece, self.send.at[a, 2 * j - 1 + s], self.recv.at[a, 0])


class Load:
    def __init__(self, r, pairs):
        self.copies = [
            pltpu.make_async_copy(src, dst, r.load_sem.at[a]) for a, (src, dst) in enumerate(pairs)
        ]

    def start(self):
        for copy in self.copies:
            copy.start()

    def finish(self, which=None):
        for a in range(len(self.copies)) if which is None else which:
            self.copies[a].wait()


class Exchange:
    def __init__(self, place, r, src, dst, name="ex"):
        self.place, self.src, self.dst = place, src, dst
        self.send, self.recv, self.local = [
            getattr(r, f"{name}_{n}") for n in ("send", "recv", "local")
        ]
        self.size = src.shape[0] // 4

    @staticmethod
    def scratch(name="ex"):
        return {
            f"{name}_send": pltpu.SemaphoreType.DMA((4,)),
            f"{name}_recv": pltpu.SemaphoreType.DMA((4,)),
            f"{name}_local": pltpu.SemaphoreType.DMA,
        }

    def each(self, act, act_self):
        p = self.place
        for j in range(4):
            chan = 2 * p.half + j % 2
            mine = (p.half == j // 2) & (p.chan == chan)
            src, dst = self.src.at[pl.ds(j * self.size, self.size)], self.dst.at[p.chan]

            def go(j=j, chan=chan, src=src, dst=dst):
                act(
                    remote(
                        src, dst, self.send.at[j], self.recv.at[p.chan],
                        {"half": j // 2, "chan": chan},
                    )
                )

            def stay(src=src, dst=dst):
                act_self(pltpu.make_async_copy(src, dst, self.local))

            pl.when(jnp.logical_not(mine))(go)
            pl.when(mine)(stay)

    def start(self):
        self.each(lambda c: c.start(), lambda c: c.start())

    def finish(self):
        p = self.place
        self.each(lambda c: c.wait_send(), lambda c: c.wait())
        for j in range(4):

            def wait(j=j):
                await_recv(self.dst.at[j], self.recv.at[j], self.send.at[0])

            pl.when(jnp.logical_not(p.own & (p.chan == j)))(wait)


class Return:
    def __init__(self, place, r, src, dst):
        self.place, self.src, self.dst = place, src, dst
        self.send, self.recv, self.local = r.back_send, r.back_recv, r.back_local
        self.size = src.shape[1]

    @staticmethod
    def scratch():
        return dict(
            back_send=pltpu.SemaphoreType.DMA((4,)),
            back_recv=pltpu.SemaphoreType.DMA((4,)),
            back_local=pltpu.SemaphoreType.DMA,
        )

    def each(self, act, act_self):
        p = self.place
        for j in range(4):
            mine = p.own & (p.chan == j)
            src, dst = self.src.at[j], self.dst.at[aligned(p.rank, self.size)]

            def go(j=j, src=src, dst=dst):
                act(
                    remote(
                        src, dst, self.send.at[j], self.recv.at[p.rank],
                        {"half": p.pack, "chan": j},
                    )
                )

            def stay(src=src, dst=dst):
                act_self(pltpu.make_async_copy(src, dst, self.local))

            pl.when(jnp.logical_not(mine))(go)
            pl.when(mine)(stay)

    def start(self):
        self.each(lambda c: c.start(), lambda c: c.start())

    def finish(self):
        p = self.place
        self.each(lambda c: c.wait_send(), lambda c: c.wait())
        for j in range(4):
            mine = (p.half == j // 2) & (p.chan == 2 * p.half + j % 2)

            def wait(j=j):
                await_recv(
                    self.dst.at[pl.ds(j * self.size, self.size)], self.recv.at[j], self.send.at[0]
                )

            pl.when(jnp.logical_not(mine))(wait)


class Scatter:
    def __init__(self, place, r, sources, totals, name="sc"):
        self.place, self.sources, self.totals = place, sources, totals
        self.send, self.recv = getattr(r, name + "_send"), getattr(r, name + "_recv")
        self.local = getattr(r, name + "_local")
        self.kept, self.got, self.late, self.cross = [
            [getattr(r, f"{name}_{part}{a}") for a in range(len(sources))]
            for part in ("kept", "got", "late", "cross")
        ]
        self.x = lax.rem(place.col, 2)
        self.y = place.col // 2
        self.to_x = {"col": place.col + 1 - 2 * self.x}
        self.to_y = {"col": lax.rem(place.col + 2, 4)}

    @staticmethod
    def scratch(shapes, name="sc"):
        n = len(shapes)
        out = {
            f"{name}_send": pltpu.SemaphoreType.DMA((n, 8)),
            f"{name}_recv": pltpu.SemaphoreType.DMA((n, 8)),
            f"{name}_local": pltpu.SemaphoreType.DMA((n, 4)),
        }
        for a, (rows, width) in enumerate(shapes):
            for part, count in (("kept", 4), ("got", 4), ("late", 2), ("cross", 2)):
                out[f"{name}_{part}{a}"] = pltpu.VMEM((count, rows // 8, width), BF)
        return out

    def each(self, which):
        return range(len(self.sources)) if which is None else which

    def piece(self, a, y, x, half):
        src = self.sources[a]
        return src.at[aligned((2 * y + x) * 2 + half, src.shape[0] // 8)]

    def firsts(self, a):
        out = []
        for i in range(2):
            out.append((self.piece(a, i, 1 - self.x, 0), i, self.to_x))
            out.append((self.piece(a, 1 - self.y, i, 1), 2 + i, self.to_y))
        return [
            remote(src, self.got[a].at[k], self.send.at[a, k], self.recv.at[a, k], device)
            for src, k, device in out
        ]

    def keeps(self, a):
        out = []
        for i in range(2):
            out.append((self.piece(a, i, self.x, 0), i))
            out.append((self.piece(a, self.y, i, 1), 2 + i))
        return [
            pltpu.make_async_copy(src, self.kept[a].at[k], self.local.at[a, k]) for src, k in out
        ]

    def seconds(self, a):
        kept, late = self.kept[a], self.late[a]
        return [
            remote(kept.at[1 - self.y], late.at[0], self.send.at[a, 4], self.recv.at[a, 4], self.to_y),
            remote(kept.at[3 - self.x], late.at[1], self.send.at[a, 5], self.recv.at[a, 5], self.to_x),
        ]

    def third(self, a, slot, part, half, chan):
        return remote(
            self.got[a].at[part],
            self.cross[a].at[slot],
            self.send.at[a, 6 + slot],
            self.recv.at[a, 6 + slot],
            {"half": half, "chan": chan},
        )

    def start(self, which=None):
        for a in self.each(which):
            for copy in self.firsts(a) + self.keeps(a):
                copy.start()

    def second(self, which=None):
        for a in self.each(which):
            for copy in self.firsts(a) + self.keeps(a):
                copy.wait()
            for k in range(4):
                total = self.kept[a][k].astype(F32) + self.got[a][k].astype(F32)
                self.kept[a][k] = total.astype(BF)
            for copy in self.seconds(a):
                copy.start()

    def middle(self, which=None):
        p = self.place
        for a in self.each(which):
            for copy in self.seconds(a):
                copy.wait()
            kept, late, got = self.kept[a], self.late[a], self.got[a]
            got[0] = (kept[self.y].astype(F32) + late[0].astype(F32)).astype(BF)
            got[1] = (kept[2 + self.x].astype(F32) + late[1].astype(F32)).astype(BF)

            @pl.when(p.own)
            def _():
                self.third(a, 0, p.other_half, p.other_half, p.chan).start()

            @pl.when(jnp.logical_not(p.own))
            def _():
                self.third(a, 0, p.half, p.half, p.far_chan).start()
                self.third(a, 1, p.other_half, p.other_half, p.far_chan).start()

    def finish(self, which=None):
        p = self.place
        for a in self.each(which):
            cross = self.cross[a]
            await_recv(cross.at[0], self.recv.at[a, 6], self.send.at[a, 6])
            await_send(cross.at[0], self.send.at[a, 6], self.recv.at[a, 6])

            @pl.when(p.own)
            def _():
                self.totals[a][...] = (
                    cross[0].astype(F32) + self.got[a][p.half].astype(F32)
                ).astype(BF)

            @pl.when(jnp.logical_not(p.own))
            def _():
                await_recv(cross.at[1], self.recv.at[a, 7], self.send.at[a, 7])
                await_send(cross.at[1], self.send.at[a, 7], self.recv.at[a, 7])
                self.totals[a][...] = (cross[0].astype(F32) + cross[1].astype(F32)).astype(BF)


class Spread:
    def __init__(self, place, r, totals, results, name="sp"):
        self.place, self.totals, self.results = place, totals, results
        self.send, self.recv, self.kept = [
            getattr(r, f"{name}_{n}") for n in ("send", "recv", "local")
        ]

    @staticmethod
    def scratch(count, name="sp"):
        return {
            f"{name}_send": pltpu.SemaphoreType.DMA((count, 7)),
            f"{name}_recv": pltpu.SemaphoreType.DMA((count, 7)),
            f"{name}_local": pltpu.SemaphoreType.DMA((count,)),
        }

    def each(self, which):
        return range(len(self.totals)) if which is None else which

    def slot(self, a, col, half):
        result = self.results[a]
        return result.at[aligned(col * 2 + half, result.shape[0] // 8)]

    def local(self, a):
        p = self.place
        return pltpu.make_async_copy(
            self.totals[a], self.slot(a, p.col, p.half), self.kept.at[a]
        )

    def out(self, a, j):
        p = self.place
        device = {"col": p.col_at(j)} if j else {"half": p.other_half}
        return remote(
            self.totals[a],
            self.slot(a, p.col, p.half),
            self.send.at[a, j],
            self.recv.at[a, j],
            device,
        )

    def pass_on(self, a, j):
        p = self.place
        piece = self.slot(a, p.col_at(4 - j), p.half)
        return remote(
            piece, piece, self.send.at[a, 3 + j], self.recv.at[a, 3 + j],
            {"half": p.other_half},
        )

    def start(self, which=None):
        for a in self.each(which):
            for j in (1, 2, 3, 0):
                self.out(a, j).start()
            self.local(a).start()

    def forward(self, which=None):
        p = self.place
        for a in self.each(which):
            for j in range(1, 4):
                piece = self.slot(a, p.col_at(4 - j), p.half)
                await_recv(piece, self.recv.at[a, j], self.send.at[a, j])
                self.pass_on(a, j).start()

    def finish(self, which=None):
        p = self.place
        for a in self.each(which):
            for j in range(4):
                self.out(a, j).wait_send()
            self.local(a).wait()
            await_recv(
                self.slot(a, p.col, p.other_half), self.recv.at[a, 0], self.send.at[a, 0]
            )
            for j in range(1, 4):
                self.pass_on(a, j).wait_send()
                piece = self.slot(a, p.col_at(4 - j), p.other_half)
                await_recv(piece, self.recv.at[a, 3 + j], self.send.at[a, 3 + j])


def call_kernel(body, ins, outs, scratch, collective_id, flops, hbm=()):
    names = list(ins) + list(outs) + list(scratch)

    def run(*refs):
        body(SimpleNamespace(**dict(zip(names, refs))))

    def spec(name):
        return pl.BlockSpec(memory_space=pl.ANY if name in hbm else pltpu.VMEM)

    results = pl.pallas_call(
        run,
        out_shape=[jax.ShapeDtypeStruct(*o) for o in outs.values()],
        in_specs=[spec(n) for n in ins],
        out_specs=[spec(n) for n in outs],
        scratch_shapes=list(scratch.values()),
        compiler_params=pltpu.CompilerParams(
            collective_id=collective_id, has_side_effects=True, vmem_limit_bytes=VMEM_LIMIT
        ),
        cost_estimate=pl.CostEstimate(flops=flops, bytes_accessed=20 << 20, transcendentals=0),
    )(*ins.values())
    return SimpleNamespace(**dict(zip(outs, results)))


def normalized(x):
    average = jnp.mean(x, 1, keepdims=True)
    centered = x - average
    variance = jnp.mean(centered * centered, 1, keepdims=True)
    inv = lax.rsqrt(variance + EPSILON)
    return centered * inv, inv


def norm_grad_rows(grad, x, gain):
    xhat, inv = normalized(x)
    gain_part = jnp.sum(grad * xhat, 0, keepdims=True)
    scaled = grad * gain
    mean_plain = jnp.mean(scaled, 1, keepdims=True)
    mean_cross = jnp.mean(scaled * xhat, 1, keepdims=True)
    return inv * (scaled - mean_plain - xhat * mean_cross), gain_part


PAD = 8


def shifted(ref, s, tile, size, offset):
    return ref[s, pl.ds(PAD + tile * size + offset, size)]


def mlp_tables(r, l):
    groups, feats, inner = r.w_ci.shape[1:]
    half = feats // 2
    for table in (r.in_re, r.in_im, r.out_re, r.out_im):
        table[...] = jnp.zeros_like(table)
    for g in range(groups):
        rows, cols = pl.ds(g * half, half), pl.ds(g * inner, inner)
        r.in_re[rows, cols] = r.w_ci[l, g, 0:half].astype(BF)
        r.in_im[rows, cols] = r.w_ci[l, g, half:feats].astype(BF)
        turned = r.w_co[l, g].T
        r.out_re[rows, cols] = turned[0:half].astype(BF)
        r.out_im[rows, cols] = turned[half:feats].astype(BF)


def mlp_scratch(shard, inner):
    table = pltpu.VMEM((shard, inner), BF)
    return dict(in_re=table, in_im=table, out_re=table, out_im=table)


MIXER = dict(in_proj="w_in", cond_in="w_ci", cond_out="w_co", out_proj="w_out", filter_spec="w_spec")
FFN = dict(gate_proj="w_gate", up_proj="w_up", down_proj="w_down")
CUTS = dict(in_proj=1, cond_in=1, cond_out=1, filter_spec=1, out_proj=0, gate_proj=0, up_proj=0, down_proj=0)
PROJ, QUERY, MIXED, GATED, SPECTRA, MIX_ROWS = 0, 3, 4, 5, 6, 12


def forward_body(r):
    place = Place()
    layers, rows, width = r.mids.shape
    length = r.seg.shape[0]
    lanes = r.w_in.shape[3]
    wide = r.both.shape[1] // 2
    tiles = 4
    size = length // tiles
    exchange = Exchange(place, r, r.stream, r.pieces)
    tables = [
        pltpu.make_async_copy(r.cosine, r.cos, r.table_sem.at[0]),
        pltpu.make_async_copy(r.sine, r.sin, r.table_sem.at[1]),
    ]

    def weights(kind, names, l):
        sems = [getattr(r, f"{kind}_{n}").at[l] for n in ("send", "recv", "local")]
        pairs = [
            (getattr(r, n).at[l], getattr(r, to).at[l], CUTS[n], 4 if n == "out_proj" else 8)
            for n, to in names.items()
        ]
        return Weights(place, sems, pairs)

    mixer_weights = [weights("mw", MIXER, l) for l in range(layers)]
    ffn_weights = [weights("fw", FFN, l) for l in range(layers)]
    place.barrier()
    exchange.start()
    own, other = place.own, jnp.logical_not(place.own)

    def gain_copy(j):
        chan = lax.rem(place.chan + j, 4)
        return remote(r.small, r.gain_parts.at[j], r.gain_send.at[j], r.gain_recv.at[j], {"chan": chan})

    for j in range(1, 4):
        gain_copy(j).start()
    seg_copy = remote(r.seg, r.seg_got, r.gain_send.at[4], r.gain_recv.at[4], {"half": place.other_half})
    taps_copy = remote(r.taps, r.taps_got, r.gain_send.at[5], r.gain_recv.at[5], {"chan": place.far_chan})

    @pl.when(own)
    def _():
        seg_copy.start()
        taps_copy.start()

    mixer_weights[0].start()
    for copy in tables:
        copy.start()
    r.edges[0:PAD] = jnp.full((PAD, 1), -1, jnp.int32)
    r.edges[PAD + length : 2 * PAD + length] = jnp.full((PAD, 1), -1, jnp.int32)
    for s in range(3):
        r.padded[s, 0:PAD] = jnp.zeros((PAD, lanes), F32)
        r.padded[s, PAD + length : 2 * PAD + length] = jnp.zeros((PAD, lanes), F32)
    r.both[...] = jnp.zeros_like(r.both)

    @pl.when(own)
    def _():
        r.edges[PAD : PAD + length] = r.seg[...]
        r.taps_out[...] = r.taps[...]
        seg_copy.wait_send()
        taps_copy.wait_send()

    @pl.when(other)
    def _():
        seg_copy.wait_recv()
        taps_copy.wait_recv()
        r.edges[PAD : PAD + length] = r.seg_got[...]
        r.taps_out[...] = r.taps_got[...]

    here = r.edges[PAD : PAD + length]
    r.mask_prev[...] = jnp.where(r.edges[PAD - 1 : PAD - 1 + length] == here, 1.0, 0.0)
    r.mask_next[...] = jnp.where(r.edges[PAD + 1 : PAD + 1 + length] == here, 1.0, 0.0)
    for j in range(1, 4):
        gain_copy(j).wait()
    r.gain_parts[0] = r.small[...]
    parts = []
    for c in range(4):
        parts.append(r.gain_parts[lax.rem(place.chan - c + 4, 4)])
    r.gains[...] = jnp.concatenate(parts, 1)
    exchange.finish()
    r.values[0] = jnp.concatenate([r.pieces[j] for j in range(4)], 1).astype(F32)

    def tap(l, o, s):
        at = 9 * l + 3 * o + s
        return r.taps_out[at : at + 1]

    saves = {}

    def save(name, *copies):
        saves[name] = [pltpu.make_async_copy(src, dst, r.save_sem.at[i]) for i, src, dst in copies]
        for copy in saves[name]:
            copy.start()

    def saved(name):
        for copy in saves.pop(name, ()):
            copy.wait()

    def mixer(l):
        group = Group(place, r, rows, 0)
        h_all = r.h_mixer.at[l]
        xhat, _ = normalized(r.values[l])
        h_all[group.at(0)] = (xhat * r.gains[l : l + 1]).astype(BF)
        group.gather_start(h_all)
        if l == 0:
            mixer_weights[0].forward()
            ffn_weights[0].start()
        mixer_weights[l].ready()
        mlp_tables(r, l)
        saved("mixer")

        def project(which, chunk=None):
            at = group.at(which, chunk)
            h = h_all[at]
            for s in range(3):
                proj = nn_dot(h, r.w_in[l, s])
                r.padded[s, pl.ds(pl.multiple_of(at.start + PAD, 8), at.size)] = proj
                r.mix[PROJ + s, at] = proj.astype(BF)

        project(0)
        group.gather_peer(h_all)
        project(2)
        for chunk in range(CHUNKS):
            group.gather_near(h_all, chunk)
            project(1, chunk)
            group.gather_diagonal(h_all, chunk)
            project(3, chunk)

        for t in range(tiles):
            at = pl.ds(t * size, size)
            prev = r.mask_prev[at]
            following = r.mask_next[at]
            shorts = []
            for s in range(3):
                shorts.append(
                    tap(l, 0, s) * shifted(r.padded, s, t, size, -1) * prev
                    + tap(l, 1, s) * shifted(r.padded, s, t, size, 0)
                    + tap(l, 2, s) * shifted(r.padded, s, t, size, 1) * following
                )
            r.mix[QUERY, at] = shorts[0].astype(BF)
            r.both[at, 0:lanes] = shorts[1].astype(BF)
            r.both[at, wide : wide + lanes] = shorts[2].astype(BF)
        if l == 0:
            for copy in tables:
                copy.wait()

        @pl.loop(0, tiles)
        def _(t):
            at = aligned(t, size)
            real = nn_dot(r.cos[at], r.both[...])
            imag = nn_dot(r.sin[at], r.both[...])
            value_re, cond_re = real[:, :lanes], real[:, wide : wide + lanes].astype(BF)
            value_im, cond_im = imag[:, :lanes], imag[:, wide : wide + lanes].astype(BF)
            pre = nn_dot(cond_re, r.in_re[...]) + nn_dot(cond_im, r.in_im[...])
            inner = (pre * normal_cdf(pre)).astype(BF)
            kernel_re = r.w_spec[l, 0, at] + nt_dot(inner, r.out_re[...])
            kernel_im = r.w_spec[l, 1, at] + nt_dot(inner, r.out_im[...])
            r.prod_re[at] = (value_re * kernel_re - value_im * kernel_im).astype(BF)
            r.prod_im[at] = (value_re * kernel_im + value_im * kernel_re).astype(BF)
            r.pre[at] = pre.astype(BF)
            for i, x in enumerate((value_re, value_im, kernel_re, kernel_im, cond_re, cond_im)):
                r.mix[SPECTRA + i, at] = x.astype(BF)

        ffn_weights[l].forward()
        if l + 1 < layers:
            mixer_weights[l + 1].start()

        def project_out(which):
            at = group.at(which)
            mixed = nn_dot(r.cos[at], r.prod_re[...]) + nn_dot(r.sin[at], r.prod_im[...])
            r.mix[MIXED, at] = mixed.astype(BF)
            gated = (r.mix[QUERY, at].astype(F32) * mixed).astype(BF)
            r.mix[GATED, at] = gated
            return nn_dot(gated, r.w_out[l])

        group.reduce_whole("diagonal", project_out(3))
        group.reduce_whole("near", project_out(1))
        group.reduce_whole("peer", project_out(2))
        r.mids[l] = r.values[l] + project_out(0)
        save("mixer", (0, r.mix, r.s_mix.at[l]), (1, r.pre, r.s_pre.at[l]), (2, h_all, r.s_h_mixer.at[l]))
        for chunk in range(CHUNKS):
            r.mids[l, group.piece(chunk)] += group.reduce_end(chunk)
        group.finish()

    def ffn(l):
        group = Group(place, r, rows, 1)
        h_all = r.h_ffn.at[l]
        xhat, _ = normalized(r.mids[l])
        h_all[group.at(0)] = (xhat * r.gains[layers + l : layers + l + 1]).astype(BF)
        group.gather_start(h_all)
        ffn_weights[l].ready()
        saved("ffn")

        def block(at):
            h = h_all[at]
            gate = nn_dot(h, r.w_gate[l])
            up = nn_dot(h, r.w_up[l])
            r.units[0, at] = gate.astype(BF)
            r.units[1, at] = up.astype(BF)
            hidden = (gate * normal_cdf(gate) * up).astype(BF)
            return nn_dot(hidden, r.w_down[l])

        r.values[l + 1] = r.mids[l] + block(group.at(0))
        group.gather_peer(h_all)
        group.reduce_whole("peer", block(group.at(2)))
        if l + 1 < layers:
            mixer_weights[l + 1].forward()
            ffn_weights[l + 1].start()
        else:
            cotangent.start()
        for chunk in range(CHUNKS):
            group.gather_near(h_all, chunk)
            r.near_part[group.piece(chunk)] = block(group.at(1, chunk))
            group.gather_diagonal(h_all, chunk)
            group.reduce_peer(1, chunk, block(group.at(3, chunk)))
            group.reduce_near(chunk, r.near_part[group.piece(chunk)])
        save("ffn", (3, r.units, r.s_units.at[l]), (4, h_all, r.s_h_ffn.at[l]))
        for chunk in range(CHUNKS):
            r.values[l + 1, group.piece(chunk)] += group.reduce_end(chunk)
        group.finish()

    cotangent = Exchange(place, r, r.cotangent, r.cot_pieces, "cot")
    for l in range(layers):
        mixer(l)
        ffn(l)
    kept = []
    for i, name in enumerate(list(MIXER.values()) + list(FFN.values())):
        if name != "w_spec":
            kept.append(
                pltpu.make_async_copy(getattr(r, name), getattr(r, name + "_out"), r.keep_sem.at[i])
            )
    for copy in kept:
        copy.start()
    cotangent.finish()
    r.carried[...] = jnp.concatenate([r.cot_pieces[j] for j in range(4)], 1).astype(F32)
    for l in range(layers):
        mixer_weights[l].finish()
        ffn_weights[l].finish()
    saved("mixer")
    saved("ffn")
    for copy in kept:
        copy.wait()


def forward(arrays, stream, cotangent, seg, small, taps, tables):
    length, shard = stream.shape
    layers, _, width, lanes = arrays["in_proj"].shape
    rows = length // 4
    units = arrays["gate_proj"].shape[2]
    groups, _, inner = arrays["cond_in"].shape[1:]
    inner *= groups
    wide = -(-lanes // 128) * 128
    gains = small.shape[0]
    held = {to: pltpu.VMEM(arrays[n].shape, arrays[n].dtype) for n, to in {**MIXER, **FFN}.items()}
    kept = {
        to + "_out": (arrays[n].shape, arrays[n].dtype)
        for n, to in {**MIXER, **FFN}.items()
        if to != "w_spec"
    }
    saves = dict(
        s_mix=((layers, MIX_ROWS, length, lanes), BF),
        s_pre=((layers, length, inner), BF),
        s_h_mixer=((layers, length, width), BF),
        s_units=((layers, 2, length, units), BF),
        s_h_ffn=((layers, length, width), BF),
    )

    def semaphores(kind, count):
        return {
            f"{kind}_send": pltpu.SemaphoreType.DMA((layers, count, 7)),
            f"{kind}_recv": pltpu.SemaphoreType.DMA((layers, count, 8)),
            f"{kind}_local": pltpu.SemaphoreType.DMA((layers, count)),
        }

    return call_kernel(
        forward_body,
        dict(
            stream=stream, cotangent=cotangent, seg=seg, small=small, taps=taps,
            cosine=tables[0], sine=tables[1], **arrays,
        ),
        dict(
            values=((layers + 1, rows, width), F32),
            mids=((layers, rows, width), F32),
            carried=((rows, width), F32),
            gains=((gains, width), F32),
            taps_out=(taps.shape, F32),
            mask_prev=((length, 1), F32),
            mask_next=((length, 1), F32),
            **saves,
            **kept,
        ),
        dict(
            pieces=pltpu.VMEM((4, rows, shard), BF),
            cot_pieces=pltpu.VMEM((4, rows, shard), BF),
            gain_parts=pltpu.VMEM((4, gains, shard), F32),
            gain_send=pltpu.SemaphoreType.DMA((6,)),
            gain_recv=pltpu.SemaphoreType.DMA((6,)),
            table_sem=pltpu.SemaphoreType.DMA((2,)),
            save_sem=pltpu.SemaphoreType.DMA((5,)),
            keep_sem=pltpu.SemaphoreType.DMA((8,)),
            seg_got=pltpu.VMEM((length, 1), jnp.int32),
            taps_got=pltpu.VMEM(taps.shape, F32),
            edges=pltpu.VMEM((length + 2 * PAD, 1), jnp.int32),
            cos=pltpu.VMEM((length, length), BF),
            sin=pltpu.VMEM((length, length), BF),
            h_mixer=pltpu.VMEM((layers, length, width), BF),
            h_ffn=pltpu.VMEM((layers, length, width), BF),
            mix=pltpu.VMEM((MIX_ROWS, length, lanes), BF),
            pre=pltpu.VMEM((length, inner), BF),
            units=pltpu.VMEM((2, length, units), BF),
            near_part=pltpu.VMEM((rows, width), F32),
            padded=pltpu.VMEM((3, length + 2 * PAD, lanes), F32),
            both=pltpu.VMEM((length, 2 * wide), BF),
            prod_re=pltpu.VMEM((length, lanes), BF),
            prod_im=pltpu.VMEM((length, lanes), BF),
            **held,
            **semaphores("mw", 5),
            **semaphores("fw", 3),
            **mlp_scratch(lanes, inner),
            **Group.scratch(rows, width, 2),
            **Exchange.scratch(),
            **Exchange.scratch("cot"),
        ),
        1,
        30 * 10**9,
        ("stream", "cotangent", "cosine", "sine") + tuple(arrays) + tuple(saves) + tuple(kept),
    )


def ffn_backward_body(l, last, r):
    place = Place()
    rows, width = r.mids.shape[1:]
    units = r.units.shape[2]
    group = Group(place, r, rows)
    load = Load(
        r,
        [
            (r.w_gate_out.at[l], r.w_gate),
            (r.w_up_out.at[l], r.w_up),
            (r.w_down_out.at[l], r.w_down),
            (r.s_units.at[l], r.units),
            (r.s_h_ffn.at[l], r.h_all),
        ],
    )
    load.start()
    layers = r.gains.shape[0] // 2
    gain = r.gains[layers + l : layers + l + 1]
    r.g_all[group.at(0)] = r.carried[...].astype(BF)
    if last:
        shard = r.returned.shape[1]
        for j in range(4):
            r.leaving[j] = r.values[l + 1, :, j * shard : (j + 1) * shard].astype(BF)
        back = Return(place, r, r.leaving, r.returned)
    place.barrier()
    group.gather_start(r.g_all)
    if last:
        back.start()
    else:
        spread = Spread(place, r, [r.ffn_total], [r.ffn_result])
        scatter = Scatter(place, r, of(r, "g_"), of(r, "t_"))
        scatter.start()
        spread.start()

    load.finish()

    def block(at):
        hidden_grad = nt_dot(r.g_all[at], r.w_down[...])
        gate = r.units[0, at].astype(F32)
        up = r.units[1, at].astype(F32)
        cdf = normal_cdf(gate)
        act = gate * cdf
        r.hidden_all[at] = (act * up).astype(BF)
        gate_grad = (hidden_grad * up * (cdf + gate * normal_pdf(gate))).astype(BF)
        up_grad = (hidden_grad * act).astype(BF)
        r.gate_grads[at] = gate_grad
        r.up_grads[at] = up_grad
        return nt_dot(gate_grad, r.w_gate[...]) + nt_dot(up_grad, r.w_up[...])

    r.own_part[...] = block(group.at(0))
    group.gather_peer(r.g_all)
    group.reduce_whole("peer", block(group.at(2)))
    if not last:
        scatter.second()
    for chunk in range(CHUNKS):
        group.gather_near(r.g_all, chunk)
        r.near_part[group.piece(chunk)] = block(group.at(1, chunk))
        group.gather_diagonal(r.g_all, chunk)
        group.reduce_peer(1, chunk, block(group.at(3, chunk)))
        group.reduce_near(chunk, r.near_part[group.piece(chunk)])
    if not last:
        scatter.middle()
        spread.forward()
    step = 256
    for u in range(units // step):
        cols = pl.ds(u * step, step)
        r.weight_grads[0 * width : 1 * width, cols] = tn_dot(r.h_all[...], r.gate_grads[:, cols]).astype(BF)
        r.weight_grads[1 * width : 2 * width, cols] = tn_dot(r.h_all[...], r.up_grads[:, cols]).astype(BF)
        r.weight_grads[pl.ds(2 * width + u * step, step)] = tn_dot(r.hidden_all[:, cols], r.g_all[...]).astype(BF)
    for chunk in range(CHUNKS):
        r.own_part[group.piece(chunk)] += group.reduce_end(chunk)
    grad, gain_part = norm_grad_rows(r.own_part[...], r.mids[l], gain)
    r.mid_grad[...] = r.carried[...] + grad
    r.gain_grad[...] = gain_part
    group.finish()
    if last:
        back.finish()
        r.output[...] = r.returned[...].astype(F32)
    else:
        spread.finish()
        scatter.finish()


GRADS = ("proj", "spec", "mlp", "small")


def of(r, prefix):
    return [getattr(r, prefix + n) for n in GRADS]


def totals_of(grads):
    return {"t_" + n: ((grads[n].shape[0] // 8, grads[n].shape[1]), BF) for n in GRADS}


def ffn_backward(l, fwd, carried, last, shard, pending):
    layers, rows, width = fwd.mids.shape
    units = fwd.w_gate_out.shape[2]
    full = rows * 4
    big = pltpu.VMEM((full, units), BF)
    held = ("w_gate_out", "w_up_out", "w_down_out", "s_units", "s_h_ffn")
    ins = dict(carried=carried, mids=fwd.mids, gains=fwd.gains)
    ins.update({n: getattr(fwd, n) for n in held})
    outs = dict(
        mid_grad=((rows, width), F32),
        weight_grads=((3 * width, units), BF),
        gain_grad=((1, width), F32),
    )
    hbm = held
    if last:
        ins.update(values=fwd.values)
        outs.update(output=((full, shard), F32))
        scratch = dict(
            leaving=pltpu.VMEM((4, rows, shard), BF),
            returned=pltpu.VMEM((full, shard), BF),
            **Return.scratch(),
        )
    else:
        grads, ffn_total = pending
        ins.update(ffn_total=ffn_total, **{"g_" + n: grads[n] for n in GRADS})
        outs.update(
            ffn_result=((8 * ffn_total.shape[0], ffn_total.shape[1]), BF),
            **totals_of(grads),
        )
        scratch = dict(**Spread.scratch(1), **Scatter.scratch([grads[n].shape for n in GRADS]))
        hbm += tuple("g_" + n for n in GRADS)
    return call_kernel(
        functools.partial(ffn_backward_body, l, last),
        ins,
        outs,
        dict(
            near_part=pltpu.VMEM((rows, width), F32),
            own_part=pltpu.VMEM((rows, width), F32),
            g_all=pltpu.VMEM((full, width), BF),
            h_all=pltpu.VMEM((full, width), BF),
            units=pltpu.VMEM((2, full, units), BF),
            w_gate=pltpu.VMEM((width, units), BF),
            w_up=pltpu.VMEM((width, units), BF),
            w_down=pltpu.VMEM((units, width), BF),
            load_sem=pltpu.SemaphoreType.DMA((5,)),
            hidden_all=big,
            gate_grads=big,
            up_grads=big,
            **Group.scratch(rows, width),
            **scratch,
        ),
        20 + l,
        12 * full * width * units,
        hbm,
    )


def mixer_backward_body(l, above, r):
    bottom = l == 0
    place = Place()
    rows = r.mid_grad.shape[0]
    length, width = r.h_all.shape
    lanes = r.w_in.shape[3]
    groups, feats, units = r.w_ci.shape[1:]
    half = feats // 2
    wide = r.both_re.shape[1] // 2
    tiles = 4
    size = length // tiles
    group = Group(place, r, rows)
    load = Load(
        r,
        [
            (r.w_out_out.at[l], r.w_out.at[0]),
            (r.w_ci_out.at[l], r.w_ci.at[0]),
            (r.w_co_out.at[l], r.w_co.at[0]),
            (r.s_mix.at[l], r.mix),
            (r.s_pre.at[l], r.pre_all),
            (r.w_in_out.at[l], r.w_in.at[0]),
            (r.s_h_mixer.at[l], r.h_all),
            (r.cosine, r.cos),
            (r.sine, r.sin),
            (r.values.at[l], r.layer_in),
        ],
    )
    load.start()
    r.m_all[group.at(0)] = r.mid_grad[...].astype(BF)
    place.barrier()
    group.gather_start(r.m_all)
    ffn_scatter = Scatter(place, r, [r.ffn_grads], [r.ffn_total], "fs")
    ffn_scatter.start()
    if above:
        spread = Spread(place, r, of(r, "t_"), of(r, "r_"))
        spread.start()
    if bottom:
        scatter = Scatter(place, r, of(r, "g_"), of(r, "u_"))
        ffn_spread = Spread(place, r, [r.ffn_total], [r.ffn_result], "fp")
        mix_spread = Spread(place, r, of(r, "u_"), of(r, "q_"), "mp")
    for s in range(3):
        r.padded[s, 0:PAD] = jnp.zeros((PAD, lanes), F32)
        r.padded[s, PAD + length : 2 * PAD + length] = jnp.zeros((PAD, lanes), F32)
    r.both_re[...] = jnp.zeros_like(r.both_re)
    r.both_im[...] = jnp.zeros_like(r.both_im)
    r.sum_in[...] = jnp.zeros_like(r.sum_in)
    r.sum_out[...] = jnp.zeros_like(r.sum_out)
    load.finish()
    mlp_tables(r, 0)

    def gated_back(which, chunk=None):
        at = group.at(which, chunk)
        gated_grad = nt_dot(r.m_all[at], r.w_out[0])
        to = pl.ds(pl.multiple_of(at.start + PAD, 8), at.size)
        r.padded[0, to] = gated_grad * r.mix[MIXED, at].astype(F32)
        r.q_g[at] = (gated_grad * r.mix[QUERY, at].astype(F32)).astype(BF)

    gated_back(0)
    group.gather_peer(r.m_all)
    gated_back(2)
    for chunk in range(CHUNKS):
        group.gather_near(r.m_all, chunk)
        gated_back(1, chunk)
        group.gather_diagonal(r.m_all, chunk)
        gated_back(3, chunk)

    @pl.loop(0, tiles)
    def _(t):
        at = aligned(t, size)
        real = nn_dot(r.cos[at], r.q_g[...])
        imag = nn_dot(r.sin[at], r.q_g[...])
        value_re, value_im, kernel_re, kernel_im = [
            r.mix[SPECTRA + i, at].astype(F32) for i in range(4)
        ]
        kernel_re_grad = real * value_re + imag * value_im
        kernel_im_grad = imag * value_re - real * value_im
        r.both_re[at, 0:lanes] = (real * kernel_re + imag * kernel_im).astype(BF)
        r.both_im[at, 0:lanes] = (imag * kernel_re - real * kernel_im).astype(BF)
        r.g_spec[at] = jnp.concatenate([kernel_re_grad, kernel_im_grad], 1).astype(BF)
        kernel_re_grad = kernel_re_grad.astype(BF)
        kernel_im_grad = kernel_im_grad.astype(BF)
        pre = r.pre_all[at].astype(F32)
        cdf = normal_cdf(pre)
        inner = (pre * cdf).astype(BF)
        inner_grad = nn_dot(kernel_re_grad, r.out_re[...]) + nn_dot(kernel_im_grad, r.out_im[...])
        pre_grad = (inner_grad * (cdf + pre * normal_pdf(pre))).astype(BF)
        r.both_re[at, wide : wide + lanes] = nt_dot(pre_grad, r.in_re[...]).astype(BF)
        r.both_im[at, wide : wide + lanes] = nt_dot(pre_grad, r.in_im[...]).astype(BF)
        r.sum_out[0] += tn_dot(kernel_re_grad, inner)
        r.sum_out[1] += tn_dot(kernel_im_grad, inner)
        r.sum_in[0] += tn_dot(r.mix[SPECTRA + 4, at], pre_grad)
        r.sum_in[1] += tn_dot(r.mix[SPECTRA + 5, at], pre_grad)

    ffn_scatter.second()
    if above:
        spread.forward()
    for g in range(groups):
        rows_at, cols = slice(g * half, (g + 1) * half), slice(g * units, (g + 1) * units)
        at = g * feats
        r.g_mlp[at : at + half] = r.sum_in[0, rows_at, cols].astype(BF)
        r.g_mlp[at + half : at + feats] = r.sum_in[1, rows_at, cols].astype(BF)
        turned = jnp.concatenate([r.sum_out[0, rows_at, cols], r.sum_out[1, rows_at, cols]], 0)
        at += groups * feats
        r.g_mlp[at : at + units] = turned.T.astype(BF)
    if bottom:
        scatter.start((1, 2))

    @pl.loop(0, tiles)
    def _(t):
        at = aligned(t, size)
        both = nn_dot(r.cos[at], r.both_re[...]) + nn_dot(r.sin[at], r.both_im[...])
        to = pl.ds(pl.multiple_of(t * size + PAD, 8), size)
        r.padded[1, to] = both[:, :lanes]
        r.padded[2, to] = both[:, wide : wide + lanes]

    def tap(o, s):
        at = 9 * l + 3 * o + s
        return r.taps[at : at + 1]

    totals = [[None] * 3 for _ in range(3)]
    for t in range(tiles):
        at = pl.ds(t * size, size)
        prev = r.mask_prev[at]
        following = r.mask_next[at]
        for s in range(3):
            here = shifted(r.padded, s, t, size, 0)
            after = shifted(r.padded, s, t, size, 1) * following
            before = shifted(r.padded, s, t, size, -1) * prev
            r.proj_grads[s, at] = (
                tap(0, s) * after + tap(1, s) * here + tap(2, s) * before
            ).astype(BF)
            proj = r.mix[PROJ + s, at].astype(F32)
            for o, g in enumerate((after, here, before)):
                part = jnp.sum(g * proj, 0, keepdims=True)
                totals[o][s] = part if t == 0 else totals[o][s] + part
    ffn_scatter.middle()

    def feats_grad(which):
        at = group.at(which)
        return sum(nt_dot(r.proj_grads[s, at], r.w_in[0, s]) for s in range(3))

    group.reduce_whole("diagonal", feats_grad(3))
    group.reduce_whole("near", feats_grad(1))
    group.reduce_whole("peer", feats_grad(2))
    for s in range(3):
        r.g_proj[s * lanes : (s + 1) * lanes] = tn_dot(r.proj_grads[s], r.h_all[...]).astype(BF)
    r.g_proj[3 * lanes :] = tn_dot(r.mix[GATED], r.m_all[...]).astype(BF)
    if bottom:
        scatter.start((0,))
        scatter.second((1, 2))
    r.own_part[...] = feats_grad(0)
    for chunk in range(CHUNKS):
        r.own_part[group.piece(chunk)] += group.reduce_end(chunk)
    grad, gain_part = norm_grad_rows(r.own_part[...], r.layer_in[...], r.gains[l : l + 1])
    carried = r.mid_grad[...] + grad
    if bottom:
        shard = r.returned.shape[1]
        for j in range(4):
            r.leaving[j] = carried[:, j * shard : (j + 1) * shard].astype(BF)
        back = Return(place, r, r.leaving, r.returned)
        back.start()
    else:
        r.carried[...] = carried
    r.small_rows[...] = jnp.zeros_like(r.small_rows)
    small = [totals[o][s] for o in range(3) for s in range(3)] + [gain_part, r.gain_two[...]]
    at = 0
    for x in small:
        for start in range(0, x.shape[1], 128):
            part = x[:, start : start + 128]
            r.small_rows[at : at + 1, 0 : part.shape[1]] = part
            at += 1
    r.g_small[...] = jnp.zeros_like(r.g_small)
    r.g_small[0 : r.small_rows.shape[0]] = r.small_rows[...].astype(BF)
    if bottom:
        scatter.start((3,))
    ffn_scatter.finish()
    if bottom:
        ffn_spread.start()
        scatter.middle((1, 2))
        scatter.second((0, 3))
        scatter.finish((1, 2))
        mix_spread.start((1, 2))
        scatter.middle((0, 3))
        ffn_spread.forward()
        scatter.finish((0, 3))
        mix_spread.start((0, 3))
        mix_spread.forward((1, 2))
        back.finish()
        r.stream_grad[...] = r.returned[...].astype(F32)
        mix_spread.forward((0, 3))
        mix_spread.finish((3,))
        if above:
            spread.finish()
        gain_sums(place, r, above)
        mix_spread.finish((0, 1, 2))
        ffn_spread.finish()
    elif above:
        spread.finish()
    group.finish()


def gain_sums(place, r, above):
    count = r.small_rows.shape[0]
    r.gain_parts[0, 0] = r.q_small[0:count]
    if above:
        r.gain_parts[0, 1] = r.r_small[0:count]

    def gain_copy(j):
        chan = lax.rem(place.chan + j, 4)
        return remote(
            r.gain_parts.at[0], r.gain_parts.at[j], r.gain_send.at[j], r.gain_recv.at[j], {"chan": chan}
        )

    for j in range(1, 4):
        gain_copy(j).start()
    for j in range(1, 4):
        gain_copy(j).wait()
    total = r.gain_parts[0].astype(F32)
    for j in range(1, 4):
        total += r.gain_parts[j].astype(F32)
    r.gain_grads[...] = total


def mixer_backward(l, fwd, mid_grad, tables, gain_two, ffn_grads, pending):
    rows, width = mid_grad.shape
    layers, _, length, lanes = fwd.s_mix.shape
    groups, feats, units = fwd.w_ci_out.shape[1:]
    inner = groups * units
    wide = -(-lanes // 128) * 128
    above = pending is not None
    held = ("w_out_out", "w_ci_out", "w_co_out", "s_mix", "s_pre", "w_in_out", "s_h_mixer")
    ins = dict(
        mid_grad=mid_grad, values=fwd.values, gains=fwd.gains, taps=fwd.taps_out,
        mask_prev=fwd.mask_prev, mask_next=fwd.mask_next, cosine=tables[0], sine=tables[1],
        gain_two=gain_two, ffn_grads=ffn_grads, **{n: getattr(fwd, n) for n in held},
    )
    grads = dict(
        g_proj=((4 * lanes, width), BF),
        g_spec=((length, 2 * lanes), BF),
        g_mlp=((2 * groups * feats, units), BF),
        g_small=((256, 128), BF),
    )
    shapes = [g[0] for g in grads.values()]
    ffn_total = ((ffn_grads.shape[0] // 8, ffn_grads.shape[1]), BF)
    outs, scratch = {}, Scatter.scratch([ffn_grads.shape], "fs")
    hbm = held + ("ffn_grads", "cosine", "sine", "values")
    if above:
        ins.update(**{"t_" + n: pending[n] for n in GRADS})
        outs.update(
            **{"r_" + n: ((pending[n].shape[0] * 8, pending[n].shape[1]), BF) for n in GRADS}
        )
        scratch.update(Spread.scratch(len(GRADS)))
    count = 32
    if l == 0:
        shard = lanes
        outs.update(
            stream_grad=((length, shard), F32),
            gain_grads=((2 if above else 1, count, 128), F32),
            ffn_result=(ffn_grads.shape, BF),
            **{"q_" + n: grads["g_" + n] for n in GRADS},
        )
        scratch.update(
            ffn_total=pltpu.VMEM(*ffn_total),
            leaving=pltpu.VMEM((4, rows, shard), BF),
            returned=pltpu.VMEM((length, shard), BF),
            gain_parts=pltpu.VMEM((4, 2 if above else 1, count, 128), BF),
            gain_send=pltpu.SemaphoreType.DMA((4,)),
            gain_recv=pltpu.SemaphoreType.DMA((4,)),
            **{n: pltpu.VMEM(*g) for n, g in grads.items()},
            **{
                "u_" + n: pltpu.VMEM((g[0][0] // 8, g[0][1]), BF)
                for n, g in zip(GRADS, grads.values())
            },
            **Return.scratch(),
            **Scatter.scratch(shapes),
            **Spread.scratch(1, "fp"),
            **Spread.scratch(len(GRADS), "mp"),
        )
    else:
        outs.update(carried=((rows, width), F32), ffn_total=ffn_total, **grads)
    return call_kernel(
        functools.partial(mixer_backward_body, l, above),
        ins,
        outs,
        dict(
            m_all=pltpu.VMEM((length, width), BF),
            h_all=pltpu.VMEM((length, width), BF),
            mix=pltpu.VMEM((MIX_ROWS, length, lanes), BF),
            pre_all=pltpu.VMEM((length, inner), BF),
            w_in=pltpu.VMEM((1,) + fwd.w_in_out.shape[1:], BF),
            w_out=pltpu.VMEM((1,) + fwd.w_out_out.shape[1:], BF),
            w_ci=pltpu.VMEM((1,) + fwd.w_ci_out.shape[1:], F32),
            w_co=pltpu.VMEM((1,) + fwd.w_co_out.shape[1:], F32),
            cos=pltpu.VMEM((length, length), BF),
            sin=pltpu.VMEM((length, length), BF),
            load_sem=pltpu.SemaphoreType.DMA((10,)),
            layer_in=pltpu.VMEM((rows, width), F32),
            padded=pltpu.VMEM((3, length + 2 * PAD, lanes), F32),
            q_g=pltpu.VMEM((length, lanes), BF),
            both_re=pltpu.VMEM((length, 2 * wide), BF),
            both_im=pltpu.VMEM((length, 2 * wide), BF),
            proj_grads=pltpu.VMEM((3, length, lanes), BF),
            own_part=pltpu.VMEM((rows, width), F32),
            sum_in=pltpu.VMEM((2, lanes, inner), F32),
            sum_out=pltpu.VMEM((2, lanes, inner), F32),
            small_rows=pltpu.VMEM((count, 128), F32),
            **mlp_scratch(lanes, inner),
            **Group.scratch(rows, width),
            **scratch,
        ),
        40 + l,
        9 * 10**9,
        hbm,
    )


def on_device(
    stream,
    segments,
    cotangent,
    norm_one,
    in_proj,
    short_taps,
    cond_in,
    cond_out,
    filter_spec,
    out_proj,
    norm_two,
    gate_proj,
    up_proj,
    down_proj,
):
    chan = lax.axis_index("chan")
    layers, width = in_proj.shape[:2]
    shard = norm_one.shape[1]
    length = filter_spec.shape[2]
    groups, feats = cond_in.shape[1:3]
    tables = dft_tables(length)
    arrays = dict(
        in_proj=in_proj.transpose(0, 2, 1, 3),
        cond_in=cond_in,
        cond_out=cond_out,
        filter_spec=filter_spec,
        out_proj=out_proj,
        gate_proj=gate_proj,
        up_proj=up_proj,
        down_proj=down_proj,
    )

    fwd = forward(
        arrays,
        stream,
        cotangent,
        segments[:, None],
        jnp.concatenate([norm_one, norm_two], 0),
        short_taps.reshape(-1, shard),
        tables,
    )
    carried = fwd.carried
    ffn_results, mixer_results = {}, {}
    grads, ffn_total, output = None, None, None
    for l in reversed(range(layers)):
        last = l + 1 == layers
        back = ffn_backward(
            l, fwd, carried, last, shard, None if last else (grads, ffn_total)
        )
        if last:
            output, pending = back.output, None
        else:
            ffn_results[l + 1] = back.ffn_result
            pending = {n: getattr(back, "t_" + n) for n in GRADS}
        down = mixer_backward(
            l, fwd, back.mid_grad, tables, back.gain_grad, back.weight_grads, pending
        )
        if not last:
            mixer_results[l + 1] = {n: getattr(down, "r_" + n) for n in GRADS}
        if l > 0:
            carried, ffn_total = down.carried, down.ffn_total
            grads = {n: getattr(down, "g_" + n) for n in GRADS}
    ffn_results[0] = down.ffn_result
    mixer_results[0] = {n: getattr(down, "q_" + n) for n in GRADS}

    def everywhere(x):
        return lax.psum(x, "outer") if lax.axis_size("outer") > 1 else x

    def stacked(get):
        return everywhere(jnp.stack([get(l) for l in range(layers)])).astype(F32)

    def mixer_stack(name, get):
        return stacked(lambda l: get(mixer_results[l][name]))

    def ffn_stack(index):
        return stacked(lambda l: ffn_results[l][index * width : (index + 1) * width])

    gain_grads = everywhere(down.gain_grads)
    steps = -(-shard // 128)
    taps_rows, gain_rows = 9 * steps, width // 128

    def gain_stack(at):
        whole = gain_grads[:, at : at + gain_rows].reshape(layers, width)
        return lax.dynamic_slice_in_dim(whole, chan * shard, shard, 1)

    mlp_rows = groups * feats
    return (
        output,
        down.stream_grad,
        gain_stack(taps_rows),
        mixer_stack("proj", lambda x: x[: 3 * shard].reshape(3, shard, width).transpose(2, 0, 1)),
        mixer_stack(
            "small",
            lambda x: x[:taps_rows].reshape(9, steps * 128)[:, :shard].reshape(short_taps.shape[1:]),
        ),
        mixer_stack("mlp", lambda x: x[:mlp_rows].reshape(cond_in.shape[1:])),
        mixer_stack("mlp", lambda x: x[mlp_rows:].reshape(cond_out.shape[1:])),
        mixer_stack("spec", lambda x: jnp.stack([x[:, :shard], x[:, shard:]])),
        mixer_stack("proj", lambda x: x[3 * shard :]),
        gain_stack(taps_rows + gain_rows),
        ffn_stack(0),
        ffn_stack(1),
        ffn_stack(2),
    )


def solution(mesh):
    dp_count, chan_count = mesh.devices.shape
    fine = Mesh(
        mesh.devices.reshape(dp_count // 8, 4, 2, chan_count), ("outer", "col", "half", "chan")
    )
    dp = ("outer", "col", "half")
    weight_specs = (
        P(None, "chan"),
        P(None, None, None, "chan"),
        P(None, None, None, "chan"),
        P(None, "chan", None, None),
        P(None, "chan", None, None),
        P(None, None, None, "chan"),
        P(None, "chan", None),
        P(None, "chan"),
        P(None, None, "chan"),
        P(None, None, "chan"),
        P(None, "chan", None),
    )
    return jax.shard_map(
        on_device,
        mesh=fine,
        in_specs=(P(dp, "chan"), P(dp), P(dp, "chan")) + weight_specs,
        out_specs=(P(dp, "chan"), P(dp, "chan")) + weight_specs,
        check_vma=False,
    )
```

```python
import functools
import math
from types import SimpleNamespace

import jax
import jax.numpy as jnp
import numpy as np
from jax import lax
from jax.experimental import pallas as pl
from jax.experimental.pallas import tpu as pltpu
from jax.sharding import Mesh
from jax.sharding import PartitionSpec as P

EPSILON = 1e-05
BF = jnp.bfloat16
F32 = jnp.float32


def dft_tables(length):
    positions = np.arange(length)
    angles = (positions[:, None] * positions[None, :] % length) * (2.0 * math.pi / length)
    scale = 1.0 / math.sqrt(length)
    cosine = np.asarray(np.cos(angles) * scale, dtype=np.float32)
    sine = np.asarray(-np.sin(angles) * scale, dtype=np.float32)
    return jnp.asarray(cosine, BF), jnp.asarray(sine, BF)


def normal_cdf(x):
    return 0.5 * (1.0 + lax.erf(x * (2.0**-0.5)))


def normal_pdf(x):
    return jnp.exp(-0.5 * x * x) * (1.0 / math.sqrt(2.0 * math.pi))


MESH = pl.DeviceIdType.MESH
VMEM_LIMIT = 63 << 20
CHUNKS = 2
PARTS = 8


def nt_dot(a, b):
    return lax.dot_general(a, b, (((1,), (1,)), ((), ())), preferred_element_type=F32)


def tn_dot(a, b):
    return lax.dot_general(a, b, (((0,), (0,)), ((), ())), preferred_element_type=F32)


def nn_dot(a, b):
    return jnp.dot(a, b, preferred_element_type=F32)


def aligned(index, size):
    return pl.ds(pl.multiple_of(index * size, size), size)


class Place:
    def __init__(self):
        self.col = lax.axis_index("col")
        self.half = lax.axis_index("half")
        self.chan = lax.axis_index("chan")
        odd = lax.rem(self.chan, 2)
        self.pack = self.chan // 2
        self.own = self.half == self.pack
        self.other_half = 1 - self.half
        self.near_chan = self.chan + 1 - 2 * odd
        self.far_chan = self.chan + 2 - 4 * self.pack
        self.rank = 2 * self.half + odd
        flip_near, flip_peer = 1 - 2 * odd, 2 - 4 * self.half
        self.ranks = [
            self.rank,
            self.rank + flip_near,
            self.rank + flip_peer,
            self.rank + flip_near + flip_peer,
        ]

    def col_at(self, step):
        return lax.rem(self.col + step, 4)

    def barrier(self):
        sem = pltpu.get_barrier_semaphore()
        devices = [{"col": self.col_at(j)} for j in range(1, 4)]
        for i in range(1, 8):
            half = self.half if i < 4 else self.other_half
            devices.append({"half": half, "chan": lax.rem(self.chan + i, 4)})
        for device in devices:
            pl.semaphore_signal(sem, inc=1, device_id=device, device_id_type=MESH)
        pl.semaphore_wait(sem, len(devices))


def remote(src, dst, send_sem, recv_sem, device):
    return pltpu.make_async_remote_copy(
        src_ref=src,
        dst_ref=dst,
        send_sem=send_sem,
        recv_sem=recv_sem,
        device_id=device,
        device_id_type=MESH,
    )


def await_recv(ref, recv_sem, send_sem):
    remote(ref, ref, send_sem, recv_sem, {"half": 1 - lax.axis_index("half")}).wait_recv()


def await_send(ref, send_sem, recv_sem):
    remote(ref, ref, send_sem, recv_sem, {"half": 1 - lax.axis_index("half")}).wait_send()


class Group:
    def __init__(self, place, r, rows, turn=0):
        self.place = place
        self.near = {"chan": place.near_chan}
        self.peer = {"half": place.other_half}
        self.send, self.recv = r.group_send.at[turn], r.group_recv.at[turn]
        self.to_peer, self.from_peer = r.to_peer, r.from_peer.at[turn]
        self.to_near, self.from_near = r.to_near, r.from_near.at[turn]
        self.rows, self.size = rows, rows // CHUNKS
        self.started = []

    @staticmethod
    def scratch(rows, width, turns=1):
        return dict(
            group_send=pltpu.SemaphoreType.DMA((turns, 6, CHUNKS)),
            group_recv=pltpu.SemaphoreType.DMA((turns, 6, CHUNKS)),
            to_peer=pltpu.VMEM((2, rows, width), BF),
            from_peer=pltpu.VMEM((turns, 2, rows, width), BF),
            to_near=pltpu.VMEM((rows, width), BF),
            from_near=pltpu.VMEM((turns, rows, width), BF),
        )

    def at(self, which, chunk=None):
        start = self.place.ranks[which] * self.rows
        if chunk is None:
            return pl.ds(pl.multiple_of(start, self.rows), self.rows)
        return pl.ds(pl.multiple_of(start + chunk * self.size, self.size), self.size)

    def start(self, src, dst, kind, chunk, device):
        copy = remote(src, dst, self.send.at[kind, chunk], self.recv.at[kind, chunk], device)
        copy.start()
        self.started.append(copy)

    def arrived(self, ref, kind, chunk):
        await_recv(ref, self.recv.at[kind, chunk], self.send.at[kind, chunk])

    def gather_start(self, full):
        for chunk in range(CHUNKS):
            own = full.at[self.at(0, chunk)]
            self.start(own, own, 0, chunk, self.near)
        for chunk in range(CHUNKS):
            own = full.at[self.at(0, chunk)]
            self.start(own, own, 1, chunk, self.peer)

    def gather_peer(self, full):
        for chunk in range(CHUNKS):
            self.arrived(full.at[self.at(2, chunk)], 1, chunk)

    def gather_near(self, full, chunk):
        piece = full.at[self.at(1, chunk)]
        self.arrived(piece, 0, chunk)
        self.start(piece, piece, 2, chunk, self.peer)

    def gather_diagonal(self, full, chunk):
        self.arrived(full.at[self.at(3, chunk)], 2, chunk)

    def piece(self, chunk):
        return pl.ds(chunk * self.size, self.size)

    def reduce_peer(self, slot, chunk, value):
        at = self.piece(chunk)
        self.to_peer[slot, at] = value.astype(BF)
        self.start(self.to_peer.at[slot, at], self.from_peer.at[slot, at], 3 + slot, chunk, self.peer)

    def reduce_near(self, chunk, value):
        at = self.piece(chunk)
        self.arrived(self.from_peer.at[1, at], 4, chunk)
        self.to_near[at] = (value + self.from_peer[1, at].astype(F32)).astype(BF)
        self.start(self.to_near.at[at], self.from_near.at[at], 5, chunk, self.near)

    def reduce_end(self, chunk):
        at = self.piece(chunk)
        self.arrived(self.from_peer.at[0, at], 3, chunk)
        self.arrived(self.from_near.at[at], 5, chunk)
        return self.from_peer[0, at].astype(F32) + self.from_near[at].astype(F32)

    def reduce_whole(self, kind, part):
        for chunk in range(CHUNKS):
            value = part[chunk * self.size : (chunk + 1) * self.size]
            if kind == "near":
                self.reduce_near(chunk, value)
            else:
                self.reduce_peer({"peer": 0, "diagonal": 1}[kind], chunk, value)

    def finish(self):
        for copy in self.started:
            copy.wait_send()


class Weights:
    def __init__(self, place, sems, pairs):
        self.place, self.pairs = place, pairs
        self.send, self.recv, self.local = sems

    def cut(self, ref, axis, parts, index):
        at = aligned(index, ref.shape[axis] // parts)
        return ref.at[(slice(None),) * axis + (at,)]

    def index(self, parts, col, half):
        return col * 2 + half if parts == 8 else col

    def each(self, which):
        which = range(len(self.pairs)) if which is None else which
        return [(a, self.pairs[a]) for a in which]

    def each_sent(self, act, which=None):
        p = self.place
        owner = {"half": p.pack, "chan": p.far_chan}
        for a, (src, dst, axis, parts) in self.each(which):

            def send(a=a, src=src, dst=dst, axis=axis, parts=parts):
                index = self.index(parts, p.col, p.half)
                act(
                    remote(
                        self.cut(src, axis, parts, index),
                        self.cut(dst, axis, parts, index),
                        self.send.at[a, 0],
                        self.recv.at[a, p.half if parts == 8 else 0],
                        owner,
                    )
                )

            if parts == 8:
                send()
            else:
                pl.when(p.half == 0)(send)

    def start(self, which=None):
        self.each_sent(lambda c: c.start(), which)

        @pl.when(self.place.own)
        def _():
            for a, (src, dst, axis, parts) in self.each(which):
                pltpu.make_async_copy(src, dst, self.local.at[a]).start()

    def forward(self, which=None):
        p = self.place

        @pl.when(jnp.logical_not(p.own))
        def _():
            for a, (src, dst, axis, parts) in self.each(which):
                for s in range(parts // 4):
                    piece = self.cut(dst, axis, parts, self.index(parts, p.col, s))
                    await_recv(piece, self.recv.at[a, s], self.send.at[a, 0])
                    for j in range(1, 4):
                        remote(
                            piece,
                            piece,
                            self.send.at[a, 2 * j - 1 + s],
                            self.recv.at[a, 2 * j + s],
                            {"col": p.col_at(j)},
                        ).start()

    def ready(self, which=None):
        p = self.place

        @pl.when(p.own)
        def _():
            for a, (src, dst, axis, parts) in self.each(which):
                pltpu.make_async_copy(src, dst, self.local.at[a]).wait()

        @pl.when(jnp.logical_not(p.own))
        def _():
            for a, (src, dst, axis, parts) in self.each(which):
                for s in range(parts // 4):
                    for j in range(1, 4):
                        piece = self.cut(dst, axis, parts, self.index(parts, p.col_at(4 - j), s))
                        await_recv(piece, self.recv.at[a, 2 * j + s], self.send.at[a, 0])

    def finish(self):
        p = self.place
        self.each_sent(lambda c: c.wait_send())

        @pl.when(jnp.logical_not(p.own))
        def _():
            for a, (src, dst, axis, parts) in enumerate(self.pairs):
                for s in range(parts // 4):
                    for j in range(1, 4):
                        piece = self.cut(dst, axis, parts, self.index(parts, p.col_at(4 - j), s))
                        await_send(piece, self.send.at[a, 2 * j - 1 + s], self.recv.at[a, 0])


class Load:
    def __init__(self, r, pairs, first=0):
        self.copies = [
            pltpu.make_async_copy(src, dst, r.load_sem.at[first + a])
            for a, (src, dst) in enumerate(pairs)
        ]

    def start(self):
        for copy in self.copies:
            copy.start()

    def finish(self, which=None):
        for a in range(len(self.copies)) if which is None else which:
            self.copies[a].wait()


class Exchange:
    def __init__(self, place, r, src, dst, name="ex"):
        self.place, self.src, self.dst = place, src, dst
        self.send, self.recv, self.local = [
            getattr(r, f"{name}_{n}") for n in ("send", "recv", "local")
        ]
        self.size = src.shape[0] // 4

    @staticmethod
    def scratch(name="ex"):
        return {
            f"{name}_send": pltpu.SemaphoreType.DMA((4,)),
            f"{name}_recv": pltpu.SemaphoreType.DMA((4,)),
            f"{name}_local": pltpu.SemaphoreType.DMA,
        }

    def each(self, act, act_self):
        p = self.place
        for j in range(4):
            chan = 2 * p.half + j % 2
            mine = (p.half == j // 2) & (p.chan == chan)
            src, dst = self.src.at[pl.ds(j * self.size, self.size)], self.dst.at[p.chan]

            def go(j=j, chan=chan, src=src, dst=dst):
                act(
                    remote(
                        src, dst, self.send.at[j], self.recv.at[p.chan],
                        {"half": j // 2, "chan": chan},
                    )
                )

            def stay(src=src, dst=dst):
                act_self(pltpu.make_async_copy(src, dst, self.local))

            pl.when(jnp.logical_not(mine))(go)
            pl.when(mine)(stay)

    def start(self):
        self.each(lambda c: c.start(), lambda c: c.start())

    def finish(self):
        p = self.place
        self.each(lambda c: c.wait_send(), lambda c: c.wait())
        for j in range(4):

            def wait(j=j):
                await_recv(self.dst.at[j], self.recv.at[j], self.send.at[0])

            pl.when(jnp.logical_not(p.own & (p.chan == j)))(wait)


class Return:
    def __init__(self, place, r, src, dst, turn):
        self.place, self.src, self.dst = place, src, dst
        self.send, self.recv = r.back_send.at[turn], r.back_recv.at[turn]
        self.local = r.back_local.at[turn]
        self.size = src.shape[1]

    @staticmethod
    def scratch():
        return dict(
            back_send=pltpu.SemaphoreType.DMA((2, 4)),
            back_recv=pltpu.SemaphoreType.DMA((2, 4)),
            back_local=pltpu.SemaphoreType.DMA((2,)),
        )

    def each(self, act, act_self):
        p = self.place
        for j in range(4):
            mine = p.own & (p.chan == j)
            src, dst = self.src.at[j], self.dst.at[aligned(p.rank, self.size)]

            def go(j=j, src=src, dst=dst):
                act(
                    remote(
                        src, dst, self.send.at[j], self.recv.at[p.rank],
                        {"half": p.pack, "chan": j},
                    )
                )

            def stay(src=src, dst=dst):
                act_self(pltpu.make_async_copy(src, dst, self.local))

            pl.when(jnp.logical_not(mine))(go)
            pl.when(mine)(stay)

    def start(self):
        self.each(lambda c: c.start(), lambda c: c.start())

    def finish(self):
        p = self.place
        self.each(lambda c: c.wait_send(), lambda c: c.wait())
        for j in range(4):
            mine = (p.half == j // 2) & (p.chan == 2 * p.half + j % 2)

            def wait(j=j):
                await_recv(
                    self.dst.at[pl.ds(j * self.size, self.size)], self.recv.at[j], self.send.at[0]
                )

            pl.when(jnp.logical_not(mine))(wait)


class Scatter:
    def __init__(self, place, r, sources, totals, name, turn):
        self.place, self.sources, self.totals = place, sources, totals
        self.send, self.recv, self.local = [
            getattr(r, f"{name}_{n}").at[turn] for n in ("send", "recv", "local")
        ]
        self.kept, self.got, self.late, self.cross = [
            [getattr(r, f"{name}_{part}{a}") for a in range(len(sources))]
            for part in ("kept", "got", "late", "cross")
        ]
        self.cross = [c.at[turn] for c in self.cross]
        self.x = lax.rem(place.col, 2)
        self.y = place.col // 2
        self.to_x = {"col": place.col + 1 - 2 * self.x}
        self.to_y = {"col": lax.rem(place.col + 2, 4)}

    @staticmethod
    def scratch(shapes, name, turns):
        n = len(shapes)
        out = {
            f"{name}_send": pltpu.SemaphoreType.DMA((turns, n, 8)),
            f"{name}_recv": pltpu.SemaphoreType.DMA((turns, n, 8)),
            f"{name}_local": pltpu.SemaphoreType.DMA((turns, n, 4)),
        }
        for a, (rows, width) in enumerate(shapes):
            for part, count in (("kept", 4), ("got", 4), ("late", 2)):
                out[f"{name}_{part}{a}"] = pltpu.VMEM((count, rows // 8, width), BF)
            out[f"{name}_cross{a}"] = pltpu.VMEM((turns, 2, rows // 8, width), BF)
        return out

    def each(self, which):
        return range(len(self.sources)) if which is None else which

    def piece(self, a, y, x, half):
        src = self.sources[a]
        return src.at[aligned((2 * y + x) * 2 + half, src.shape[0] // 8)]

    def firsts(self, a):
        out = []
        for i in range(2):
            out.append((self.piece(a, i, 1 - self.x, 0), i, self.to_x))
            out.append((self.piece(a, 1 - self.y, i, 1), 2 + i, self.to_y))
        return [
            remote(src, self.got[a].at[k], self.send.at[a, k], self.recv.at[a, k], device)
            for src, k, device in out
        ]

    def keeps(self, a):
        out = []
        for i in range(2):
            out.append((self.piece(a, i, self.x, 0), i))
            out.append((self.piece(a, self.y, i, 1), 2 + i))
        return [
            pltpu.make_async_copy(src, self.kept[a].at[k], self.local.at[a, k]) for src, k in out
        ]

    def seconds(self, a):
        kept, late = self.kept[a], self.late[a]
        return [
            remote(kept.at[1 - self.y], late.at[0], self.send.at[a, 4], self.recv.at[a, 4], self.to_y),
            remote(kept.at[3 - self.x], late.at[1], self.send.at[a, 5], self.recv.at[a, 5], self.to_x),
        ]

    def summed(self, part):
        return self.y + part * (2 + self.x - self.y)

    def third(self, a, slot, part, half, chan):
        return remote(
            self.kept[a].at[self.summed(part)],
            self.cross[a].at[slot],
            self.send.at[a, 6 + slot],
            self.recv.at[a, 6 + slot],
            {"half": half, "chan": chan},
        )

    def start(self, which=None):
        for a in self.each(which):
            for copy in self.firsts(a) + self.keeps(a):
                copy.start()

    def second(self, which=None):
        for a in self.each(which):
            for copy in self.firsts(a) + self.keeps(a):
                copy.wait()
            for k in range(4):
                total = self.kept[a][k].astype(F32) + self.got[a][k].astype(F32)
                self.kept[a][k] = total.astype(BF)
            for copy in self.seconds(a):
                copy.start()

    def middle(self, which=None):
        p = self.place
        for a in self.each(which):
            for copy in self.seconds(a):
                copy.wait()
            kept, late = self.kept[a], self.late[a]
            for part in range(2):
                at = self.summed(part)
                kept[at] = (kept[at].astype(F32) + late[part].astype(F32)).astype(BF)

            @pl.when(p.own)
            def _():
                self.third(a, 0, p.other_half, p.other_half, p.chan).start()

            @pl.when(jnp.logical_not(p.own))
            def _():
                self.third(a, 0, p.half, p.half, p.far_chan).start()
                self.third(a, 1, p.other_half, p.other_half, p.far_chan).start()

    def finish(self, which=None):
        p = self.place
        for a in self.each(which):
            cross = self.cross[a]
            await_recv(cross.at[0], self.recv.at[a, 6], self.send.at[a, 6])
            await_send(cross.at[0], self.send.at[a, 6], self.recv.at[a, 6])

            @pl.when(p.own)
            def _():
                self.totals[a][...] = (
                    cross[0].astype(F32) + self.kept[a][self.summed(p.half)].astype(F32)
                ).astype(BF)

            @pl.when(jnp.logical_not(p.own))
            def _():
                await_recv(cross.at[1], self.recv.at[a, 7], self.send.at[a, 7])
                await_send(cross.at[1], self.send.at[a, 7], self.recv.at[a, 7])
                self.totals[a][...] = (cross[0].astype(F32) + cross[1].astype(F32)).astype(BF)


class Spread:
    def __init__(self, place, r, totals, results, name, turn):
        self.place, self.totals, self.results = place, totals, results
        self.send, self.recv, self.kept = [
            getattr(r, f"{name}_{n}").at[turn] for n in ("send", "recv", "local")
        ]

    @staticmethod
    def scratch(count, name, turns):
        return {
            f"{name}_send": pltpu.SemaphoreType.DMA((turns, count, 7)),
            f"{name}_recv": pltpu.SemaphoreType.DMA((turns, count, 7)),
            f"{name}_local": pltpu.SemaphoreType.DMA((turns, count)),
        }

    def each(self, which):
        return range(len(self.totals)) if which is None else which

    def slot(self, a, col, half):
        result = self.results[a]
        return result.at[aligned(col * 2 + half, result.shape[0] // 8)]

    def local(self, a):
        p = self.place
        return pltpu.make_async_copy(
            self.totals[a], self.slot(a, p.col, p.half), self.kept.at[a]
        )

    def out(self, a, j):
        p = self.place
        device = {"col": p.col_at(j)} if j else {"half": p.other_half}
        return remote(
            self.totals[a],
            self.slot(a, p.col, p.half),
            self.send.at[a, j],
            self.recv.at[a, j],
            device,
        )

    def pass_on(self, a, j):
        p = self.place
        piece = self.slot(a, p.col_at(4 - j), p.half)
        return remote(
            piece, piece, self.send.at[a, 3 + j], self.recv.at[a, 3 + j],
            {"half": p.other_half},
        )

    def start(self, which=None):
        for a in self.each(which):
            for j in (1, 2, 3, 0):
                self.out(a, j).start()
            self.local(a).start()

    def forward(self, which=None):
        p = self.place
        for a in self.each(which):
            for j in range(1, 4):
                piece = self.slot(a, p.col_at(4 - j), p.half)
                await_recv(piece, self.recv.at[a, j], self.send.at[a, j])
                self.pass_on(a, j).start()

    def finish(self, which=None):
        p = self.place
        for a in self.each(which):
            for j in range(4):
                self.out(a, j).wait_send()
            self.local(a).wait()
            await_recv(
                self.slot(a, p.col, p.other_half), self.recv.at[a, 0], self.send.at[a, 0]
            )
            for j in range(1, 4):
                self.pass_on(a, j).wait_send()
                piece = self.slot(a, p.col_at(4 - j), p.other_half)
                await_recv(piece, self.recv.at[a, 3 + j], self.send.at[a, 3 + j])


def call_kernel(body, ins, outs, scratch, collective_id, flops, hbm=()):
    names = list(ins) + list(outs) + list(scratch)

    def run(*refs):
        body(SimpleNamespace(**dict(zip(names, refs))))

    def spec(name):
        return pl.BlockSpec(memory_space=pl.ANY if name in hbm else pltpu.VMEM)

    results = pl.pallas_call(
        run,
        out_shape=[jax.ShapeDtypeStruct(*o) for o in outs.values()],
        in_specs=[spec(n) for n in ins],
        out_specs=[spec(n) for n in outs],
        scratch_shapes=list(scratch.values()),
        compiler_params=pltpu.CompilerParams(
            collective_id=collective_id, has_side_effects=True, vmem_limit_bytes=VMEM_LIMIT
        ),
        cost_estimate=pl.CostEstimate(flops=flops, bytes_accessed=20 << 20, transcendentals=0),
    )(*ins.values())
    return SimpleNamespace(**dict(zip(outs, results)))


def normalized(x):
    average = jnp.mean(x, 1, keepdims=True)
    centered = x - average
    variance = jnp.mean(centered * centered, 1, keepdims=True)
    inv = lax.rsqrt(variance + EPSILON)
    return centered * inv, inv


def norm_grad_rows(grad, x, gain):
    xhat, inv = normalized(x)
    gain_part = jnp.sum(grad * xhat, 0, keepdims=True)
    scaled = grad * gain
    mean_plain = jnp.mean(scaled, 1, keepdims=True)
    mean_cross = jnp.mean(scaled * xhat, 1, keepdims=True)
    return inv * (scaled - mean_plain - xhat * mean_cross), gain_part


PAD = 8


def shifted(ref, s, tile, size, offset):
    return ref[s, pl.ds(PAD + tile * size + offset, size)]


def mlp_tables(r, l):
    groups, feats, inner = r.w_ci.shape[1:]
    half = feats // 2
    for table in (r.in_re, r.in_im, r.out_re, r.out_im):
        table[...] = jnp.zeros_like(table)
    for g in range(groups):
        rows, cols = pl.ds(g * half, half), pl.ds(g * inner, inner)
        r.in_re[rows, cols] = r.w_ci[l, g, 0:half].astype(BF)
        r.in_im[rows, cols] = r.w_ci[l, g, half:feats].astype(BF)
        turned = r.w_co[l, g].T
        r.out_re[rows, cols] = turned[0:half].astype(BF)
        r.out_im[rows, cols] = turned[half:feats].astype(BF)


def mlp_scratch(shard, inner):
    table = pltpu.VMEM((shard, inner), BF)
    return dict(in_re=table, in_im=table, out_re=table, out_im=table)


MIXER = dict(in_proj="w_in", cond_in="w_ci", cond_out="w_co", out_proj="w_out", filter_spec="w_spec")
FFN = dict(gate_proj="w_gate", up_proj="w_up", down_proj="w_down")
CUTS = dict(in_proj=1, cond_in=1, cond_out=1, filter_spec=1, out_proj=0, gate_proj=0, up_proj=0, down_proj=0)
PROJ, QUERY, MIXED, SPECTRA, MIX_ROWS = 0, 3, 4, 5, 11


def forward_body(r):
    place = Place()
    layers, rows, width = r.mids.shape
    length = r.seg.shape[0]
    lanes = r.w_in.shape[3]
    wide = r.both.shape[1] // 2
    tiles = 4
    size = length // tiles
    exchange = Exchange(place, r, r.stream, r.pieces)
    tables = [
        pltpu.make_async_copy(r.cosine, r.cos, r.table_sem.at[0]),
        pltpu.make_async_copy(r.sine, r.sin, r.table_sem.at[1]),
    ]

    def weights(kind, names, l):
        sems = [getattr(r, f"{kind}_{n}").at[l] for n in ("send", "recv", "local")]
        pairs = [
            (getattr(r, n).at[l], getattr(r, to).at[l], CUTS[n], 4 if n == "out_proj" else 8)
            for n, to in names.items()
        ]
        return Weights(place, sems, pairs)

    rest = (1, 2, 3, 4)
    mixer_weights = [weights("mw", MIXER, l) for l in range(layers)]
    ffn_weights = [weights("fw", FFN, l) for l in range(layers)]
    place.barrier()
    exchange.start()
    own, other = place.own, jnp.logical_not(place.own)

    def gain_copy(j):
        chan = lax.rem(place.chan + j, 4)
        return remote(r.small, r.gain_parts.at[j], r.gain_send.at[j], r.gain_recv.at[j], {"chan": chan})

    for j in range(1, 4):
        gain_copy(j).start()
    seg_copy = remote(r.seg, r.seg_got, r.gain_send.at[4], r.gain_recv.at[4], {"half": place.other_half})
    taps_copy = remote(r.taps, r.taps_got, r.gain_send.at[5], r.gain_recv.at[5], {"chan": place.far_chan})

    @pl.when(own)
    def _():
        seg_copy.start()
        taps_copy.start()

    mixer_weights[0].start((0,))
    for copy in tables:
        copy.start()
    r.edges[0:PAD] = jnp.full((PAD, 1), -1, jnp.int32)
    r.edges[PAD + length : 2 * PAD + length] = jnp.full((PAD, 1), -1, jnp.int32)
    for s in range(3):
        r.padded[s, 0:PAD] = jnp.zeros((PAD, lanes), F32)
        r.padded[s, PAD + length : 2 * PAD + length] = jnp.zeros((PAD, lanes), F32)
    r.both[...] = jnp.zeros_like(r.both)

    @pl.when(own)
    def _():
        r.edges[PAD : PAD + length] = r.seg[...]
        r.taps_out[...] = r.taps[...]
        seg_copy.wait_send()
        taps_copy.wait_send()

    @pl.when(other)
    def _():
        seg_copy.wait_recv()
        taps_copy.wait_recv()
        r.edges[PAD : PAD + length] = r.seg_got[...]
        r.taps_out[...] = r.taps_got[...]

    here = r.edges[PAD : PAD + length]
    r.masks[:, 0:1] = jnp.where(r.edges[PAD - 1 : PAD - 1 + length] == here, 1.0, 0.0)
    r.masks[:, 1:2] = jnp.where(r.edges[PAD + 1 : PAD + 1 + length] == here, 1.0, 0.0)
    for j in range(1, 4):
        gain_copy(j).wait()
    r.gain_parts[0] = r.small[...]
    parts = []
    for c in range(4):
        parts.append(r.gain_parts[lax.rem(place.chan - c + 4, 4)])
    r.gains[...] = jnp.concatenate(parts, 1)
    exchange.finish()
    mixer_weights[0].start(rest)
    r.values[0] = jnp.concatenate([r.pieces[j] for j in range(4)], 1).astype(F32)

    def tap(l, o, s):
        at = 9 * l + 3 * o + s
        return r.taps_out[at : at + 1]

    saves = {}

    def save(name, *copies):
        saves[name] = [pltpu.make_async_copy(src, dst, r.save_sem.at[i]) for i, src, dst in copies]
        for copy in saves[name]:
            copy.start()

    def saved(name):
        for copy in saves.pop(name, ()):
            copy.wait()

    def mixer(l):
        group = Group(place, r, rows, 0)
        h_all = r.h_mixer.at[l]
        xhat, _ = normalized(r.values[l])
        h_all[group.at(0)] = (xhat * r.gains[l : l + 1]).astype(BF)
        group.gather_start(h_all)
        if l == 0:
            mixer_weights[0].forward((0,))
        mixer_weights[l].ready((0,))
        saved("mixer")

        def project(which, chunk=None):
            at = group.at(which, chunk)
            h = h_all[at]
            for s in range(3):
                proj = nn_dot(h, r.w_in[l, s])
                r.padded[s, pl.ds(pl.multiple_of(at.start + PAD, 8), at.size)] = proj
                r.mix[PROJ + s, at] = proj.astype(BF)

        project(0)
        group.gather_peer(h_all)
        project(2)
        for chunk in range(CHUNKS):
            group.gather_near(h_all, chunk)
            project(1, chunk)
            group.gather_diagonal(h_all, chunk)
            project(3, chunk)

        if l == 0:
            mixer_weights[0].forward(rest)
            ffn_weights[0].start()
        for t in range(tiles):
            at = pl.ds(t * size, size)
            prev = r.masks[at, 0:1]
            following = r.masks[at, 1:2]
            shorts = []
            for s in range(3):
                shorts.append(
                    tap(l, 0, s) * shifted(r.padded, s, t, size, -1) * prev
                    + tap(l, 1, s) * shifted(r.padded, s, t, size, 0)
                    + tap(l, 2, s) * shifted(r.padded, s, t, size, 1) * following
                )
            r.mix[QUERY, at] = shorts[0].astype(BF)
            r.both[at, 0:lanes] = shorts[1].astype(BF)
            r.both[at, wide : wide + lanes] = shorts[2].astype(BF)
        mixer_weights[l].ready(rest)
        mlp_tables(r, l)
        if l == 0:
            for copy in tables:
                copy.wait()

        @pl.loop(0, tiles)
        def _(t):
            at = aligned(t, size)
            real = nn_dot(r.cos[at], r.both[...])
            imag = nn_dot(r.sin[at], r.both[...])
            value_re, cond_re = real[:, :lanes], real[:, wide : wide + lanes].astype(BF)
            value_im, cond_im = imag[:, :lanes], imag[:, wide : wide + lanes].astype(BF)
            pre = nn_dot(cond_re, r.in_re[...]) + nn_dot(cond_im, r.in_im[...])
            inner = (pre * normal_cdf(pre)).astype(BF)
            kernel_re = r.w_spec[l, 0, at] + nt_dot(inner, r.out_re[...])
            kernel_im = r.w_spec[l, 1, at] + nt_dot(inner, r.out_im[...])
            r.prod_re[at] = (value_re * kernel_re - value_im * kernel_im).astype(BF)
            r.prod_im[at] = (value_re * kernel_im + value_im * kernel_re).astype(BF)
            r.pre[at] = pre.astype(BF)
            for i, x in enumerate((value_re, value_im, kernel_re, kernel_im, cond_re, cond_im)):
                r.mix[SPECTRA + i, at] = x.astype(BF)

        ffn_weights[l].forward()
        if l + 1 < layers:
            mixer_weights[l + 1].start()

        def project_out(which):
            at = group.at(which)
            mixed = nn_dot(r.cos[at], r.prod_re[...]) + nn_dot(r.sin[at], r.prod_im[...])
            r.mix[MIXED, at] = mixed.astype(BF)
            gated = (r.mix[QUERY, at].astype(F32) * mixed).astype(BF)
            return nn_dot(gated, r.w_out[l])

        group.reduce_whole("diagonal", project_out(3))
        group.reduce_whole("near", project_out(1))
        group.reduce_whole("peer", project_out(2))
        r.mids[l] = r.values[l] + project_out(0)
        save("mixer", (0, r.mix, r.s_mix.at[l]), (1, r.pre, r.s_pre.at[l]), (2, h_all, r.s_h_mixer.at[l]))
        for chunk in range(CHUNKS):
            r.mids[l, group.piece(chunk)] += group.reduce_end(chunk)
        group.finish()

    def ffn(l):
        group = Group(place, r, rows, 1)
        h_all = r.h_ffn.at[l]
        xhat, _ = normalized(r.mids[l])
        h_all[group.at(0)] = (xhat * r.gains[layers + l : layers + l + 1]).astype(BF)
        group.gather_start(h_all)
        ffn_weights[l].ready()
        saved("ffn")

        def block(at):
            h = h_all[at]
            gate = nn_dot(h, r.w_gate[l])
            up = nn_dot(h, r.w_up[l])
            r.units[0, at] = gate.astype(BF)
            r.units[1, at] = up.astype(BF)
            hidden = (gate * normal_cdf(gate) * up).astype(BF)
            return nn_dot(hidden, r.w_down[l])

        r.values[l + 1] = r.mids[l] + block(group.at(0))
        group.gather_peer(h_all)
        group.reduce_whole("peer", block(group.at(2)))
        if l + 1 == layers:
            cotangent.start()
        for chunk in range(CHUNKS):
            group.gather_near(h_all, chunk)
            r.near_part[group.piece(chunk)] = block(group.at(1, chunk))
            group.gather_diagonal(h_all, chunk)
            group.reduce_peer(1, chunk, block(group.at(3, chunk)))
            group.reduce_near(chunk, r.near_part[group.piece(chunk)])
        if l + 1 < layers:
            mixer_weights[l + 1].forward()
            ffn_weights[l + 1].start()
        save("ffn", (3, r.units, r.s_units.at[l]), (4, h_all, r.s_h_ffn.at[l]))
        for chunk in range(CHUNKS):
            r.values[l + 1, group.piece(chunk)] += group.reduce_end(chunk)
        group.finish()

    cotangent = Exchange(place, r, r.cotangent, r.cot_pieces, "cot")
    for l in range(layers):
        mixer(l)
        ffn(l)
    kept = []
    for i, name in enumerate(list(MIXER.values()) + list(FFN.values())):
        if name != "w_spec":
            kept.append(
                pltpu.make_async_copy(getattr(r, name), getattr(r, name + "_out"), r.keep_sem.at[i])
            )
    for copy in kept:
        copy.start()
    cotangent.finish()
    r.carried[...] = jnp.concatenate([r.cot_pieces[j] for j in range(4)], 1).astype(F32)
    for l in range(layers):
        mixer_weights[l].finish()
        ffn_weights[l].finish()
    saved("mixer")
    saved("ffn")
    for copy in kept:
        copy.wait()


def forward(arrays, stream, cotangent, seg, small, taps, tables):
    length, shard = stream.shape
    layers, _, width, lanes = arrays["in_proj"].shape
    rows = length // 4
    units = arrays["gate_proj"].shape[2]
    groups, _, inner = arrays["cond_in"].shape[1:]
    inner *= groups
    wide = -(-lanes // 128) * 128
    gains = small.shape[0]
    held = {to: pltpu.VMEM(arrays[n].shape, arrays[n].dtype) for n, to in {**MIXER, **FFN}.items()}
    kept = {
        to + "_out": (arrays[n].shape, arrays[n].dtype)
        for n, to in {**MIXER, **FFN}.items()
        if to != "w_spec"
    }
    saves = dict(
        s_mix=((layers, MIX_ROWS, length, lanes), BF),
        s_pre=((layers, length, inner), BF),
        s_h_mixer=((layers, length, width), BF),
        s_units=((layers, 2, length, units), BF),
        s_h_ffn=((layers, length, width), BF),
    )

    def semaphores(kind, count):
        return {
            f"{kind}_send": pltpu.SemaphoreType.DMA((layers, count, 7)),
            f"{kind}_recv": pltpu.SemaphoreType.DMA((layers, count, 8)),
            f"{kind}_local": pltpu.SemaphoreType.DMA((layers, count)),
        }

    return call_kernel(
        forward_body,
        dict(
            stream=stream, cotangent=cotangent, seg=seg, small=small, taps=taps,
            cosine=tables[0], sine=tables[1], **arrays,
        ),
        dict(
            values=((layers + 1, rows, width), F32),
            mids=((layers, rows, width), F32),
            carried=((rows, width), F32),
            gains=((gains, width), F32),
            taps_out=(taps.shape, F32),
            masks=((length, 2), F32),
            **saves,
            **kept,
        ),
        dict(
            pieces=pltpu.VMEM((4, rows, shard), BF),
            cot_pieces=pltpu.VMEM((4, rows, shard), BF),
            gain_parts=pltpu.VMEM((4, gains, shard), F32),
            gain_send=pltpu.SemaphoreType.DMA((6,)),
            gain_recv=pltpu.SemaphoreType.DMA((6,)),
            table_sem=pltpu.SemaphoreType.DMA((2,)),
            save_sem=pltpu.SemaphoreType.DMA((5,)),
            keep_sem=pltpu.SemaphoreType.DMA((8,)),
            seg_got=pltpu.VMEM((length, 1), jnp.int32),
            taps_got=pltpu.VMEM(taps.shape, F32),
            edges=pltpu.VMEM((length + 2 * PAD, 1), jnp.int32),
            cos=pltpu.VMEM((length, length), BF),
            sin=pltpu.VMEM((length, length), BF),
            h_mixer=pltpu.VMEM((layers, length, width), BF),
            h_ffn=pltpu.VMEM((layers, length, width), BF),
            mix=pltpu.VMEM((MIX_ROWS, length, lanes), BF),
            pre=pltpu.VMEM((length, inner), BF),
            units=pltpu.VMEM((2, length, units), BF),
            near_part=pltpu.VMEM((rows, width), F32),
            padded=pltpu.VMEM((3, length + 2 * PAD, lanes), F32),
            both=pltpu.VMEM((length, 2 * wide), BF),
            prod_re=pltpu.VMEM((length, lanes), BF),
            prod_im=pltpu.VMEM((length, lanes), BF),
            **held,
            **semaphores("mw", 5),
            **semaphores("fw", 3),
            **mlp_scratch(lanes, inner),
            **Group.scratch(rows, width, 2),
            **Exchange.scratch(),
            **Exchange.scratch("cot"),
        ),
        1,
        30 * 10**9,
        ("stream", "cotangent", "cosine", "sine") + tuple(arrays) + tuple(saves) + tuple(kept),
    )


GRADS = ("proj", "spec", "mlp", "small")
SMALL_ROWS = 32


def of(r, prefix):
    return [getattr(r, prefix + n) for n in GRADS]


def backward_body(r):
    place = Place()
    layers, rows, width = r.mids.shape
    length = r.m_all.shape[0]
    lanes = r.w_in.shape[3]
    groups, feats, inner = r.w_ci.shape[1:]
    units = r.units.shape[2]
    half = feats // 2
    wide = 256 * (-(-lanes // 256))
    tiles = 4
    size = length // tiles
    w_gate, w_up, w_down = [r.w_ffn.at[pl.ds(i * width, width)] for i in range(3)]
    hidden_all, gate_grads, up_grads = [r.work.at[i] for i in range(3)]
    both_re, both_im = [r.work.at[i, :, pl.ds(0, 2 * wide)] for i in range(2)]
    q_g = r.work.at[2, :, pl.ds(0, wide)]
    proj_grads = [r.work.at[i, :, pl.ds(2 * wide, wide)] for i in range(3)]

    hidden = groups * inner
    sum_in, sum_out = [
        [held.at[pl.ds(0, lanes), pl.ds(i * hidden, hidden)] for i in range(2)]
        for held in (r.near_part, r.own_part)
    ]

    def load_ffn(l):
        load = Load(
            r,
            [
                (r.w_gate_out.at[l], w_gate),
                (r.w_up_out.at[l], w_up),
                (r.w_down_out.at[l], w_down),
                (r.s_units.at[l], r.units),
            ],
        )
        load.start()
        return load

    def load_mixer(l):
        load = Load(
            r,
            [
                (r.w_out_out.at[l], r.w_out.at[0]),
                (r.w_ci_out.at[l], r.w_ci.at[0]),
                (r.w_co_out.at[l], r.w_co.at[0]),
                (r.s_mix.at[l], r.mix),
                (r.s_pre.at[l], r.pre_all),
                (r.w_in_out.at[l], r.w_in.at[0]),
            ],
            6,
        )
        load.start()
        return load

    def load_rows(rows_of, h_of):
        load = Load(r, [(rows_of, r.row_in), (h_of, r.h_all)], 12)
        load.start()
        return load

    first = Load(
        r,
        [
            (r.values.at[layers], r.near_part),
            (r.carried, r.grad),
            (r.cosine, r.cos),
            (r.sine, r.sin),
        ],
        14,
    )
    first.start()
    pending = {"ffn": load_ffn(layers - 1), "mixer": load_mixer(layers - 1)}

    ffn_scatter = [Scatter(place, r, [r.weight_grads], [r.ffn_total], "fs", l) for l in range(layers)]
    mix_scatter = [Scatter(place, r, of(r, "g_"), of(r, "u_"), "ms", l) for l in range(layers)]
    freed = [
        r.weight_grads.at[pl.ds(0, 4 * lanes)],
        r.units.at[0, :, pl.ds(0, 2 * lanes)],
        r.units.at[1, pl.ds(0, 2 * groups * feats), pl.ds(0, inner)],
        r.units.at[1, pl.ds(0, 256), pl.ds(inner, 128)],
    ]
    ffn_spread, mix_spread = [], []
    for l in range(layers):
        ffn_to = r.r_ffn.at[l] if l else r.w_ffn
        mix_to = [o.at[l] for o in of(r, "r_")] if l else freed
        ffn_spread.append(Spread(place, r, [r.ffn_total], [ffn_to], "fp", l))
        mix_spread.append(Spread(place, r, of(r, "u_"), mix_to, "mp", l))

    shard = r.leaving.shape[2]
    output = Return(place, r, r.leaving, r.output, 0)
    stream_grad = Return(place, r, r.leaving, r.stream_grad, 1)

    def leave(x):
        for j in range(4):
            r.leaving[j] = x[:, j * shard : (j + 1) * shard].astype(BF)

    for s in range(3):
        r.padded[s, 0:PAD] = jnp.zeros((PAD, lanes), F32)
        r.padded[s, PAD + length : 2 * PAD + length] = jnp.zeros((PAD, lanes), F32)
    place.barrier()

    def ffn(l):
        top = l + 1 == layers
        group = Group(place, r, rows, 1)
        load = load_rows(r.mids.at[l], r.s_h_ffn.at[l])
        gain = r.gains[layers + l : layers + l + 1]
        if top:
            first.finish((0, 1))
        r.g_all[group.at(0)] = r.grad[...].astype(BF)
        group.gather_start(r.g_all)
        if top:
            leave(r.near_part[...])
            output.start()
        pending["ffn"].finish()
        if not top:
            pending["mixer"] = load_mixer(l)

        def block(at):
            hidden_grad = nt_dot(r.g_all[at], w_down[...])
            gate = r.units[0, at].astype(F32)
            up = r.units[1, at].astype(F32)
            cdf = normal_cdf(gate)
            act = gate * cdf
            hidden_all[at] = (act * up).astype(BF)
            gate_grad = (hidden_grad * up * (cdf + gate * normal_pdf(gate))).astype(BF)
            up_grad = (hidden_grad * act).astype(BF)
            gate_grads[at] = gate_grad
            up_grads[at] = up_grad
            return nt_dot(gate_grad, w_gate[...]) + nt_dot(up_grad, w_up[...])

        r.own_part[...] = block(group.at(0))
        group.gather_peer(r.g_all)
        group.reduce_whole("peer", block(group.at(2)))
        if not top:
            ffn_scatter[l + 1].finish()
            ffn_spread[l + 1].start()
        for chunk in range(CHUNKS):
            group.gather_near(r.g_all, chunk)
            r.near_part[group.piece(chunk)] = block(group.at(1, chunk))
            group.gather_diagonal(r.g_all, chunk)
            group.reduce_peer(1, chunk, block(group.at(3, chunk)))
            group.reduce_near(chunk, r.near_part[group.piece(chunk)])
        load.finish()
        step = 256
        for u in range(units // step):
            cols = pl.ds(u * step, step)
            r.weight_grads[0 * width : 1 * width, cols] = tn_dot(r.h_all[...], gate_grads[:, cols]).astype(BF)
            r.weight_grads[1 * width : 2 * width, cols] = tn_dot(r.h_all[...], up_grads[:, cols]).astype(BF)
            r.weight_grads[pl.ds(2 * width + u * step, step)] = tn_dot(hidden_all[:, cols], r.g_all[...]).astype(BF)
        if not top:
            mix_scatter[l + 1].second()
        ffn_scatter[l].start()
        for chunk in range(CHUNKS):
            r.own_part[group.piece(chunk)] += group.reduce_end(chunk)
        grad, gain_part = norm_grad_rows(r.own_part[...], r.row_in[...], gain)
        r.grad[...] += grad
        r.gain_two[...] = gain_part
        group.finish()
        if not top:
            mix_scatter[l + 1].middle()

    def mixer(l):
        top, bottom = l + 1 == layers, l == 0
        group = Group(place, r, rows, 0)
        load = load_rows(r.values.at[l], r.s_h_mixer.at[l])
        r.m_all[group.at(0)] = r.grad[...].astype(BF)
        group.gather_start(r.m_all)
        if not bottom:
            pending["ffn"] = load_ffn(l - 1)
        for i in range(2):
            r.work[i, :, 0 : 2 * wide] = jnp.zeros((length, 2 * wide), BF)
        r.near_part[...] = jnp.zeros_like(r.near_part)
        r.own_part[...] = jnp.zeros_like(r.own_part)
        pending["mixer"].finish()
        mlp_tables(r, 0)

        def gated_back(which, chunk=None):
            at = group.at(which, chunk)
            gated_grad = nt_dot(r.m_all[at], r.w_out[0])
            to = pl.ds(pl.multiple_of(at.start + PAD, 8), at.size)
            r.padded[0, to] = gated_grad * r.mix[MIXED, at].astype(F32)
            q_g[at, 0:lanes] = (gated_grad * r.mix[QUERY, at].astype(F32)).astype(BF)

        gated_back(0)
        group.gather_peer(r.m_all)
        gated_back(2)
        for chunk in range(CHUNKS):
            group.gather_near(r.m_all, chunk)
            gated_back(1, chunk)
            group.gather_diagonal(r.m_all, chunk)
            gated_back(3, chunk)
        if top:
            first.finish((2, 3))
        else:
            mix_scatter[l + 1].finish()
            mix_spread[l + 1].start()
            ffn_spread[l + 1].forward()

        @pl.loop(0, tiles)
        def _(t):
            at = aligned(t, size)
            real = nn_dot(r.cos[at], q_g[:, 0:lanes])
            imag = nn_dot(r.sin[at], q_g[:, 0:lanes])
            value_re, value_im, kernel_re, kernel_im = [
                r.mix[SPECTRA + i, at].astype(F32) for i in range(4)
            ]
            kernel_re_grad = real * value_re + imag * value_im
            kernel_im_grad = imag * value_re - real * value_im
            both_re[at, 0:lanes] = (real * kernel_re + imag * kernel_im).astype(BF)
            both_im[at, 0:lanes] = (imag * kernel_re - real * kernel_im).astype(BF)
            r.g_spec[at] = jnp.concatenate([kernel_re_grad, kernel_im_grad], 1).astype(BF)
            kernel_re_grad = kernel_re_grad.astype(BF)
            kernel_im_grad = kernel_im_grad.astype(BF)
            pre = r.pre_all[at].astype(F32)
            cdf = normal_cdf(pre)
            act = (pre * cdf).astype(BF)
            inner_grad = nn_dot(kernel_re_grad, r.out_re[...]) + nn_dot(kernel_im_grad, r.out_im[...])
            pre_grad = (inner_grad * (cdf + pre * normal_pdf(pre))).astype(BF)
            both_re[at, wide : wide + lanes] = nt_dot(pre_grad, r.in_re[...]).astype(BF)
            both_im[at, wide : wide + lanes] = nt_dot(pre_grad, r.in_im[...]).astype(BF)
            sum_out[0][...] += tn_dot(kernel_re_grad, act)
            sum_out[1][...] += tn_dot(kernel_im_grad, act)
            sum_in[0][...] += tn_dot(r.mix[SPECTRA + 4, at], pre_grad)
            sum_in[1][...] += tn_dot(r.mix[SPECTRA + 5, at], pre_grad)

        for g in range(groups):
            rows_at, cols = slice(g * half, (g + 1) * half), slice(g * inner, (g + 1) * inner)
            at = g * feats
            r.g_mlp[at : at + half] = sum_in[0][rows_at, cols].astype(BF)
            r.g_mlp[at + half : at + feats] = sum_in[1][rows_at, cols].astype(BF)
            turned = jnp.concatenate([sum_out[0][rows_at, cols], sum_out[1][rows_at, cols]], 0)
            at += groups * feats
            r.g_mlp[at : at + inner] = turned.T.astype(BF)
        ffn_scatter[l].second()
        mix_scatter[l].start((1, 2))

        @pl.loop(0, tiles)
        def _(t):
            at = aligned(t, size)
            both = nn_dot(r.cos[at], both_re[...]) + nn_dot(r.sin[at], both_im[...])
            to = pl.ds(pl.multiple_of(t * size + PAD, 8), size)
            r.padded[1, to] = both[:, :lanes]
            r.padded[2, to] = both[:, wide : wide + lanes]

        def tap(o, s):
            at = 9 * l + 3 * o + s
            return r.taps_out[at : at + 1]

        totals = [[None] * 3 for _ in range(3)]
        for t in range(tiles):
            at = pl.ds(t * size, size)
            prev = r.masks[at, 0:1]
            following = r.masks[at, 1:2]
            for s in range(3):
                here = shifted(r.padded, s, t, size, 0)
                after = shifted(r.padded, s, t, size, 1) * following
                before = shifted(r.padded, s, t, size, -1) * prev
                proj_grads[s][at, 0:lanes] = (
                    tap(0, s) * after + tap(1, s) * here + tap(2, s) * before
                ).astype(BF)
                proj = r.mix[PROJ + s, at].astype(F32)
                for o, g in enumerate((after, here, before)):
                    part = jnp.sum(g * proj, 0, keepdims=True)
                    totals[o][s] = part if t == 0 else totals[o][s] + part

        def feats_grad(which):
            at = group.at(which)
            return sum(nt_dot(proj_grads[s][at, 0:lanes], r.w_in[0, s]) for s in range(3))

        group.reduce_whole("diagonal", feats_grad(3))
        group.reduce_whole("near", feats_grad(1))
        group.reduce_whole("peer", feats_grad(2))
        load.finish()
        for s in range(3):
            r.g_proj[s * lanes : (s + 1) * lanes] = tn_dot(proj_grads[s][:, 0:lanes], r.h_all[...]).astype(BF)
        q_g[:, 0:lanes] = (r.mix[QUERY].astype(F32) * r.mix[MIXED].astype(F32)).astype(BF)
        r.g_proj[3 * lanes :] = tn_dot(q_g[:, 0:lanes], r.m_all[...]).astype(BF)
        mix_scatter[l].start((0,))
        ffn_scatter[l].middle()
        if bottom:
            mix_scatter[l].second((1, 2))
        if not top:
            mix_spread[l + 1].forward()
        r.own_part[...] = feats_grad(0)
        for chunk in range(CHUNKS):
            r.own_part[group.piece(chunk)] += group.reduce_end(chunk)
        grad, gain_part = norm_grad_rows(r.own_part[...], r.row_in[...], r.gains[l : l + 1])
        if bottom:
            output.finish()
            leave(r.grad[...] + grad)
            stream_grad.start()
        else:
            r.grad[...] += grad
        r.small_rows[...] = jnp.zeros_like(r.small_rows)
        small = [totals[o][s] for o in range(3) for s in range(3)] + [gain_part, r.gain_two[...]]
        at = 0
        for x in small:
            for start in range(0, x.shape[1], 128):
                part = x[:, start : start + 128]
                r.small_rows[at : at + 1, 0 : part.shape[1]] = part
                at += 1
        r.g_small[...] = jnp.zeros_like(r.g_small)
        r.g_small[0:SMALL_ROWS] = r.small_rows[...].astype(BF)
        mix_scatter[l].start((3,))
        group.finish()
        if not top:
            ffn_spread[l + 1].finish()
            mix_spread[l + 1].finish()

    for l in reversed(range(layers)):
        ffn(l)
        mixer(l)
    above = [
        pltpu.make_async_copy(
            r.r_small.at[l, pl.ds(0, SMALL_ROWS)], r.gain_parts.at[0, l], r.end_sem.at[l]
        )
        for l in range(1, layers)
    ]
    for copy in above:
        copy.start()
    ffn_scatter[0].finish()
    ffn_spread[0].start()
    mix_scatter[0].middle((1, 2))
    mix_scatter[0].second((0, 3))
    mix_scatter[0].finish((1, 2))
    mix_spread[0].start((1, 2))
    mix_scatter[0].middle((0, 3))
    ffn_spread[0].forward()
    mix_scatter[0].finish((0, 3))
    mix_spread[0].start((0, 3))
    mix_spread[0].forward((1, 2))
    stream_grad.finish()
    ffn_spread[0].finish()
    ends = [pltpu.make_async_copy(r.w_ffn, r.r_ffn.at[0], r.end_sem.at[0])]
    ends[0].start()
    mix_spread[0].forward((3, 0))
    mix_spread[0].finish((3,))
    r.gain_parts[0, 0] = freed[3][0:SMALL_ROWS, :]
    for copy in above:
        copy.wait()

    def gain_copy(j):
        chan = lax.rem(place.chan + j, 4)
        return remote(
            r.gain_parts.at[0], r.gain_parts.at[j], r.gain_send.at[j], r.gain_recv.at[j], {"chan": chan}
        )

    for j in range(1, 4):
        gain_copy(j).start()
    mix_spread[0].finish((1, 2, 0))
    for a, n in enumerate(GRADS):
        ends.append(
            pltpu.make_async_copy(
                freed[a], getattr(r, "r_" + n).at[0], r.end_sem.at[layers + a]
            )
        )
        ends[-1].start()
    for j in range(1, 4):
        gain_copy(j).wait()
    total = r.gain_parts[0].astype(F32)
    for j in range(1, 4):
        total += r.gain_parts[j].astype(F32)
    r.gain_grads[...] = total
    for copy in ends:
        copy.wait()


def backward(fwd, tables):
    layers, rows, width = fwd.mids.shape
    units = fwd.w_gate_out.shape[2]
    _, _, length, lanes = fwd.s_mix.shape
    groups, feats, inner = fwd.w_ci_out.shape[1:]
    hidden = groups * inner
    held = (
        "w_gate_out", "w_up_out", "w_down_out", "s_units", "s_h_ffn", "mids", "values", "carried",
        "w_out_out", "w_ci_out", "w_co_out", "s_mix", "s_pre", "w_in_out", "s_h_mixer",
    )
    near = ("gains", "taps_out", "masks")
    ins = dict(cosine=tables[0], sine=tables[1], **{n: getattr(fwd, n) for n in held + near})
    grads = dict(
        proj=(4 * lanes, width),
        spec=(length, 2 * lanes),
        mlp=(2 * groups * feats, inner),
        small=(256, 128),
    )
    ffn_shape = (3 * width, units)
    outs = dict(
        output=((length, lanes), BF),
        stream_grad=((length, lanes), BF),
        r_ffn=((layers,) + ffn_shape, BF),
        **{"r_" + n: ((layers,) + g, BF) for n, g in grads.items()},
    )
    hbm = held + ("cosine", "sine") + tuple(outs)
    outs.update(gain_grads=((layers, SMALL_ROWS, 128), F32))
    row = pltpu.VMEM((rows, width), F32)
    return call_kernel(
        backward_body,
        ins,
        outs,
        dict(
            grad=row,
            own_part=row,
            near_part=row,
            row_in=row,
            leaving=pltpu.VMEM((4, rows, lanes), BF),
            gain_two=pltpu.VMEM((1, width), F32),
            g_all=pltpu.VMEM((length, width), BF),
            m_all=pltpu.VMEM((length, width), BF),
            work=pltpu.VMEM((3, length, width), BF),
            w_ffn=pltpu.VMEM(ffn_shape, BF),
            weight_grads=pltpu.VMEM(ffn_shape, BF),
            units=pltpu.VMEM((2, length, units), BF),
            ffn_total=pltpu.VMEM((ffn_shape[0] // 8, ffn_shape[1]), BF),
            h_all=pltpu.VMEM((length, width), BF),
            mix=pltpu.VMEM((MIX_ROWS, length, lanes), BF),
            pre_all=pltpu.VMEM((length, hidden), BF),
            w_in=pltpu.VMEM((1,) + fwd.w_in_out.shape[1:], BF),
            w_out=pltpu.VMEM((1,) + fwd.w_out_out.shape[1:], BF),
            w_ci=pltpu.VMEM((1,) + fwd.w_ci_out.shape[1:], F32),
            w_co=pltpu.VMEM((1,) + fwd.w_co_out.shape[1:], F32),
            cos=pltpu.VMEM((length, length), BF),
            sin=pltpu.VMEM((length, length), BF),
            padded=pltpu.VMEM((3, length + 2 * PAD, lanes), F32),
            small_rows=pltpu.VMEM((SMALL_ROWS, 128), F32),
            gain_parts=pltpu.VMEM((4, layers, SMALL_ROWS, 128), BF),
            gain_send=pltpu.SemaphoreType.DMA((4,)),
            gain_recv=pltpu.SemaphoreType.DMA((4,)),
            load_sem=pltpu.SemaphoreType.DMA((18,)),
            end_sem=pltpu.SemaphoreType.DMA((layers + len(GRADS),)),
            **{"g_" + n: pltpu.VMEM(g, BF) for n, g in grads.items()},
            **{"u_" + n: pltpu.VMEM((g[0] // 8, g[1]), BF) for n, g in grads.items()},
            **mlp_scratch(lanes, hidden),
            **Group.scratch(rows, width, 2),
            **Return.scratch(),
            **Scatter.scratch([ffn_shape], "fs", layers),
            **Scatter.scratch(list(grads.values()), "ms", layers),
            **Spread.scratch(1, "fp", layers),
            **Spread.scratch(len(GRADS), "mp", layers),
        ),
        2,
        40 * 10**9,
        hbm,
    )


def on_device(
    stream,
    segments,
    cotangent,
    norm_one,
    in_proj,
    short_taps,
    cond_in,
    cond_out,
    filter_spec,
    out_proj,
    norm_two,
    gate_proj,
    up_proj,
    down_proj,
):
    chan = lax.axis_index("chan")
    layers, width = in_proj.shape[:2]
    shard = norm_one.shape[1]
    length = filter_spec.shape[2]
    groups, feats = cond_in.shape[1:3]
    tables = dft_tables(length)
    arrays = dict(
        in_proj=in_proj.transpose(0, 2, 1, 3),
        cond_in=cond_in,
        cond_out=cond_out,
        filter_spec=filter_spec,
        out_proj=out_proj,
        gate_proj=gate_proj,
        up_proj=up_proj,
        down_proj=down_proj,
    )

    fwd = forward(
        arrays,
        stream,
        cotangent,
        segments[:, None],
        jnp.concatenate([norm_one, norm_two], 0),
        short_taps.reshape(-1, shard),
        tables,
    )
    back = backward(fwd, tables)

    def everywhere(x):
        return lax.psum(x, "outer") if lax.axis_size("outer") > 1 else x

    def summed(name):
        return everywhere(getattr(back, name))

    gain_grads = summed("gain_grads")
    steps = -(-shard // 128)
    taps_rows, gain_rows = 9 * steps, width // 128

    def gain_stack(at):
        whole = gain_grads[:, at : at + gain_rows].reshape(layers, width)
        return lax.dynamic_slice_in_dim(whole, chan * shard, shard, 1)

    proj, spec, mlp = summed("r_proj"), summed("r_spec"), summed("r_mlp")
    small, ffn = summed("r_small"), summed("r_ffn")
    mlp_rows = groups * feats
    g_in = proj[:, : 3 * shard].reshape(layers, 3, shard, width).transpose(0, 3, 1, 2)
    g_taps = small[:, :taps_rows].reshape(layers, 9, steps * 128)[:, :, :shard]
    g_spec = jnp.stack([spec[:, :, :shard], spec[:, :, shard:]], 1)
    results = (
        back.output,
        back.stream_grad,
        gain_stack(taps_rows),
        g_in,
        g_taps.reshape(short_taps.shape),
        mlp[:, :mlp_rows].reshape(cond_in.shape),
        mlp[:, mlp_rows:].reshape(cond_out.shape),
        g_spec,
        proj[:, 3 * shard :],
        gain_stack(taps_rows + gain_rows),
        ffn[:, :width],
        ffn[:, width : 2 * width],
        ffn[:, 2 * width :],
    )
    return tuple(x.astype(F32) for x in results)


def solution(mesh):
    dp_count, chan_count = mesh.devices.shape
    fine = Mesh(
        mesh.devices.reshape(dp_count // 8, 4, 2, chan_count), ("outer", "col", "half", "chan")
    )
    dp = ("outer", "col", "half")
    weight_specs = (
        P(None, "chan"),
        P(None, None, None, "chan"),
        P(None, None, None, "chan"),
        P(None, "chan", None, None),
        P(None, "chan", None, None),
        P(None, None, None, "chan"),
        P(None, "chan", None),
        P(None, "chan"),
        P(None, None, "chan"),
        P(None, None, "chan"),
        P(None, "chan", None),
    )
    return jax.shard_map(
        on_device,
        mesh=fine,
        in_specs=(P(dp, "chan"), P(dp), P(dp, "chan")) + weight_specs,
        out_specs=(P(dp, "chan"), P(dp, "chan")) + weight_specs,
        check_vma=False,
    )
```

```python
import functools
import math
from types import SimpleNamespace

import jax
import jax.numpy as jnp
import numpy as np
from jax import lax
from jax.experimental import pallas as pl
from jax.experimental.pallas import tpu as pltpu
from jax.sharding import Mesh
from jax.sharding import PartitionSpec as P

EPSILON = 1e-05
BF = jnp.bfloat16
F32 = jnp.float32


def dft_tables(length):
    positions = np.arange(length)
    angles = (positions[:, None] * positions[None, :] % length) * (2.0 * math.pi / length)
    scale = 1.0 / math.sqrt(length)
    cosine = np.asarray(np.cos(angles) * scale, dtype=np.float32)
    sine = np.asarray(-np.sin(angles) * scale, dtype=np.float32)
    return jnp.asarray(cosine, BF), jnp.asarray(sine, BF)


def normal_cdf(x):
    return 0.5 * (1.0 + lax.erf(x * (2.0**-0.5)))


def normal_pdf(x):
    return jnp.exp(-0.5 * x * x) * (1.0 / math.sqrt(2.0 * math.pi))


MESH = pl.DeviceIdType.MESH
VMEM_LIMIT = 63 << 20
CHUNKS = 2
PARTS = 8


def nt_dot(a, b):
    return lax.dot_general(a, b, (((1,), (1,)), ((), ())), preferred_element_type=F32)


def tn_dot(a, b):
    return lax.dot_general(a, b, (((0,), (0,)), ((), ())), preferred_element_type=F32)


def nn_dot(a, b):
    return jnp.dot(a, b, preferred_element_type=F32)


def aligned(index, size):
    return pl.ds(pl.multiple_of(index * size, size), size)


class Place:
    def __init__(self):
        self.col = lax.axis_index("col")
        self.half = lax.axis_index("half")
        self.chan = lax.axis_index("chan")
        odd = lax.rem(self.chan, 2)
        self.pack = self.chan // 2
        self.own = self.half == self.pack
        self.other_half = 1 - self.half
        self.near_chan = self.chan + 1 - 2 * odd
        self.far_chan = self.chan + 2 - 4 * self.pack
        self.rank = 2 * self.half + odd
        flip_near, flip_peer = 1 - 2 * odd, 2 - 4 * self.half
        self.ranks = [
            self.rank,
            self.rank + flip_near,
            self.rank + flip_peer,
            self.rank + flip_near + flip_peer,
        ]

    def col_at(self, step):
        return lax.rem(self.col + step, 4)

    def barrier(self):
        sem = pltpu.get_barrier_semaphore()
        devices = [{"col": self.col_at(j)} for j in range(1, 4)]
        for i in range(1, 8):
            half = self.half if i < 4 else self.other_half
            devices.append({"half": half, "chan": lax.rem(self.chan + i, 4)})
        for device in devices:
            pl.semaphore_signal(sem, inc=1, device_id=device, device_id_type=MESH)
        pl.semaphore_wait(sem, len(devices))


def remote(src, dst, send_sem, recv_sem, device):
    return pltpu.make_async_remote_copy(
        src_ref=src,
        dst_ref=dst,
        send_sem=send_sem,
        recv_sem=recv_sem,
        device_id=device,
        device_id_type=MESH,
    )


def await_recv(ref, recv_sem, send_sem):
    remote(ref, ref, send_sem, recv_sem, {"half": 1 - lax.axis_index("half")}).wait_recv()


def await_send(ref, send_sem, recv_sem):
    remote(ref, ref, send_sem, recv_sem, {"half": 1 - lax.axis_index("half")}).wait_send()


class Group:
    def __init__(self, place, r, rows, turn=0):
        self.place = place
        self.near = {"chan": place.near_chan}
        self.peer = {"half": place.other_half}
        self.send, self.recv = r.group_send.at[turn], r.group_recv.at[turn]
        self.to_peer, self.from_peer = r.to_peer, r.from_peer.at[turn]
        self.to_near, self.from_near = r.to_near, r.from_near.at[turn]
        self.rows, self.size = rows, rows // CHUNKS
        self.started = []

    @staticmethod
    def scratch(rows, width, turns=1):
        return dict(
            group_send=pltpu.SemaphoreType.DMA((turns, 6, CHUNKS)),
            group_recv=pltpu.SemaphoreType.DMA((turns, 6, CHUNKS)),
            to_peer=pltpu.VMEM((2, rows, width), BF),
            from_peer=pltpu.VMEM((turns, 2, rows, width), BF),
            to_near=pltpu.VMEM((rows, width), BF),
            from_near=pltpu.VMEM((turns, rows, width), BF),
        )

    def at(self, which, chunk=None):
        start = self.place.ranks[which] * self.rows
        if chunk is None:
            return pl.ds(pl.multiple_of(start, self.rows), self.rows)
        return pl.ds(pl.multiple_of(start + chunk * self.size, self.size), self.size)

    def start(self, src, dst, kind, chunk, device):
        copy = remote(src, dst, self.send.at[kind, chunk], self.recv.at[kind, chunk], device)
        copy.start()
        self.started.append(copy)

    def arrived(self, ref, kind, chunk):
        await_recv(ref, self.recv.at[kind, chunk], self.send.at[kind, chunk])

    def gather_start(self, full):
        for chunk in range(CHUNKS):
            own = full.at[self.at(0, chunk)]
            self.start(own, own, 0, chunk, self.near)
        for chunk in range(CHUNKS):
            own = full.at[self.at(0, chunk)]
            self.start(own, own, 1, chunk, self.peer)

    def gather_peer(self, full):
        for chunk in range(CHUNKS):
            self.arrived(full.at[self.at(2, chunk)], 1, chunk)

    def gather_near(self, full, chunk):
        piece = full.at[self.at(1, chunk)]
        self.arrived(piece, 0, chunk)
        self.start(piece, piece, 2, chunk, self.peer)

    def gather_diagonal(self, full, chunk):
        self.arrived(full.at[self.at(3, chunk)], 2, chunk)

    def piece(self, chunk):
        return pl.ds(chunk * self.size, self.size)

    def reduce_peer(self, slot, chunk, value):
        at = self.piece(chunk)
        self.to_peer[slot, at] = value.astype(BF)
        self.start(self.to_peer.at[slot, at], self.from_peer.at[slot, at], 3 + slot, chunk, self.peer)

    def reduce_near(self, chunk, value):
        at = self.piece(chunk)
        self.arrived(self.from_peer.at[1, at], 4, chunk)
        self.to_near[at] = (value + self.from_peer[1, at].astype(F32)).astype(BF)
        self.start(self.to_near.at[at], self.from_near.at[at], 5, chunk, self.near)

    def reduce_end(self, chunk):
        at = self.piece(chunk)
        self.arrived(self.from_peer.at[0, at], 3, chunk)
        self.arrived(self.from_near.at[at], 5, chunk)
        return self.from_peer[0, at].astype(F32) + self.from_near[at].astype(F32)

    def reduce_whole(self, kind, part):
        for chunk in range(CHUNKS):
            value = part[chunk * self.size : (chunk + 1) * self.size]
            if kind == "near":
                self.reduce_near(chunk, value)
            else:
                self.reduce_peer({"peer": 0, "diagonal": 1}[kind], chunk, value)

    def finish(self):
        for copy in self.started:
            copy.wait_send()


class Weights:
    def __init__(self, place, sems, pairs):
        self.place, self.pairs = place, pairs
        self.send, self.recv, self.local = sems

    def cut(self, ref, axis, parts, index):
        at = aligned(index, ref.shape[axis] // parts)
        return ref.at[(slice(None),) * axis + (at,)]

    def index(self, parts, col, half):
        return col * 2 + half if parts == 8 else col

    def each(self, which):
        which = range(len(self.pairs)) if which is None else which
        return [(a, self.pairs[a]) for a in which]

    def each_sent(self, act, which=None):
        p = self.place
        owner = {"half": p.pack, "chan": p.far_chan}
        for a, (src, dst, axis, parts) in self.each(which):

            def send(a=a, src=src, dst=dst, axis=axis, parts=parts):
                index = self.index(parts, p.col, p.half)
                act(
                    remote(
                        self.cut(src, axis, parts, index),
                        self.cut(dst, axis, parts, index),
                        self.send.at[a, 0],
                        self.recv.at[a, p.half if parts == 8 else 0],
                        owner,
                    )
                )

            if parts == 8:
                send()
            else:
                pl.when(p.half == 0)(send)

    def start(self, which=None):
        self.each_sent(lambda c: c.start(), which)

        @pl.when(self.place.own)
        def _():
            for a, (src, dst, axis, parts) in self.each(which):
                pltpu.make_async_copy(src, dst, self.local.at[a]).start()

    def forward(self, which=None):
        p = self.place

        @pl.when(jnp.logical_not(p.own))
        def _():
            for a, (src, dst, axis, parts) in self.each(which):
                for s in range(parts // 4):
                    piece = self.cut(dst, axis, parts, self.index(parts, p.col, s))
                    await_recv(piece, self.recv.at[a, s], self.send.at[a, 0])
                    for j in range(1, 4):
                        remote(
                            piece,
                            piece,
                            self.send.at[a, 2 * j - 1 + s],
                            self.recv.at[a, 2 * j + s],
                            {"col": p.col_at(j)},
                        ).start()

    def ready(self, which=None):
        p = self.place

        @pl.when(p.own)
        def _():
            for a, (src, dst, axis, parts) in self.each(which):
                pltpu.make_async_copy(src, dst, self.local.at[a]).wait()

        @pl.when(jnp.logical_not(p.own))
        def _():
            for a, (src, dst, axis, parts) in self.each(which):
                for s in range(parts // 4):
                    for j in range(1, 4):
                        piece = self.cut(dst, axis, parts, self.index(parts, p.col_at(4 - j), s))
                        await_recv(piece, self.recv.at[a, 2 * j + s], self.send.at[a, 0])

    def finish(self):
        p = self.place
        self.each_sent(lambda c: c.wait_send())

        @pl.when(jnp.logical_not(p.own))
        def _():
            for a, (src, dst, axis, parts) in enumerate(self.pairs):
                for s in range(parts // 4):
                    for j in range(1, 4):
                        piece = self.cut(dst, axis, parts, self.index(parts, p.col_at(4 - j), s))
                        await_send(piece, self.send.at[a, 2 * j - 1 + s], self.recv.at[a, 0])


class Load:
    def __init__(self, r, pairs, first=0):
        self.copies = [
            pltpu.make_async_copy(src, dst, r.load_sem.at[first + a])
            for a, (src, dst) in enumerate(pairs)
        ]

    def start(self):
        for copy in self.copies:
            copy.start()

    def finish(self, which=None):
        for a in range(len(self.copies)) if which is None else which:
            self.copies[a].wait()


class Exchange:
    def __init__(self, place, r, src, dst, name="ex"):
        self.place, self.src, self.dst = place, src, dst
        self.send, self.recv, self.local = [
            getattr(r, f"{name}_{n}") for n in ("send", "recv", "local")
        ]
        self.size = src.shape[0] // 4

    @staticmethod
    def scratch(name="ex"):
        return {
            f"{name}_send": pltpu.SemaphoreType.DMA((4,)),
            f"{name}_recv": pltpu.SemaphoreType.DMA((4,)),
            f"{name}_local": pltpu.SemaphoreType.DMA,
        }

    def each(self, act, act_self):
        p = self.place
        for j in range(4):
            chan = 2 * p.half + j % 2
            mine = (p.half == j // 2) & (p.chan == chan)
            src, dst = self.src.at[pl.ds(j * self.size, self.size)], self.dst.at[p.chan]

            def go(j=j, chan=chan, src=src, dst=dst):
                act(
                    remote(
                        src, dst, self.send.at[j], self.recv.at[p.chan],
                        {"half": j // 2, "chan": chan},
                    )
                )

            def stay(src=src, dst=dst):
                act_self(pltpu.make_async_copy(src, dst, self.local))

            pl.when(jnp.logical_not(mine))(go)
            pl.when(mine)(stay)

    def start(self):
        self.each(lambda c: c.start(), lambda c: c.start())

    def finish(self):
        p = self.place
        self.each(lambda c: c.wait_send(), lambda c: c.wait())
        for j in range(4):

            def wait(j=j):
                await_recv(self.dst.at[j], self.recv.at[j], self.send.at[0])

            pl.when(jnp.logical_not(p.own & (p.chan == j)))(wait)


class Return:
    def __init__(self, place, r, src, dst, turn):
        self.place, self.src, self.dst = place, src, dst
        self.send, self.recv = r.back_send.at[turn], r.back_recv.at[turn]
        self.local = r.back_local.at[turn]
        self.size = src.shape[1]

    @staticmethod
    def scratch():
        return dict(
            back_send=pltpu.SemaphoreType.DMA((2, 4)),
            back_recv=pltpu.SemaphoreType.DMA((2, 4)),
            back_local=pltpu.SemaphoreType.DMA((2,)),
        )

    def each(self, act, act_self):
        p = self.place
        for j in range(4):
            mine = p.own & (p.chan == j)
            src, dst = self.src.at[j], self.dst.at[aligned(p.rank, self.size)]

            def go(j=j, src=src, dst=dst):
                act(
                    remote(
                        src, dst, self.send.at[j], self.recv.at[p.rank],
                        {"half": p.pack, "chan": j},
                    )
                )

            def stay(src=src, dst=dst):
                act_self(pltpu.make_async_copy(src, dst, self.local))

            pl.when(jnp.logical_not(mine))(go)
            pl.when(mine)(stay)

    def start(self):
        self.each(lambda c: c.start(), lambda c: c.start())

    def finish(self):
        p = self.place
        self.each(lambda c: c.wait_send(), lambda c: c.wait())
        for j in range(4):
            mine = (p.half == j // 2) & (p.chan == 2 * p.half + j % 2)

            def wait(j=j):
                await_recv(
                    self.dst.at[pl.ds(j * self.size, self.size)], self.recv.at[j], self.send.at[0]
                )

            pl.when(jnp.logical_not(mine))(wait)


class Scatter:
    def __init__(self, place, r, sources, totals, name, turn):
        self.place, self.sources, self.totals = place, sources, totals
        self.send, self.recv, self.local = [
            getattr(r, f"{name}_{n}").at[turn] for n in ("send", "recv", "local")
        ]
        self.kept, self.got, self.late, self.cross = [
            [getattr(r, f"{name}_{part}{a}") for a in range(len(sources))]
            for part in ("kept", "got", "late", "cross")
        ]
        self.cross = [c.at[turn] for c in self.cross]
        self.x = lax.rem(place.col, 2)
        self.y = place.col // 2
        self.to_x = {"col": place.col + 1 - 2 * self.x}
        self.to_y = {"col": lax.rem(place.col + 2, 4)}

    @staticmethod
    def scratch(shapes, name, turns):
        n = len(shapes)
        out = {
            f"{name}_send": pltpu.SemaphoreType.DMA((turns, n, 8)),
            f"{name}_recv": pltpu.SemaphoreType.DMA((turns, n, 8)),
            f"{name}_local": pltpu.SemaphoreType.DMA((turns, n, 4)),
        }
        for a, (rows, width) in enumerate(shapes):
            for part, count in (("kept", 4), ("got", 4), ("late", 2)):
                out[f"{name}_{part}{a}"] = pltpu.VMEM((count, rows // 8, width), BF)
            out[f"{name}_cross{a}"] = pltpu.VMEM((turns, 2, rows // 8, width), BF)
        return out

    def each(self, which):
        return range(len(self.sources)) if which is None else which

    def piece(self, a, y, x, half):
        src = self.sources[a]
        return src.at[aligned((2 * y + x) * 2 + half, src.shape[0] // 8)]

    def firsts(self, a):
        out = []
        for i in range(2):
            out.append((self.piece(a, i, 1 - self.x, 0), i, self.to_x))
            out.append((self.piece(a, 1 - self.y, i, 1), 2 + i, self.to_y))
        return [
            remote(src, self.got[a].at[k], self.send.at[a, k], self.recv.at[a, k], device)
            for src, k, device in out
        ]

    def keeps(self, a):
        out = []
        for i in range(2):
            out.append((self.piece(a, i, self.x, 0), i))
            out.append((self.piece(a, self.y, i, 1), 2 + i))
        return [
            pltpu.make_async_copy(src, self.kept[a].at[k], self.local.at[a, k]) for src, k in out
        ]

    def seconds(self, a):
        kept, late = self.kept[a], self.late[a]
        return [
            remote(kept.at[1 - self.y], late.at[0], self.send.at[a, 4], self.recv.at[a, 4], self.to_y),
            remote(kept.at[3 - self.x], late.at[1], self.send.at[a, 5], self.recv.at[a, 5], self.to_x),
        ]

    def summed(self, part):
        return self.y + part * (2 + self.x - self.y)

    def third(self, a, slot, part, half, chan):
        return remote(
            self.kept[a].at[self.summed(part)],
            self.cross[a].at[slot],
            self.send.at[a, 6 + slot],
            self.recv.at[a, 6 + slot],
            {"half": half, "chan": chan},
        )

    def start(self, which=None):
        for a in self.each(which):
            for copy in self.firsts(a) + self.keeps(a):
                copy.start()

    def second(self, which=None):
        for a in self.each(which):
            for copy in self.firsts(a) + self.keeps(a):
                copy.wait()
            for k in range(4):
                self.kept[a][k] = self.kept[a][k] + self.got[a][k]
            for copy in self.seconds(a):
                copy.start()

    def middle(self, which=None):
        p = self.place
        for a in self.each(which):
            for copy in self.seconds(a):
                copy.wait()
            kept, late = self.kept[a], self.late[a]
            for part in range(2):
                at = self.summed(part)
                kept[at] = kept[at] + late[part]

            @pl.when(p.own)
            def _():
                self.third(a, 0, p.other_half, p.other_half, p.chan).start()

            @pl.when(jnp.logical_not(p.own))
            def _():
                self.third(a, 0, p.half, p.half, p.far_chan).start()
                self.third(a, 1, p.other_half, p.other_half, p.far_chan).start()

    def finish(self, which=None):
        p = self.place
        for a in self.each(which):
            cross = self.cross[a]
            await_recv(cross.at[0], self.recv.at[a, 6], self.send.at[a, 6])
            await_send(cross.at[0], self.send.at[a, 6], self.recv.at[a, 6])

            @pl.when(p.own)
            def _():
                self.totals[a][...] = cross[0] + self.kept[a][self.summed(p.half)]

            @pl.when(jnp.logical_not(p.own))
            def _():
                await_recv(cross.at[1], self.recv.at[a, 7], self.send.at[a, 7])
                await_send(cross.at[1], self.send.at[a, 7], self.recv.at[a, 7])
                self.totals[a][...] = cross[0] + cross[1]


class Spread:
    def __init__(self, place, r, totals, results, name, turn):
        self.place, self.totals, self.results = place, totals, results
        self.send, self.recv, self.kept = [
            getattr(r, f"{name}_{n}").at[turn] for n in ("send", "recv", "local")
        ]

    @staticmethod
    def scratch(count, name, turns):
        return {
            f"{name}_send": pltpu.SemaphoreType.DMA((turns, count, 7)),
            f"{name}_recv": pltpu.SemaphoreType.DMA((turns, count, 7)),
            f"{name}_local": pltpu.SemaphoreType.DMA((turns, count)),
        }

    def each(self, which):
        return range(len(self.totals)) if which is None else which

    def slot(self, a, col, half):
        result = self.results[a]
        return result.at[aligned(col * 2 + half, result.shape[0] // 8)]

    def local(self, a):
        p = self.place
        return pltpu.make_async_copy(
            self.totals[a], self.slot(a, p.col, p.half), self.kept.at[a]
        )

    def out(self, a, j):
        p = self.place
        device = {"col": p.col_at(j)} if j else {"half": p.other_half}
        return remote(
            self.totals[a],
            self.slot(a, p.col, p.half),
            self.send.at[a, j],
            self.recv.at[a, j],
            device,
        )

    def pass_on(self, a, j):
        p = self.place
        piece = self.slot(a, p.col_at(4 - j), p.half)
        return remote(
            piece, piece, self.send.at[a, 3 + j], self.recv.at[a, 3 + j],
            {"half": p.other_half},
        )

    def start(self, which=None):
        for a in self.each(which):
            for j in (1, 2, 3, 0):
                self.out(a, j).start()
            self.local(a).start()

    def forward(self, which=None):
        p = self.place
        for a in self.each(which):
            for j in range(1, 4):
                piece = self.slot(a, p.col_at(4 - j), p.half)
                await_recv(piece, self.recv.at[a, j], self.send.at[a, j])
                self.pass_on(a, j).start()

    def finish(self, which=None):
        p = self.place
        for a in self.each(which):
            for j in range(4):
                self.out(a, j).wait_send()
            self.local(a).wait()
            await_recv(
                self.slot(a, p.col, p.other_half), self.recv.at[a, 0], self.send.at[a, 0]
            )
            for j in range(1, 4):
                self.pass_on(a, j).wait_send()
                piece = self.slot(a, p.col_at(4 - j), p.other_half)
                await_recv(piece, self.recv.at[a, 3 + j], self.send.at[a, 3 + j])


def call_kernel(body, ins, outs, scratch, collective_id, flops, hbm=()):
    names = list(ins) + list(outs) + list(scratch)

    def run(*refs):
        body(SimpleNamespace(**dict(zip(names, refs))))

    def spec(name):
        return pl.BlockSpec(memory_space=pl.ANY if name in hbm else pltpu.VMEM)

    results = pl.pallas_call(
        run,
        out_shape=[jax.ShapeDtypeStruct(*o) for o in outs.values()],
        in_specs=[spec(n) for n in ins],
        out_specs=[spec(n) for n in outs],
        scratch_shapes=list(scratch.values()),
        compiler_params=pltpu.CompilerParams(
            collective_id=collective_id, has_side_effects=True, vmem_limit_bytes=VMEM_LIMIT
        ),
        cost_estimate=pl.CostEstimate(flops=flops, bytes_accessed=20 << 20, transcendentals=0),
    )(*ins.values())
    return SimpleNamespace(**dict(zip(outs, results)))


def normalized(x):
    average = jnp.mean(x, 1, keepdims=True)
    centered = x - average
    variance = jnp.mean(centered * centered, 1, keepdims=True)
    inv = lax.rsqrt(variance + EPSILON)
    return centered * inv, inv


def norm_grad_rows(grad, x, gain):
    xhat, inv = normalized(x)
    gain_part = jnp.sum(grad * xhat, 0, keepdims=True)
    scaled = grad * gain
    mean_plain = jnp.mean(scaled, 1, keepdims=True)
    mean_cross = jnp.mean(scaled * xhat, 1, keepdims=True)
    return inv * (scaled - mean_plain - xhat * mean_cross), gain_part


PAD = 8


def shifted(ref, s, tile, size, offset):
    return ref[s, pl.ds(PAD + tile * size + offset, size)]


def mlp_tables(r, l):
    groups, feats, inner = r.w_ci.shape[1:]
    half = feats // 2
    for table in (r.in_re, r.in_im, r.out_re, r.out_im):
        table[...] = jnp.zeros_like(table)
    for g in range(groups):
        rows, cols = pl.ds(g * half, half), pl.ds(g * inner, inner)
        r.in_re[rows, cols] = r.w_ci[l, g, 0:half].astype(BF)
        r.in_im[rows, cols] = r.w_ci[l, g, half:feats].astype(BF)
        turned = r.w_co[l, g].T
        r.out_re[rows, cols] = turned[0:half].astype(BF)
        r.out_im[rows, cols] = turned[half:feats].astype(BF)


def mlp_scratch(shard, inner):
    table = pltpu.VMEM((shard, inner), BF)
    return dict(in_re=table, in_im=table, out_re=table, out_im=table)


MIXER = dict(in_proj="w_in", cond_in="w_ci", cond_out="w_co", out_proj="w_out", filter_spec="w_spec")
FFN = dict(gate_proj="w_gate", up_proj="w_up", down_proj="w_down")
CUTS = dict(in_proj=1, cond_in=1, cond_out=1, filter_spec=2, out_proj=0, gate_proj=0, up_proj=0, down_proj=0)
PROJ, QUERY, MIXED, SPECTRA, MIX_ROWS = 0, 3, 4, 5, 11


def forward_body(r):
    place = Place()
    layers, rows, width = r.mids.shape
    length = r.seg.shape[0]
    lanes = r.w_in.shape[3]
    wide = r.both.shape[1] // 2
    tiles = 4
    size = length // tiles
    exchange = Exchange(place, r, r.stream, r.pieces)
    tables = [
        pltpu.make_async_copy(r.cosine, r.cos, r.table_sem.at[0]),
        pltpu.make_async_copy(r.sine, r.sin, r.table_sem.at[1]),
    ]

    def weights(kind, names, l):
        sems = [getattr(r, f"{kind}_{n}").at[l] for n in ("send", "recv", "local")]
        pairs = [
            (getattr(r, n).at[l], getattr(r, to).at[l], CUTS[n], 4 if n == "out_proj" else 8)
            for n, to in names.items()
        ]
        return Weights(place, sems, pairs)

    rest = (1, 2, 3, 4)
    mixer_weights = [weights("mw", MIXER, l) for l in range(layers)]
    ffn_weights = [weights("fw", FFN, l) for l in range(layers)]
    place.barrier()
    exchange.start()
    own, other = place.own, jnp.logical_not(place.own)

    def gain_copy(j):
        chan = lax.rem(place.chan + j, 4)
        return remote(r.small, r.gain_parts.at[j], r.gain_send.at[j], r.gain_recv.at[j], {"chan": chan})

    for j in range(1, 4):
        gain_copy(j).start()
    seg_copy = remote(r.seg, r.seg_got, r.gain_send.at[4], r.gain_recv.at[4], {"half": place.other_half})
    taps_copy = remote(r.taps, r.taps_got, r.gain_send.at[5], r.gain_recv.at[5], {"chan": place.far_chan})

    @pl.when(own)
    def _():
        seg_copy.start()
        taps_copy.start()

    mixer_weights[0].start((0,))
    for copy in tables:
        copy.start()
    r.edges[0:PAD] = jnp.full((PAD, 1), -1, jnp.int32)
    r.edges[PAD + length : 2 * PAD + length] = jnp.full((PAD, 1), -1, jnp.int32)
    for s in range(3):
        r.padded[s, 0:PAD] = jnp.zeros((PAD, lanes), F32)
        r.padded[s, PAD + length : 2 * PAD + length] = jnp.zeros((PAD, lanes), F32)
    r.both[...] = jnp.zeros_like(r.both)

    @pl.when(own)
    def _():
        r.edges[PAD : PAD + length] = r.seg[...]
        r.taps_out[...] = r.taps[...]
        seg_copy.wait_send()
        taps_copy.wait_send()

    @pl.when(other)
    def _():
        seg_copy.wait_recv()
        taps_copy.wait_recv()
        r.edges[PAD : PAD + length] = r.seg_got[...]
        r.taps_out[...] = r.taps_got[...]

    here = r.edges[PAD : PAD + length]
    r.masks[:, 0:1] = jnp.where(r.edges[PAD - 1 : PAD - 1 + length] == here, 1.0, 0.0)
    r.masks[:, 1:2] = jnp.where(r.edges[PAD + 1 : PAD + 1 + length] == here, 1.0, 0.0)
    for j in range(1, 4):
        gain_copy(j).wait()
    r.gain_parts[0] = r.small[...]
    parts = []
    for c in range(4):
        parts.append(r.gain_parts[lax.rem(place.chan - c + 4, 4)])
    r.gains[...] = jnp.concatenate(parts, 1)
    exchange.finish()
    mixer_weights[0].start(rest)
    r.values[0] = jnp.concatenate([r.pieces[j] for j in range(4)], 1).astype(F32)

    def tap(l, o, s):
        at = 9 * l + 3 * o + s
        return r.taps_out[at : at + 1]

    saves = {}

    def save(name, *copies):
        saves[name] = [pltpu.make_async_copy(src, dst, r.save_sem.at[i]) for i, src, dst in copies]
        for copy in saves[name]:
            copy.start()

    def saved(name):
        for copy in saves.pop(name, ()):
            copy.wait()

    def mixer(l):
        group = Group(place, r, rows, 0)
        h_all = r.h_mixer.at[l]
        xhat, _ = normalized(r.values[l])
        h_all[group.at(0)] = (xhat * r.gains[l : l + 1]).astype(BF)
        group.gather_start(h_all)
        if l == 0:
            mixer_weights[0].forward((0,))
        mixer_weights[l].ready((0,))
        saved("mixer")

        def project(which, chunk=None):
            at = group.at(which, chunk)
            h = h_all[at]
            for s in range(3):
                proj = nn_dot(h, r.w_in[l, s])
                r.padded[s, pl.ds(pl.multiple_of(at.start + PAD, 8), at.size)] = proj
                r.mix[PROJ + s, at] = proj.astype(BF)

        project(0)
        if l == 0:
            ffn_weights[0].start()
        group.gather_peer(h_all)
        project(2)
        for chunk in range(CHUNKS):
            group.gather_near(h_all, chunk)
            project(1, chunk)
            group.gather_diagonal(h_all, chunk)
            project(3, chunk)

        if l == 0:
            mixer_weights[0].forward(rest)
        for t in range(tiles):
            at = pl.ds(t * size, size)
            prev = r.masks[at, 0:1]
            following = r.masks[at, 1:2]
            shorts = []
            for s in range(3):
                shorts.append(
                    tap(l, 0, s) * shifted(r.padded, s, t, size, -1) * prev
                    + tap(l, 1, s) * shifted(r.padded, s, t, size, 0)
                    + tap(l, 2, s) * shifted(r.padded, s, t, size, 1) * following
                )
            r.mix[QUERY, at] = shorts[0].astype(BF)
            r.both[at, 0:lanes] = shorts[1].astype(BF)
            r.both[at, wide : wide + lanes] = shorts[2].astype(BF)
        mixer_weights[l].ready(rest)
        mlp_tables(r, l)
        if l == 0:
            for copy in tables:
                copy.wait()

        @pl.loop(0, tiles)
        def _(t):
            at = aligned(t, size)
            real = nn_dot(r.cos[at], r.both[...])
            imag = nn_dot(r.sin[at], r.both[...])
            value_re, cond_re = real[:, :lanes], real[:, wide : wide + lanes].astype(BF)
            value_im, cond_im = imag[:, :lanes], imag[:, wide : wide + lanes].astype(BF)
            pre = nn_dot(cond_re, r.in_re[...]) + nn_dot(cond_im, r.in_im[...])
            inner = (pre * normal_cdf(pre)).astype(BF)
            kernel_re = r.w_spec[l, 0, :, at].T + nt_dot(inner, r.out_re[...])
            kernel_im = r.w_spec[l, 1, :, at].T + nt_dot(inner, r.out_im[...])
            r.prod_re[at] = (value_re * kernel_re - value_im * kernel_im).astype(BF)
            r.prod_im[at] = (value_re * kernel_im + value_im * kernel_re).astype(BF)
            r.pre[at] = pre.astype(BF)
            for i, x in enumerate((value_re, value_im, kernel_re, kernel_im, cond_re, cond_im)):
                r.mix[SPECTRA + i, at] = x.astype(BF)

        ffn_weights[l].forward()
        if l + 1 < layers:
            mixer_weights[l + 1].start()

        def project_out(which):
            at = group.at(which)
            mixed = nn_dot(r.cos[at], r.prod_re[...]) + nn_dot(r.sin[at], r.prod_im[...])
            r.mix[MIXED, at] = mixed.astype(BF)
            gated = (r.mix[QUERY, at].astype(F32) * mixed).astype(BF)
            return nn_dot(gated, r.w_out[l])

        group.reduce_whole("diagonal", project_out(3))
        group.reduce_whole("near", project_out(1))
        group.reduce_whole("peer", project_out(2))
        r.mids[l] = r.values[l] + project_out(0)
        save("mixer", (0, r.mix, r.s_mix.at[l]), (1, r.pre, r.s_pre.at[l]), (2, h_all, r.s_h_mixer.at[l]))
        for chunk in range(CHUNKS):
            r.mids[l, group.piece(chunk)] += group.reduce_end(chunk)
        group.finish()

    def ffn(l):
        group = Group(place, r, rows, 1)
        h_all = r.h_ffn.at[l]
        xhat, _ = normalized(r.mids[l])
        h_all[group.at(0)] = (xhat * r.gains[layers + l : layers + l + 1]).astype(BF)
        group.gather_start(h_all)
        ffn_weights[l].ready()
        saved("ffn")

        def block(at):
            h = h_all[at]
            gate = nn_dot(h, r.w_gate[l])
            up = nn_dot(h, r.w_up[l])
            r.units[0, at] = gate.astype(BF)
            r.units[1, at] = up.astype(BF)
            hidden = (gate * normal_cdf(gate) * up).astype(BF)
            return nn_dot(hidden, r.w_down[l])

        r.values[l + 1] = r.mids[l] + block(group.at(0))
        group.gather_peer(h_all)
        group.reduce_whole("peer", block(group.at(2)))
        if l + 1 == layers:
            cotangent.start()
        for chunk in range(CHUNKS):
            group.gather_near(h_all, chunk)
            r.near_part[group.piece(chunk)] = block(group.at(1, chunk))
            group.gather_diagonal(h_all, chunk)
            group.reduce_peer(1, chunk, block(group.at(3, chunk)))
            group.reduce_near(chunk, r.near_part[group.piece(chunk)])
        if l + 1 < layers:
            mixer_weights[l + 1].forward()
            ffn_weights[l + 1].start()
        save("ffn", (3, r.units, r.s_units.at[l]), (4, h_all, r.s_h_ffn.at[l]))
        for chunk in range(CHUNKS):
            r.values[l + 1, group.piece(chunk)] += group.reduce_end(chunk)
        group.finish()

    cotangent = Exchange(place, r, r.cotangent, r.cot_pieces, "cot")
    for l in range(layers):
        mixer(l)
        ffn(l)
    kept = []
    for i, name in enumerate(list(MIXER.values()) + list(FFN.values())):
        if name != "w_spec":
            kept.append(
                pltpu.make_async_copy(getattr(r, name), getattr(r, name + "_out"), r.keep_sem.at[i])
            )
    for copy in kept:
        copy.start()
    cotangent.finish()
    r.carried[...] = jnp.concatenate([r.cot_pieces[j] for j in range(4)], 1).astype(F32)
    for l in range(layers):
        mixer_weights[l].finish()
        ffn_weights[l].finish()
    saved("mixer")
    saved("ffn")
    for copy in kept:
        copy.wait()


def forward(arrays, stream, cotangent, seg, small, taps, tables):
    length, shard = stream.shape
    layers, _, width, lanes = arrays["in_proj"].shape
    rows = length // 4
    units = arrays["gate_proj"].shape[2]
    groups, _, inner = arrays["cond_in"].shape[1:]
    inner *= groups
    wide = -(-lanes // 128) * 128
    gains = small.shape[0]
    held = {to: pltpu.VMEM(arrays[n].shape, arrays[n].dtype) for n, to in {**MIXER, **FFN}.items()}
    kept = {
        to + "_out": (arrays[n].shape, arrays[n].dtype)
        for n, to in {**MIXER, **FFN}.items()
        if to != "w_spec"
    }
    saves = dict(
        s_mix=((layers, MIX_ROWS, length, lanes), BF),
        s_pre=((layers, length, inner), BF),
        s_h_mixer=((layers, length, width), BF),
        s_units=((layers, 2, length, units), BF),
        s_h_ffn=((layers, length, width), BF),
    )

    def semaphores(kind, count):
        return {
            f"{kind}_send": pltpu.SemaphoreType.DMA((layers, count, 7)),
            f"{kind}_recv": pltpu.SemaphoreType.DMA((layers, count, 8)),
            f"{kind}_local": pltpu.SemaphoreType.DMA((layers, count)),
        }

    return call_kernel(
        forward_body,
        dict(
            stream=stream, cotangent=cotangent, seg=seg, small=small, taps=taps,
            cosine=tables[0], sine=tables[1], **arrays,
        ),
        dict(
            values=((layers + 1, rows, width), F32),
            mids=((layers, rows, width), F32),
            carried=((rows, width), F32),
            gains=((gains, width), F32),
            taps_out=(taps.shape, F32),
            masks=((length, 2), F32),
            **saves,
            **kept,
        ),
        dict(
            pieces=pltpu.VMEM((4, rows, shard), BF),
            cot_pieces=pltpu.VMEM((4, rows, shard), BF),
            gain_parts=pltpu.VMEM((4, gains, shard), F32),
            gain_send=pltpu.SemaphoreType.DMA((6,)),
            gain_recv=pltpu.SemaphoreType.DMA((6,)),
            table_sem=pltpu.SemaphoreType.DMA((2,)),
            save_sem=pltpu.SemaphoreType.DMA((5,)),
            keep_sem=pltpu.SemaphoreType.DMA((8,)),
            seg_got=pltpu.VMEM((length, 1), jnp.int32),
            taps_got=pltpu.VMEM(taps.shape, F32),
            edges=pltpu.VMEM((length + 2 * PAD, 1), jnp.int32),
            cos=pltpu.VMEM((length, length), BF),
            sin=pltpu.VMEM((length, length), BF),
            h_mixer=pltpu.VMEM((layers, length, width), BF),
            h_ffn=pltpu.VMEM((layers, length, width), BF),
            mix=pltpu.VMEM((MIX_ROWS, length, lanes), BF),
            pre=pltpu.VMEM((length, inner), BF),
            units=pltpu.VMEM((2, length, units), BF),
            near_part=pltpu.VMEM((rows, width), F32),
            padded=pltpu.VMEM((3, length + 2 * PAD, lanes), F32),
            both=pltpu.VMEM((length, 2 * wide), BF),
            prod_re=pltpu.VMEM((length, lanes), BF),
            prod_im=pltpu.VMEM((length, lanes), BF),
            **held,
            **semaphores("mw", 5),
            **semaphores("fw", 3),
            **mlp_scratch(lanes, inner),
            **Group.scratch(rows, width, 2),
            **Exchange.scratch(),
            **Exchange.scratch("cot"),
        ),
        1,
        30 * 10**9,
        ("stream", "cotangent", "cosine", "sine") + tuple(arrays) + tuple(saves) + tuple(kept),
    )


GRADS = ("proj", "spec", "mlp", "small")
SMALL_ROWS = 32


def of(r, prefix):
    return [getattr(r, prefix + n) for n in GRADS]


def backward_body(r):
    place = Place()
    layers, rows, width = r.mids.shape
    length = r.m_all.shape[0]
    lanes = r.w_in.shape[3]
    groups, feats, inner = r.w_ci.shape[1:]
    units = r.units.shape[2]
    half = feats // 2
    wide = 256 * (-(-lanes // 256))
    tiles = 4
    size = length // tiles
    w_gate, w_up, w_down = [r.w_ffn.at[pl.ds(i * width, width)] for i in range(3)]
    hidden_all, gate_grads, up_grads = [r.work.at[i] for i in range(3)]
    both_re, both_im = [r.work.at[i, :, pl.ds(0, 2 * wide)] for i in range(2)]
    q_g = r.work.at[2, :, pl.ds(0, wide)]
    proj_grads = [r.work.at[i, :, pl.ds(2 * wide, wide)] for i in range(3)]

    hidden = groups * inner
    sum_in, sum_out = [
        [held.at[pl.ds(0, lanes), pl.ds(i * hidden, hidden)] for i in range(2)]
        for held in (r.near_part, r.own_part)
    ]

    def load_ffn(l):
        load = Load(
            r,
            [
                (r.w_gate_out.at[l], w_gate),
                (r.w_up_out.at[l], w_up),
                (r.w_down_out.at[l], w_down),
                (r.s_units.at[l], r.units),
            ],
        )
        load.start()
        return load

    def load_mixer(l):
        load = Load(
            r,
            [
                (r.w_out_out.at[l], r.w_out.at[0]),
                (r.w_ci_out.at[l], r.w_ci.at[0]),
                (r.w_co_out.at[l], r.w_co.at[0]),
                (r.s_mix.at[l], r.mix),
                (r.s_pre.at[l], r.pre_all),
                (r.w_in_out.at[l], r.w_in.at[0]),
            ],
            6,
        )
        load.start()
        return load

    def load_rows(rows_of, h_of):
        load = Load(r, [(rows_of, r.row_in), (h_of, r.h_all)], 12)
        load.start()
        return load

    first = Load(
        r,
        [
            (r.values.at[layers], r.near_part),
            (r.carried, r.grad),
            (r.cosine, r.cos),
            (r.sine, r.sin),
        ],
        14,
    )
    first.start()
    pending = {"ffn": load_ffn(layers - 1), "mixer": load_mixer(layers - 1)}

    ffn_scatter = [Scatter(place, r, [r.weight_grads], [r.ffn_total], "fs", l) for l in range(layers)]
    mix_scatter = [Scatter(place, r, of(r, "g_"), of(r, "u_"), "ms", l) for l in range(layers)]
    freed = [
        r.weight_grads.at[pl.ds(0, 4 * lanes)],
        r.cos.at[pl.ds(0, 2 * lanes)],
        r.units.at[1, pl.ds(0, 2 * groups * feats), pl.ds(0, inner)],
        r.units.at[1, pl.ds(0, 256), pl.ds(inner, 128)],
    ]
    ffn_spread, mix_spread = [], []
    for l in range(layers):
        ffn_to = r.r_ffn.at[l] if l else r.w_ffn
        mix_to = [o.at[l] for o in of(r, "r_")] if l else freed
        ffn_spread.append(Spread(place, r, [r.ffn_total], [ffn_to], "fp", l))
        mix_spread.append(Spread(place, r, of(r, "u_"), mix_to, "mp", l))

    shard = r.leaving.shape[2]
    output = Return(place, r, r.leaving, r.output, 0)
    stream_grad = Return(place, r, r.leaving, r.stream_grad, 1)

    def leave(x):
        for j in range(4):
            r.leaving[j] = x[:, j * shard : (j + 1) * shard].astype(BF)

    for s in range(3):
        r.padded[s, 0:PAD] = jnp.zeros((PAD, lanes), F32)
        r.padded[s, PAD + length : 2 * PAD + length] = jnp.zeros((PAD, lanes), F32)
    place.barrier()

    def ffn(l):
        top = l + 1 == layers
        group = Group(place, r, rows, 1)
        load = load_rows(r.mids.at[l], r.s_h_ffn.at[l])
        gain = r.gains[layers + l : layers + l + 1]
        if top:
            first.finish((0, 1))
        r.g_all[group.at(0)] = r.grad[...].astype(BF)
        group.gather_start(r.g_all)
        if top:
            leave(r.near_part[...])
            output.start()
        pending["ffn"].finish()
        if not top:
            pending["mixer"] = load_mixer(l)

        def block(at):
            hidden_grad = nt_dot(r.g_all[at], w_down[...])
            gate = r.units[0, at].astype(F32)
            up = r.units[1, at].astype(F32)
            cdf = normal_cdf(gate)
            act = gate * cdf
            hidden_all[at] = (act * up).astype(BF)
            gate_grad = (hidden_grad * up * (cdf + gate * normal_pdf(gate))).astype(BF)
            up_grad = (hidden_grad * act).astype(BF)
            gate_grads[at] = gate_grad
            up_grads[at] = up_grad
            return nt_dot(gate_grad, w_gate[...]) + nt_dot(up_grad, w_up[...])

        r.own_part[...] = block(group.at(0))
        group.gather_peer(r.g_all)
        group.reduce_whole("peer", block(group.at(2)))
        for chunk in range(CHUNKS):
            group.gather_near(r.g_all, chunk)
            r.near_part[group.piece(chunk)] = block(group.at(1, chunk))
            group.gather_diagonal(r.g_all, chunk)
            group.reduce_peer(1, chunk, block(group.at(3, chunk)))
            group.reduce_near(chunk, r.near_part[group.piece(chunk)])
        load.finish()
        if not top:
            ffn_spread[l + 1].forward()
        step = 256
        for u in range(units // step):
            cols = pl.ds(u * step, step)
            r.weight_grads[0 * width : 1 * width, cols] = tn_dot(r.h_all[...], gate_grads[:, cols]).astype(BF)
            r.weight_grads[1 * width : 2 * width, cols] = tn_dot(r.h_all[...], up_grads[:, cols]).astype(BF)
            r.weight_grads[pl.ds(2 * width + u * step, step)] = tn_dot(hidden_all[:, cols], r.g_all[...]).astype(BF)
        if not top:
            mix_scatter[l + 1].second()
        ffn_scatter[l].start()
        for chunk in range(CHUNKS):
            r.own_part[group.piece(chunk)] += group.reduce_end(chunk)
        grad, gain_part = norm_grad_rows(r.own_part[...], r.row_in[...], gain)
        r.grad[...] += grad
        r.gain_two[...] = gain_part
        group.finish()
        if not top:
            mix_scatter[l + 1].middle()
            ffn_spread[l + 1].finish()

    def mixer(l):
        top, bottom = l + 1 == layers, l == 0
        group = Group(place, r, rows, 0)
        load = load_rows(r.values.at[l], r.s_h_mixer.at[l])
        r.m_all[group.at(0)] = r.grad[...].astype(BF)
        group.gather_start(r.m_all)
        if not bottom:
            pending["ffn"] = load_ffn(l - 1)
        for i in range(2):
            r.work[i, :, 0 : 2 * wide] = jnp.zeros((length, 2 * wide), BF)
        r.near_part[...] = jnp.zeros_like(r.near_part)
        r.own_part[...] = jnp.zeros_like(r.own_part)
        pending["mixer"].finish()
        mlp_tables(r, 0)

        def gated_back(which, chunk=None):
            at = group.at(which, chunk)
            gated_grad = nt_dot(r.m_all[at], r.w_out[0])
            to = pl.ds(pl.multiple_of(at.start + PAD, 8), at.size)
            r.padded[0, to] = gated_grad * r.mix[MIXED, at].astype(F32)
            q_g[at, 0:lanes] = (gated_grad * r.mix[QUERY, at].astype(F32)).astype(BF)

        gated_back(0)
        group.gather_peer(r.m_all)
        gated_back(2)
        for chunk in range(CHUNKS):
            group.gather_near(r.m_all, chunk)
            gated_back(1, chunk)
            group.gather_diagonal(r.m_all, chunk)
            gated_back(3, chunk)
        ffn_scatter[l].second()
        if top:
            first.finish((2, 3))
        else:
            mix_scatter[l + 1].finish()
            mix_spread[l + 1].start()

        @pl.loop(0, tiles)
        def _(t):
            at = aligned(t, size)
            real = nn_dot(r.cos[at], q_g[:, 0:lanes])
            imag = nn_dot(r.sin[at], q_g[:, 0:lanes])
            value_re, value_im, kernel_re, kernel_im = [
                r.mix[SPECTRA + i, at].astype(F32) for i in range(4)
            ]
            kernel_re_grad = real * value_re + imag * value_im
            kernel_im_grad = imag * value_re - real * value_im
            both_re[at, 0:lanes] = (real * kernel_re + imag * kernel_im).astype(BF)
            both_im[at, 0:lanes] = (imag * kernel_re - real * kernel_im).astype(BF)
            r.g_spec[0:lanes, at] = kernel_re_grad.T.astype(BF)
            r.g_spec[lanes : 2 * lanes, at] = kernel_im_grad.T.astype(BF)
            kernel_re_grad = kernel_re_grad.astype(BF)
            kernel_im_grad = kernel_im_grad.astype(BF)
            pre = r.pre_all[at].astype(F32)
            cdf = normal_cdf(pre)
            act = (pre * cdf).astype(BF)
            inner_grad = nn_dot(kernel_re_grad, r.out_re[...]) + nn_dot(kernel_im_grad, r.out_im[...])
            pre_grad = (inner_grad * (cdf + pre * normal_pdf(pre))).astype(BF)
            both_re[at, wide : wide + lanes] = nt_dot(pre_grad, r.in_re[...]).astype(BF)
            both_im[at, wide : wide + lanes] = nt_dot(pre_grad, r.in_im[...]).astype(BF)
            sum_out[0][...] += tn_dot(kernel_re_grad, act)
            sum_out[1][...] += tn_dot(kernel_im_grad, act)
            sum_in[0][...] += tn_dot(r.mix[SPECTRA + 4, at], pre_grad)
            sum_in[1][...] += tn_dot(r.mix[SPECTRA + 5, at], pre_grad)

        for g in range(groups):
            rows_at, cols = slice(g * half, (g + 1) * half), slice(g * inner, (g + 1) * inner)
            at = g * feats
            r.g_mlp[at : at + half] = sum_in[0][rows_at, cols].astype(BF)
            r.g_mlp[at + half : at + feats] = sum_in[1][rows_at, cols].astype(BF)
            turned = jnp.concatenate([sum_out[0][rows_at, cols], sum_out[1][rows_at, cols]], 0)
            at += groups * feats
            r.g_mlp[at : at + inner] = turned.T.astype(BF)
        ffn_scatter[l].middle()

        @pl.loop(0, tiles)
        def _(t):
            at = aligned(t, size)
            both = nn_dot(r.cos[at], both_re[...]) + nn_dot(r.sin[at], both_im[...])
            to = pl.ds(pl.multiple_of(t * size + PAD, 8), size)
            r.padded[1, to] = both[:, :lanes]
            r.padded[2, to] = both[:, wide : wide + lanes]

        mix_scatter[l].start((1, 2))

        def tap(o, s):
            at = 9 * l + 3 * o + s
            return r.taps_out[at : at + 1]

        totals = [[None] * 3 for _ in range(3)]
        for t in range(tiles):
            at = pl.ds(t * size, size)
            prev = r.masks[at, 0:1]
            following = r.masks[at, 1:2]
            for s in range(3):
                here = shifted(r.padded, s, t, size, 0)
                after = shifted(r.padded, s, t, size, 1) * following
                before = shifted(r.padded, s, t, size, -1) * prev
                proj_grads[s][at, 0:lanes] = (
                    tap(0, s) * after + tap(1, s) * here + tap(2, s) * before
                ).astype(BF)
                proj = r.mix[PROJ + s, at].astype(F32)
                for o, g in enumerate((after, here, before)):
                    part = jnp.sum(g * proj, 0, keepdims=True)
                    totals[o][s] = part if t == 0 else totals[o][s] + part

        def feats_grad(which):
            at = group.at(which)
            return sum(nt_dot(proj_grads[s][at, 0:lanes], r.w_in[0, s]) for s in range(3))

        load.finish()
        for s in range(3):
            r.g_proj[s * lanes : (s + 1) * lanes] = tn_dot(proj_grads[s][:, 0:lanes], r.h_all[...]).astype(BF)
        q_g[:, 0:lanes] = (r.mix[QUERY].astype(F32) * r.mix[MIXED].astype(F32)).astype(BF)
        r.g_proj[3 * lanes :] = tn_dot(q_g[:, 0:lanes], r.m_all[...]).astype(BF)
        mix_scatter[l].start((0,))
        group.reduce_whole("diagonal", feats_grad(3))
        group.reduce_whole("near", feats_grad(1))
        group.reduce_whole("peer", feats_grad(2))
        ffn_scatter[l].finish()
        ffn_spread[l].start()
        if bottom:
            mix_scatter[l].second((1, 2))
        if not top:
            mix_spread[l + 1].forward()
        r.own_part[...] = feats_grad(0)
        for chunk in range(CHUNKS):
            r.own_part[group.piece(chunk)] += group.reduce_end(chunk)
        grad, gain_part = norm_grad_rows(r.own_part[...], r.row_in[...], r.gains[l : l + 1])
        if bottom:
            output.finish()
            leave(r.grad[...] + grad)
            stream_grad.start()
        else:
            r.grad[...] += grad
        r.small_rows[...] = jnp.zeros_like(r.small_rows)
        small = [totals[o][s] for o in range(3) for s in range(3)] + [gain_part, r.gain_two[...]]
        at = 0
        for x in small:
            for start in range(0, x.shape[1], 128):
                part = x[:, start : start + 128]
                r.small_rows[at : at + 1, 0 : part.shape[1]] = part
                at += 1
        r.g_small[...] = jnp.zeros_like(r.g_small)
        r.g_small[0:SMALL_ROWS] = r.small_rows[...].astype(BF)
        mix_scatter[l].start((3,))
        group.finish()
        if not top:
            mix_spread[l + 1].finish()

    for l in reversed(range(layers)):
        ffn(l)
        mixer(l)
    above = [
        pltpu.make_async_copy(
            r.r_small.at[l, pl.ds(0, SMALL_ROWS)], r.gain_parts.at[0, l], r.end_sem.at[l]
        )
        for l in range(1, layers)
    ]
    for copy in above:
        copy.start()
    mix_scatter[0].middle((1, 2))
    mix_scatter[0].second((0, 3))
    mix_scatter[0].finish((1, 2))
    mix_spread[0].start((1, 2))
    mix_scatter[0].middle((0, 3))
    ffn_spread[0].forward()
    mix_scatter[0].finish((0, 3))
    mix_spread[0].start((0, 3))
    mix_spread[0].forward((1, 2))
    stream_grad.finish()
    ffn_spread[0].finish()
    ends = [pltpu.make_async_copy(r.w_ffn, r.r_ffn.at[0], r.end_sem.at[0])]
    ends[0].start()
    mix_spread[0].forward((3, 0))
    mix_spread[0].finish((3,))
    r.gain_parts[0, 0] = freed[3][0:SMALL_ROWS, :]
    for copy in above:
        copy.wait()

    def gain_copy(j):
        chan = lax.rem(place.chan + j, 4)
        return remote(
            r.gain_parts.at[0], r.gain_parts.at[j], r.gain_send.at[j], r.gain_recv.at[j], {"chan": chan}
        )

    for j in range(1, 4):
        gain_copy(j).start()
    mix_spread[0].finish((1, 2, 0))
    for a, n in enumerate(GRADS):
        ends.append(
            pltpu.make_async_copy(
                freed[a], getattr(r, "r_" + n).at[0], r.end_sem.at[layers + a]
            )
        )
        ends[-1].start()
    for j in range(1, 4):
        gain_copy(j).wait()
    total = r.gain_parts[0].astype(F32)
    for j in range(1, 4):
        total += r.gain_parts[j].astype(F32)
    r.gain_grads[...] = total
    for copy in ends:
        copy.wait()


def backward(fwd, tables):
    layers, rows, width = fwd.mids.shape
    units = fwd.w_gate_out.shape[2]
    _, _, length, lanes = fwd.s_mix.shape
    groups, feats, inner = fwd.w_ci_out.shape[1:]
    hidden = groups * inner
    held = (
        "w_gate_out", "w_up_out", "w_down_out", "s_units", "s_h_ffn", "mids", "values", "carried",
        "w_out_out", "w_ci_out", "w_co_out", "s_mix", "s_pre", "w_in_out", "s_h_mixer",
    )
    near = ("gains", "taps_out", "masks")
    ins = dict(cosine=tables[0], sine=tables[1], **{n: getattr(fwd, n) for n in held + near})
    grads = dict(
        proj=(4 * lanes, width),
        spec=(2 * lanes, length),
        mlp=(2 * groups * feats, inner),
        small=(256, 128),
    )
    ffn_shape = (3 * width, units)
    outs = dict(
        output=((length, lanes), BF),
        stream_grad=((length, lanes), BF),
        r_ffn=((layers,) + ffn_shape, BF),
        **{"r_" + n: ((layers,) + g, BF) for n, g in grads.items()},
    )
    hbm = held + ("cosine", "sine") + tuple(outs)
    outs.update(gain_grads=((layers, SMALL_ROWS, 128), F32))
    row = pltpu.VMEM((rows, width), F32)
    return call_kernel(
        backward_body,
        ins,
        outs,
        dict(
            grad=row,
            own_part=row,
            near_part=row,
            row_in=row,
            leaving=pltpu.VMEM((4, rows, lanes), BF),
            gain_two=pltpu.VMEM((1, width), F32),
            g_all=pltpu.VMEM((length, width), BF),
            m_all=pltpu.VMEM((length, width), BF),
            work=pltpu.VMEM((3, length, width), BF),
            w_ffn=pltpu.VMEM(ffn_shape, BF),
            weight_grads=pltpu.VMEM(ffn_shape, BF),
            units=pltpu.VMEM((2, length, units), BF),
            ffn_total=pltpu.VMEM((ffn_shape[0] // 8, ffn_shape[1]), BF),
            h_all=pltpu.VMEM((length, width), BF),
            mix=pltpu.VMEM((MIX_ROWS, length, lanes), BF),
            pre_all=pltpu.VMEM((length, hidden), BF),
            w_in=pltpu.VMEM((1,) + fwd.w_in_out.shape[1:], BF),
            w_out=pltpu.VMEM((1,) + fwd.w_out_out.shape[1:], BF),
            w_ci=pltpu.VMEM((1,) + fwd.w_ci_out.shape[1:], F32),
            w_co=pltpu.VMEM((1,) + fwd.w_co_out.shape[1:], F32),
            cos=pltpu.VMEM((length, length), BF),
            sin=pltpu.VMEM((length, length), BF),
            padded=pltpu.VMEM((3, length + 2 * PAD, lanes), F32),
            small_rows=pltpu.VMEM((SMALL_ROWS, 128), F32),
            gain_parts=pltpu.VMEM((4, layers, SMALL_ROWS, 128), BF),
            gain_send=pltpu.SemaphoreType.DMA((4,)),
            gain_recv=pltpu.SemaphoreType.DMA((4,)),
            load_sem=pltpu.SemaphoreType.DMA((18,)),
            end_sem=pltpu.SemaphoreType.DMA((layers + len(GRADS),)),
            **{"g_" + n: pltpu.VMEM(g, BF) for n, g in grads.items()},
            **{"u_" + n: pltpu.VMEM((g[0] // 8, g[1]), BF) for n, g in grads.items()},
            **mlp_scratch(lanes, hidden),
            **Group.scratch(rows, width, 2),
            **Return.scratch(),
            **Scatter.scratch([ffn_shape], "fs", layers),
            **Scatter.scratch(list(grads.values()), "ms", layers),
            **Spread.scratch(1, "fp", layers),
            **Spread.scratch(len(GRADS), "mp", layers),
        ),
        2,
        40 * 10**9,
        hbm,
    )


def on_device(
    stream,
    segments,
    cotangent,
    norm_one,
    in_proj,
    short_taps,
    cond_in,
    cond_out,
    filter_spec,
    out_proj,
    norm_two,
    gate_proj,
    up_proj,
    down_proj,
):
    chan = lax.axis_index("chan")
    layers, width = in_proj.shape[:2]
    shard = norm_one.shape[1]
    length = filter_spec.shape[2]
    groups, feats = cond_in.shape[1:3]
    tables = dft_tables(length)
    arrays = dict(
        in_proj=in_proj.transpose(0, 2, 1, 3),
        cond_in=cond_in,
        cond_out=cond_out,
        filter_spec=filter_spec.transpose(0, 1, 3, 2),
        out_proj=out_proj,
        gate_proj=gate_proj,
        up_proj=up_proj,
        down_proj=down_proj,
    )

    fwd = forward(
        arrays,
        stream,
        cotangent,
        segments[:, None],
        jnp.concatenate([norm_one, norm_two], 0),
        short_taps.reshape(-1, shard),
        tables,
    )
    back = backward(fwd, tables)

    def everywhere(x):
        return lax.psum(x, "outer") if lax.axis_size("outer") > 1 else x

    def summed(name):
        return everywhere(getattr(back, name))

    gain_grads = summed("gain_grads")
    steps = -(-shard // 128)
    taps_rows, gain_rows = 9 * steps, width // 128

    def gain_stack(at):
        whole = gain_grads[:, at : at + gain_rows].reshape(layers, width)
        return lax.dynamic_slice_in_dim(whole, chan * shard, shard, 1)

    proj, spec, mlp = summed("r_proj"), summed("r_spec"), summed("r_mlp")
    small, ffn = summed("r_small"), summed("r_ffn")
    mlp_rows = groups * feats
    g_in = proj[:, : 3 * shard].reshape(layers, 3, shard, width).transpose(0, 3, 1, 2)
    g_taps = small[:, :taps_rows].reshape(layers, 9, steps * 128)[:, :, :shard]
    g_spec = spec.reshape(layers, 2, shard, length).transpose(0, 1, 3, 2)
    results = (
        back.output,
        back.stream_grad,
        gain_stack(taps_rows),
        g_in,
        g_taps.reshape(short_taps.shape),
        mlp[:, :mlp_rows].reshape(cond_in.shape),
        mlp[:, mlp_rows:].reshape(cond_out.shape),
        g_spec,
        proj[:, 3 * shard :],
        gain_stack(taps_rows + gain_rows),
        ffn[:, :width],
        ffn[:, width : 2 * width],
        ffn[:, 2 * width :],
    )
    return tuple(x.astype(F32) for x in results)


def solution(mesh):
    dp_count, chan_count = mesh.devices.shape
    fine = Mesh(
        mesh.devices.reshape(dp_count // 8, 4, 2, chan_count), ("outer", "col", "half", "chan")
    )
    dp = ("outer", "col", "half")
    weight_specs = (
        P(None, "chan"),
        P(None, None, None, "chan"),
        P(None, None, None, "chan"),
        P(None, "chan", None, None),
        P(None, "chan", None, None),
        P(None, None, None, "chan"),
        P(None, "chan", None),
        P(None, "chan"),
        P(None, None, "chan"),
        P(None, None, "chan"),
        P(None, "chan", None),
    )
    return jax.shard_map(
        on_device,
        mesh=fine,
        in_specs=(P(dp, "chan"), P(dp), P(dp, "chan")) + weight_specs,
        out_specs=(P(dp, "chan"), P(dp, "chan")) + weight_specs,
        check_vma=False,
    )
```
